32 devices in a mesh: section: 2 (over core), dp: 16 (over z, y, x).
Axes of the slice: x: 2, y: 2, z: 4, core: 2. Of those that a mesh axis runs over, the one named last changes fastest.
Arguments:
- stream_pair: float32 [2, 32768, 767], P('section', 'dp'), may hold values from -6 to 6
- norm_gains: float32 [2, 768], P('section'), may hold values from 0.25 to 1.75
- first_proj: bfloat16 [2, 768, 3072], P('section', None, 'dp'), may hold values from -0.3125 to 0.3125
- down_proj: bfloat16 [768, 3072], P(None, ('section', 'dp')), may hold values from -0.109375 to 0.109375
- doc_lengths: int32 [64, 4], P('dp'), may hold values from 1 to 256, 512 in all within a row
- pad_mask: int32 [32768], P('dp'), may hold values 0 or 1
Outputs:
- layer_out: float32 [2, 32768, 767], P('section', 'dp')
- gain_grad: float32 [2, 768], P('section', 'dp')
- first_grad: float32 [2, 768, 3072], P('section', None, 'dp')
- down_grad: float32 [768, 3072], P(None, ('section', 'dp'))
The draws below stay inside these ranges and needn't reach their ends.
Inputs may be any that keep to these rules, and one draw needn't show every extreme that they name: `doc_lengths`: each row sums to 512; one sequence of every row has exactly 256 tokens.
All inputs are finite; a program needn't handle non-finite values. No bound on the sum of `pad_mask` on one device may be relied on, other than what follows from the above.
Results may differ from the reference program's by a relative error of at most 0.013.
The reference program's roundings to bfloat16 on the way count: a program that leaves them out, or rounds other values in their place, can miss the bound.
Values may be sent and summed in bfloat16 or wider, within the bound.
A program may use at most 384 MiB of HBM per device.

```python
import math
import jax
import jax.numpy as jnp
import numpy as np
from jax import lax

HEADS = 12
HEAD_DIM = 64
FF = 3072
D = 768
CW = 767
SLOTS = 512
MB = 4
DOCS = 4
LONGEST = 256
TOKENS = 32768
N_DP = 16


def plant(drawn, own_key, low, largest):
    index_at = [jax.random.randint(jax.random.fold_in(own_key, axis), (), 0, length) for axis, length in enumerate(drawn.shape)]
    main_axis = drawn.shape.index(max(drawn.shape))
    neighbour = index_at[:main_axis] + [(index_at[main_axis] + 1) % drawn.shape[main_axis]] + index_at[main_axis + 1:]
    return drawn.at[tuple(index_at)].set(low).at[tuple(neighbour)].set(largest)


def block_scale(own_key, extent, cuts, smallest, largest):
    level, own = 1.0, jax.random.fold_in(own_key, 6)
    for axis_at, blocks in cuts:
        draws = jnp.exp(jax.random.uniform(jax.random.fold_in(own, axis_at), (blocks,), jnp.float32, smallest / len(cuts), largest / len(cuts)))
        level = level * jnp.repeat(draws, extent[axis_at] // blocks).reshape([-1 if axis == axis_at else 1 for axis in range(len(extent))])
    return level


def profile(count, total, most, lean):
    portions = [(1 << 20) // math.isqrt(grade ** lean) + 1 for grade in range(2, count + 1)]
    spare, holding = total - most - (count - 1), [1] * (count - 1)
    while spare > 0:
        free = [i for i in range(count - 1) if holding[i] < most]
        whole, left = sum([portions[i] for i in free]), spare
        for i in free:
            extra = min(most - holding[i], max(1, left * portions[i] // whole), spare)
            holding[i] = holding[i] + extra
            spare = spare - extra
    return np.array([most] + holding)


def ragged_sizes(rng, count, total, bound, slope):
    if count == 2:
        one = jax.random.randint(rng, (), max(1, total - bound), min(bound, total - 1) + 1)
        return jnp.stack([one, total - one])
    tallies = jnp.asarray(profile(count, total, bound, slope), jnp.int32)
    pairs = (count - 1) // 2
    source_of, receiver = tallies[1:1 + 2 * pairs:2], tallies[2:2 + 2 * pairs:2]
    slack = jnp.minimum(source_of - 1, bound - receiver)
    shifted = jax.random.randint(jax.random.fold_in(rng, 1), (pairs,), 0, 1 << 20) % (slack + 1)
    tallies = tallies.at[1:1 + 2 * pairs:2].set(source_of - shifted).at[2:2 + 2 * pairs:2].set(receiver + shifted)
    return tallies[jax.random.permutation(jax.random.fold_in(rng, 2), count)]


def bell_draw(rng, shape, spread, most, pieces=(), dtype=jnp.bfloat16):
    values = jax.random.normal(rng, shape, jnp.float32) * spread
    if len(pieces) > 0:
        values = block_scale(rng, shape, pieces, -0.22, 0.18) * values
    return jnp.clip(values, min=-most, max=most).astype(dtype)


def setup_inputs(seed: int = 0) -> dict:
    keys = jax.random.split(jax.random.key(seed), 7)
    stream_pair = bell_draw(keys[0], (2, TOKENS, CW), 1.0, 6.0, ((0, 2), (1, 16)), jnp.float32)
    norm_gains = jnp.clip(1.0 + 0.15 * jax.random.normal(keys[1], (2, D), jnp.float32), 0.25, 1.75)
    first_proj = bell_draw(keys[2], (2, D, FF), (D // 2) ** -0.5, 0.3125, ((0, 2), (2, 16)))
    down_proj = bell_draw(keys[3], (D, FF), FF ** -0.5, 0.109375, ((1, 32),))
    doc_lengths = jax.vmap(lambda own: ragged_sizes(own, DOCS, SLOTS, LONGEST, 1))(jax.random.split(keys[4], (N_DP * MB))).reshape((N_DP * MB, DOCS)).astype(jnp.int32)
    pad_mask = plant((jax.random.randint(keys[5], (TOKENS,), 0, 8) < 7).astype(jnp.int32), jax.random.fold_in(keys[5], 1), 0, 1)
    return dict(stream_pair=stream_pair, norm_gains=norm_gains, first_proj=first_proj, down_proj=down_proj, doc_lengths=doc_lengths, pad_mask=pad_mask)


@jax.custom_vjp
def low(v):
    return lax.optimization_barrier(v.astype(jnp.bfloat16)).astype(jnp.float32)

@jax.custom_vjp
def low_back(v):
    return v

def low_keep(v):
    return (low(v), None)

def low_pass(kept, grad):
    return (grad,)

def back_keep(v):
    return (v, None)

def back_low(kept, grad):
    return (low(grad),)
low.defvjp(low_keep, low_pass)
low_back.defvjp(back_keep, back_low)
epsilon = 1e-05
masked_score = -1e+30

def expand(stream):
    return jnp.concatenate([stream, -lax.optimization_barrier(jnp.sum(stream, axis=-1, keepdims=True))], axis=-1)

def shrink(branch):
    return (branch - lax.optimization_barrier(jnp.mean(branch, axis=-1, keepdims=True)))[:, :-1]

def rms_normed(expanded, gain):
    return expanded * lax.rsqrt(lax.optimization_barrier(jnp.mean(expanded * expanded, axis=-1, keepdims=True)) + epsilon) * gain

def highest_dot(left, right):
    return jnp.dot(left, right, precision=lax.Precision.HIGHEST)

def visible(lengths, token_marks):
    doc_ends = jnp.cumsum(lengths).astype(jnp.int32)
    positions = lax.iota(jnp.int32, SLOTS)
    doc_index = lax.optimization_barrier(jnp.sum((positions[:, None] >= doc_ends[None, :]).astype(jnp.int32), axis=1))
    same_doc = doc_index[:, None] == doc_index[None, :]
    causal = positions[None, :] <= positions[:, None]
    key_live = (token_marks[None, :] == 1) | (positions[None, :] == positions[:, None])
    return same_doc & causal & key_live

def attend(stream, gain, weights, seen):
    normed = low(rms_normed(expand(stream), gain))
    projected = low_back(low(highest_dot(normed, weights[:, :3 * D])))
    query_heads = projected[:, :D].reshape(SLOTS, HEADS, HEAD_DIM)
    key_heads = projected[:, D:2 * D].reshape(SLOTS, HEADS, HEAD_DIM)
    value_heads = projected[:, 2 * D:].reshape(SLOTS, HEADS, HEAD_DIM)
    scores = jnp.einsum('qhd,khd->hqk', query_heads, key_heads, precision=lax.Precision.HIGHEST) * HEAD_DIM ** (-0.5)
    scores = jnp.where(seen[None], low_back(scores), masked_score)
    probs = low(jax.nn.softmax(scores, axis=-1))
    attended = jnp.einsum('hqk,khd->qhd', probs, value_heads, precision=lax.Precision.HIGHEST).reshape(SLOTS, D)
    attended = low_back(low(attended))
    branch = low_back(highest_dot(attended, weights[:, 3 * D:]))
    return stream + shrink(branch)

def mixer_half(stream, gain, weights, down):
    normed = low(rms_normed(expand(stream), gain))
    pre_act = low_back(highest_dot(normed, weights))
    activated = low(jax.nn.gelu(pre_act, approximate=True))
    branch = low_back(highest_dot(activated, down.T))
    return stream + shrink(branch)

def reference(stream_pair, norm_gains, first_proj, down_proj, doc_lengths, pad_mask):
    buffers = N_DP * MB
    inputs = stream_pair[0].reshape(buffers, SLOTS, D - 1)
    token_marks = pad_mask.reshape(buffers, SLOTS)
    cotangent = stream_pair[1].reshape(buffers, SLOTS, D - 1) * token_marks[..., None].astype(jnp.float32)
    gains_full = norm_gains.astype(jnp.float32)
    first_full = first_proj.astype(jnp.float32)
    down_full = down_proj.astype(jnp.float32)

    def one_buffer(running, buffer_item):
        stream, stream_cot, lengths, buffer_marks = buffer_item
        seen = visible(lengths, buffer_marks)

        def layer_pass(entering, gains_in, first_in, down_in):
            middle_stream = attend(entering, gains_in[0], first_in[0], seen)
            return mixer_half(middle_stream, gains_in[1], first_in[1], down_in)
        result, pullback = jax.vjp(layer_pass, stream, gains_full, first_full, down_full)
        stream_grad, gains_grad, first_part, down_part = pullback(stream_cot)
        running = (running[0] + gains_grad, running[1] + first_part, running[2] + down_part)
        return (running, (result, stream_grad))
    initial = (jnp.zeros_like(gains_full), jnp.zeros_like(first_full), jnp.zeros_like(down_full))
    totals, stacked = lax.scan(one_buffer, initial, (inputs, cotangent, doc_lengths, token_marks))
    results, input_grads = stacked
    layer_out = jnp.stack([input_grads.reshape(-1, D - 1), results.reshape(-1, D - 1)])
    return (layer_out, totals[0], totals[1], totals[2])
```

```python
import functools
import jax, jax.numpy as jnp
from jax import lax
from jax.experimental import pallas as pl
from jax.experimental.pallas import tpu as pltpu
from jax.sharding import PartitionSpec as P

HEADS, HEAD_DIM, FF, D, SLOTS = 12, 64, 3072, 768, 512
EPS, MASKED = 1e-05, -1e30
f32, bf16 = jnp.float32, jnp.bfloat16
CHUNK = 768

def nn(a, b):
    return lax.dot_general(a, b, (((1,), (0,)), ((), ())), preferred_element_type=f32)
def nt(a, b):
    return lax.dot_general(a, b, (((1,), (1,)), ((), ())), preferred_element_type=f32)
def tn(a, b):
    return lax.dot_general(a, b, (((0,), (0,)), ((), ())), preferred_element_type=f32)

def last_row(shape):
    return lax.broadcasted_iota(jnp.int32, shape, 0) == shape[0] - 1

def expanded(x):
    return jnp.where(last_row(x.shape), -jnp.sum(x, axis=0, keepdims=True), x)

def inv_rms(x):
    return lax.rsqrt(jnp.mean(x * x, axis=0, keepdims=True) + EPS)

def bias_block(ends, live, first_key, keys, first_query, queries):
    shape = (keys, queries)
    kp = lax.broadcasted_iota(jnp.int32, shape, 0) + first_key
    qp = lax.broadcasted_iota(jnp.int32, shape, 1) + first_query
    kd = sum((kp >= e).astype(jnp.int32) for e in ends)
    qd = sum((qp >= e).astype(jnp.int32) for e in ends)
    seen = (kd == qd) & (kp <= qp) & ((live > 0.5) | (kp == qp))
    return jnp.where(seen, 0.0, MASKED)

def attn_fwd(ends_ref, x_ref, g0_ref, g1_ref, mask_ref, w_ref,
             qkv_ref, att_ref, lse_ref, h0_ref, x1_ref, h1_ref, bias_ref):
    T = x_ref.shape[1]
    nb = T // SLOTS
    @pl.loop(0, T // 256)
    def _(t):
        c = pl.ds(pl.multiple_of(t * 256, 256), 256)
        x = expanded(x_ref[:, c])
        h0_ref[:, c] = (x * inv_rms(x) * g0_ref[:, :1]).astype(bf16)
    for b in range(nb):
        ends = [ends_ref[b, j] for j in range(3)]
        marks = jnp.broadcast_to(mask_ref[:1, b * SLOTS:(b + 1) * SLOTS], (128, SLOTS)).T
        for qb in range(2):
            nk = 256 * (qb + 1)
            for q0 in (0, 128):
                bias_ref[b, :nk, qb * 256 + q0: qb * 256 + q0 + 128] = bias_block(ends, marks[:nk], 0, nk, qb * 256 + q0, 128)
    @pl.loop(0, 9)
    def _(m):
        r = pl.ds(pl.multiple_of(m * 256, 256), 256)
        qkv_ref[r, :] = nn(w_ref[r, :], h0_ref[...]).astype(bf16)
    for b in range(nb):
        cols = slice(b * SLOTS, (b + 1) * SLOTS)
        @pl.loop(0, HEADS // 2)
        def _(hp):
            for hh in range(2):
                h = hp * 2 + hh
                off = pl.multiple_of(h * HEAD_DIM, HEAD_DIM)
                q = qkv_ref[pl.ds(off, HEAD_DIM), cols] * bf16(HEAD_DIM ** -0.5)
                k = qkv_ref[pl.ds(off + D, HEAD_DIM), cols].T
                v = qkv_ref[pl.ds(off + 2 * D, HEAD_DIM), cols]
                for qb in range(2):
                    nk, lo = 256 * (qb + 1), qb * 256
                    s = nn(k[:nk], q[:, lo:lo + 256]) + bias_ref[b, :nk, lo:lo + 256]
                    mx = jnp.max(s, axis=0, keepdims=True)
                    p = jnp.exp(s - mx)
                    tot = jnp.sum(p, axis=0, keepdims=True)
                    lse_ref[pl.ds(h, 1), b * SLOTS + lo: b * SLOTS + lo + 256] = mx + jnp.log(tot)
                    low = (p * (1.0 / tot)).astype(bf16)
                    att_ref[pl.ds(off, HEAD_DIM), b * SLOTS + lo: b * SLOTS + lo + 256] = nn(v[:, :nk], low).astype(bf16)
    @pl.loop(0, T // 256)
    def _(t):
        c = pl.ds(pl.multiple_of(t * 256, 256), 256)
        x = expanded(x_ref[:, c])
        a = nn(w_ref[3 * D:, :], att_ref[:, c])
        x1 = expanded(jnp.where(last_row(x.shape), 0.0, x + (a - jnp.mean(a, axis=0, keepdims=True))))
        x1_ref[:, c] = x1
        h1_ref[:, c] = (x1 * inv_rms(x1) * g1_ref[:, :1]).astype(bf16)

C0 = 0.7978845608028654
def gelu_both(u):
    u2 = u * u
    inner = C0 * u * (1.0 + 0.044715 * u2)
    t = jnp.tanh(inner)
    half = 0.5 * (1.0 + t)
    slope = half + 0.5 * u * (1.0 - t * t) * (C0 * (1.0 + 3 * 0.044715 * u2))
    return u * half, slope

def norm_back(x, r, gain, dh):
    e = gain * dh
    dx = r * e - x * (r * r * r) * jnp.mean(x * e, axis=0, keepdims=True)
    return dx, dh * x * r

def lane_fold(v):
    return sum(v[:, i * 128:(i + 1) * 128] for i in range(v.shape[1] // 128))

def ffn(g_ref, g1_ref, mask_ref, x1_ref, h1_ref, w1_ref, wd_ref,
        out1_ref, dy_ref, gw1_ref, gwd_ref, gg_ref, dm_ref, z_ref, du_ref, u_ref, macc, hacc):
    T = g_ref.shape[1]
    nt_ = T // 256
    @pl.loop(0, nt_)
    def _(t):
        c = pl.ds(pl.multiple_of(t * 256, 256), 256)
        g = g_ref[:, c] * mask_ref[:1, c]
        dm_ref[:, c] = (g - jnp.mean(g, axis=0, keepdims=True)).astype(bf16)
    macc[...] = jnp.zeros_like(macc)
    hacc[...] = jnp.zeros_like(hacc)
    @pl.loop(0, FF // CHUNK)
    def _(p):
        base = p * CHUNK
        @pl.loop(0, CHUNK // 256)
        def _(m):
            r = pl.ds(pl.multiple_of(base + m * 256, 256), 256)
            rl = pl.ds(pl.multiple_of(m * 256, 256), 256)
            for n in range(T // 512):
                cs = slice(n * 512, (n + 1) * 512)
                z, slope = gelu_both(nn(w1_ref[r, :], h1_ref[:, cs]))
                z_ref[rl, cs] = z.astype(bf16)
                du_ref[rl, cs] = (nn(wd_ref[r, :], dm_ref[:, cs]) * slope).astype(bf16)
        rows = pl.ds(pl.multiple_of(base, CHUNK), CHUNK)
        @pl.loop(0, 3)
        def _(m):
            o = pl.ds(pl.multiple_of(m * 256, 256), 256)
            macc[o, :] += tn(wd_ref[rows, o], z_ref[...])
            hacc[o, :] += tn(w1_ref[rows, o], du_ref[...])
            r = pl.ds(pl.multiple_of(base + m * 256, 256), 256)
            gw1_ref[r, :] = nt(du_ref[o, :], h1_ref[...]).astype(gw1_ref.dtype)
            gwd_ref[r, :] = nt(z_ref[o, :], dm_ref[...]).astype(gwd_ref.dtype)
    gg_ref[...] = jnp.zeros_like(gg_ref)
    @pl.loop(0, nt_)
    def _(t):
        c = pl.ds(pl.multiple_of(t * 256, 256), 256)
        x1, m = x1_ref[:, c], macc[:, c]
        out1_ref[:, c] = x1 + (m - jnp.mean(m, axis=0, keepdims=True))
        g = g_ref[:, c] * mask_ref[:1, c]
        dx, gg = norm_back(x1, inv_rms(x1), g1_ref[:, :1], hacc[:, c])
        gg_ref[...] += lane_fold(gg)
        dy_ref[:, c] = g + dx - dx[D - 1:, :]

def attn_bwd(ends_ref, x_ref, g0_ref, mask_ref, w_ref, qkv_ref, att_ref, lse_ref, h0_ref, dy_ref,
             out0_ref, gw_ref, gg_ref, da_ref, dat_ref, dqkv_ref, bias_ref):
    T = x_ref.shape[1]
    nb = T // SLOTS
    for b in range(nb):
        ends = [ends_ref[b, j] for j in range(3)]
        marks = jnp.broadcast_to(mask_ref[:1, b * SLOTS:(b + 1) * SLOTS], (128, SLOTS)).T
        for qb in range(2):
            nk = 256 * (qb + 1)
            for q0 in (0, 128):
                bias_ref[b, :nk, qb * 256 + q0: qb * 256 + q0 + 128] = bias_block(ends, marks[:nk], 0, nk, qb * 256 + q0, 128)
    @pl.loop(0, T // 256)
    def _(t):
        c = pl.ds(pl.multiple_of(t * 256, 256), 256)
        dy = dy_ref[:, c]
        da_ref[:, c] = (dy - jnp.mean(dy, axis=0, keepdims=True)).astype(bf16)
    @pl.loop(0, 3)
    def _(m):
        o = pl.ds(pl.multiple_of(m * 256, 256), 256)
        r = pl.ds(pl.multiple_of(3 * D + m * 256, 256), 256)
        gw_ref[r, :] = nt(da_ref[o, :], att_ref[...]).astype(gw_ref.dtype)
        dat_ref[o, :] = tn(w_ref[3 * D:, o], da_ref[...]).astype(bf16)
    for b in range(nb):
        cols = slice(b * SLOTS, (b + 1) * SLOTS)
        @pl.loop(0, HEADS)
        def _(h):
            off = pl.multiple_of(h * HEAD_DIM, HEAD_DIM)
            q = qkv_ref[pl.ds(off, HEAD_DIM), cols] * bf16(HEAD_DIM ** -0.5)
            kt = qkv_ref[pl.ds(off + D, HEAD_DIM), cols]
            k = kt.T
            v = qkv_ref[pl.ds(off + 2 * D, HEAD_DIM), cols].T
            d = dat_ref[pl.ds(off, HEAD_DIM), cols]
            dks, dvs = [], []
            for qb in range(2):
                nk, lo = 256 * (qb + 1), qb * 256
                s = nn(k[:nk], q[:, lo:lo + 256]) + bias_ref[b, :nk, lo:lo + 256]
                p = jnp.exp(s - lse_ref[pl.ds(h, 1), b * SLOTS + lo: b * SLOTS + lo + 256])
                dp = nn(v[:nk], d[:, lo:lo + 256])
                ds = (p * (dp - jnp.sum(p * dp, axis=0, keepdims=True))).astype(bf16)
                low = p.astype(bf16)
                dqkv_ref[pl.ds(off, HEAD_DIM), b * SLOTS + lo: b * SLOTS + lo + 256] = (nn(kt[:, :nk], ds) * HEAD_DIM ** -0.5).astype(bf16)
                dks.append(nt(q[:, lo:lo + 256], ds))
                dvs.append(nt(d[:, lo:lo + 256], low))
            for at, parts in ((D, dks), (2 * D, dvs)):
                dqkv_ref[pl.ds(off + at, HEAD_DIM), b * SLOTS: b * SLOTS + 256] = (parts[0] + parts[1][:, :256]).astype(bf16)
                dqkv_ref[pl.ds(off + at, HEAD_DIM), b * SLOTS + 256: (b + 1) * SLOTS] = parts[1][:, 256:].astype(bf16)
    @pl.loop(0, 9)
    def _(m):
        r = pl.ds(pl.multiple_of(m * 256, 256), 256)
        gw_ref[r, :] = nt(dqkv_ref[r, :], h0_ref[...]).astype(gw_ref.dtype)
    gg_ref[...] = jnp.zeros_like(gg_ref)
    @pl.loop(0, T // 256)
    def _(t):
        c = pl.ds(pl.multiple_of(t * 256, 256), 256)
        x = expanded(x_ref[:, c])
        dh = tn(w_ref[:3 * D, :], dqkv_ref[:, c])
        dx, gg = norm_back(x, inv_rms(x), g0_ref[:, :1], dh)
        gg_ref[...] += lane_fold(gg)
        out0_ref[:, c] = dy_ref[:, c] + dx - dx[D - 1:, :]

V = pl.BlockSpec(memory_space=pltpu.VMEM)
S = pl.BlockSpec(memory_space=pltpu.SMEM)
def sds(*shape, dtype=f32):
    return jax.ShapeDtypeStruct(shape, dtype)
PARAMS = pltpu.CompilerParams(vmem_limit_bytes=60 * 2**20)

def run_attn_fwd(ends, x, g0, g1, mask, w):
    T = x.shape[1]
    return pl.pallas_call(attn_fwd, in_specs=[S] + [V] * 5, out_specs=[V] * 6,
        out_shape=[sds(3 * D, T, dtype=bf16), sds(D, T, dtype=bf16), sds(16, T), sds(D, T, dtype=bf16), sds(D, T), sds(D, T, dtype=bf16)],
        scratch_shapes=[pltpu.VMEM((T // SLOTS, SLOTS, SLOTS), f32)], compiler_params=PARAMS, name="attn_fwd")(ends, x, g0, g1, mask, w)

def run_ffn(g, g1, mask, x1, h1, w1, wd, gdt=bf16):
    T = g.shape[1]
    return pl.pallas_call(ffn, in_specs=[V] * 7, out_specs=[V] * 5,
        out_shape=[sds(D, T), sds(D, T), sds(FF, D, dtype=gdt), sds(FF, D, dtype=gdt), sds(D, 128)],
        scratch_shapes=[pltpu.VMEM((D, T), bf16), pltpu.VMEM((CHUNK, T), bf16), pltpu.VMEM((CHUNK, T), bf16), pltpu.VMEM((8, 128), f32), pltpu.VMEM((D, T), f32), pltpu.VMEM((D, T), f32)],
        compiler_params=PARAMS, name="ffn")(g, g1, mask, x1, h1, w1, wd)

def run_attn_bwd(ends, x, g0, mask, w, qkv, att, lse, h0, dy, gdt=bf16):
    T = x.shape[1]
    return pl.pallas_call(attn_bwd, in_specs=[S] + [V] * 9, out_specs=[V] * 3,
        out_shape=[sds(D, T), sds(FF, D, dtype=gdt), sds(D, 128)],
        scratch_shapes=[pltpu.VMEM((D, T), bf16), pltpu.VMEM((D, T), bf16), pltpu.VMEM((3 * D, T), bf16), pltpu.VMEM((T // SLOTS, SLOTS, SLOTS), f32)],
        compiler_params=PARAMS, name="attn_bwd")(ends, x, g0, mask, w, qkv, att, lse, h0, dy)

MESH = pl.DeviceIdType.MESH
HBM = pl.BlockSpec(memory_space=pl.ANY)


def place():
    s, d = lax.axis_index("section"), lax.axis_index("dp")
    x, y, z = lax.rem(d, 2), lax.rem(d // 2, 2), d // 4
    return s, x, y, z


def neighbours(s, x, y, z):
    at = lambda s, x, y, z: (s, z * 4 + y * 2 + x)
    zs = [at(s, x, y, lax.rem(z + k, 4)) for k in range(1, 4)]
    return at(1 - s, x, y, z), at(s, 1 - x, y, z), at(s, x, 1 - y, z), zs


def greet(devices):
    barrier = pltpu.get_barrier_semaphore()
    for device in devices:
        pl.semaphore_signal(barrier, inc=1, device_id=device, device_id_type=MESH)
    pl.semaphore_wait(barrier, len(devices))


def push(src, dst, send, recv, device):
    copy = pltpu.make_async_remote_copy(
        src_ref=src, dst_ref=dst, send_sem=send, recv_sem=recv, device_id=device, device_id_type=MESH
    )
    copy.start()
    return copy


def gather_kernel(w_ref, wd_ref, s_ref, g_ref, wf, wdf, own_x, own_g, gains, send, recv, local):
    s, x, y, z = place()
    sib, nx, ny, nz = neighbours(s, x, y, z)
    greet([sib, nx, ny, *nz])
    T = own_x.shape[1]
    copies = []
    sets = ((w_ref, wf), (wd_ref, wdf))
    n = 0
    pend = []
    for i, (src, full) in enumerate(sets):
        here = pltpu.make_async_copy(src, full.at[s, z, y, x], local.at[i])
        here.start()
        zc = [push(src, full.at[s, z, y, x], send.at[i, k], recv.at[i, k], nz[k]) for k in range(3)]
        pend.append((here, zc))
    def stream(kind, keep, give, index):
        def go():
            c = pltpu.make_async_copy(s_ref.at[:, pl.ds(index * T, T)], keep, local.at[2])
            c.start()
            r = push(s_ref.at[:, pl.ds((1 - index) * T, T)], keep, send.at[2, 0], recv.at[2, 0], sib)
            c.wait()
            r.wait_send()
        return go
    pl.when(s == 0)(stream(0, own_x, own_x, 0))
    pl.when(s == 1)(stream(1, own_g, own_g, 1))
    gl = pltpu.make_async_copy(g_ref, gains.at[s], local.at[3])
    gl.start()
    gr = push(g_ref, gains.at[s], send.at[2, 1], recv.at[2, 1], sib)
    p2 = []
    for i, (src, full) in enumerate(sets):
        here, zc = pend[i]
        here.wait()
        for c in zc:
            c.wait()
        a = push(full.at[s, :, y, x, 0], full.at[s, :, y, x, 0], send.at[i, 3], recv.at[i, 3], ny)
        b = push(full.at[s, :, y, x, 1], full.at[s, :, y, x, 1], send.at[i, 4], recv.at[i, 4], nx)
        copies.append(push(full.at[s, :, y, x], full.at[s, :, y, x], send.at[i, 5], recv.at[i, 5], sib))
        p2.append((a, b))
    p3 = []
    for i, (src, full) in enumerate(sets):
        a, b = p2[i]
        a.wait()
        c = push(full.at[s, :, :, x, 0], full.at[s, :, :, x, 0], send.at[i, 6], recv.at[i, 6], nx)
        b.wait()
        d = push(full.at[s, :, y, :, 1], full.at[s, :, y, :, 1], send.at[i, 7], recv.at[i, 7], ny)
        copies.append(push(full.at[s, :, 1 - y, x, 0], full.at[s, :, 1 - y, x, 0], send.at[i, 8], recv.at[i, 8], sib))
        copies.append(push(full.at[s, :, y, 1 - x, 1], full.at[s, :, y, 1 - x, 1], send.at[i, 9], recv.at[i, 9], sib))
        p3.append((c, d))
    for i, (src, full) in enumerate(sets):
        c, d = p3[i]
        c.wait()
        copies.append(push(full.at[s, :, :, 1 - x, 0], full.at[s, :, :, 1 - x, 0], send.at[i, 10], recv.at[i, 10], sib))
        d.wait()
        copies.append(push(full.at[s, :, 1 - y, :, 1], full.at[s, :, 1 - y, :, 1], send.at[i, 11], recv.at[i, 11], sib))
    for c in copies:
        c.wait()
    gl.wait()
    gr.wait()
    pl.when(s == 0)(lambda: pltpu.make_async_remote_copy(
        src_ref=own_g, dst_ref=own_g, send_sem=send.at[2, 0], recv_sem=recv.at[2, 0], device_id=sib, device_id_type=MESH).wait_recv())
    pl.when(s == 1)(lambda: pltpu.make_async_remote_copy(
        src_ref=own_x, dst_ref=own_x, send_sem=send.at[2, 0], recv_sem=recv.at[2, 0], device_id=sib, device_id_type=MESH).wait_recv())


def gather(w, wd, stream, gain):
    T = stream.shape[1] // 2
    rows, low = w.shape[0], wd.shape[0]
    shapes = [sds(2, 4, 2, 2, 2, rows // 2, D, dtype=bf16), sds(2, 4, 2, 2, 2, low // 2, D, dtype=bf16),
              sds(D, T), sds(D, T), sds(2, D, 128)]
    wf, wdf, x, g, gains = pl.pallas_call(
        gather_kernel, in_specs=[HBM] * 4, out_specs=[HBM] * 5, out_shape=shapes,
        scratch_shapes=[pltpu.SemaphoreType.DMA((3, 12)), pltpu.SemaphoreType.DMA((3, 12)), pltpu.SemaphoreType.DMA((4,))],
        compiler_params=pltpu.CompilerParams(collective_id=1, has_side_effects=True), name="gather",
    )(w.reshape(2, rows // 2, D), wd.reshape(2, low // 2, D), stream, gain)
    return wf.reshape(2, FF, D), wdf.reshape(FF, D), x, g, gains


def scatter_kernel(gw, gwd, o0, o1, gg, fw, fwd, out, gout,
                   accw, accd, sibw, sibd, l1w, l1d, l2w, l2d, l3w, l3d, gacc, gl, send, recv, local):
    s, x, y, z = place()
    sib, nx, ny, nz = neighbours(s, x, y, z)
    greet([sib, nx, ny, *nz])
    T = o0.shape[1]
    sets = ((gw, fw, accw, sibw, l1w, l2w, l3w), (gwd, fwd, accd, sibd, l1d, l2d, l3d))
    mine = []
    for i, (src, fin, acc, land, *_) in enumerate(sets):
        own = pltpu.make_async_copy(src.at[s], acc, local.at[i])
        own.start()
        mine.append((own, push(src.at[1 - s], land, send.at[i, 0], recv.at[i, 0], sib)))
    own = pltpu.make_async_copy(gg.at[s], gacc, local.at[2])
    own.start()
    gs = push(gg.at[1 - s], gl.at[0], send.at[2, 0], recv.at[2, 0], sib)
    def give(keep, other, index):
        def go():
            c = pltpu.make_async_copy(keep, out.at[:, pl.ds(index * T, T)], local.at[3])
            c.start()
            r = push(other, out.at[:, pl.ds(index * T, T)], send.at[2, 1], recv.at[2, 1], sib)
            c.wait()
            r.wait()
        return go
    def add(acc, index, land):
        acc[index] = (acc[index].astype(f32) + land.astype(f32)).astype(bf16)
    p1 = []
    for i, (src, fin, acc, land, l1, l2, l3) in enumerate(sets):
        own_, rem = mine[i]
        own_.wait()
        rem.wait()
        @pl.loop(0, 4)
        def _(zz):
            for a in range(2):
                for b in range(2):
                    add(acc, (zz, a, b), land[zz, a, b])
        p1.append((push(acc.at[:, :, 1 - x, 0], l1.at[0], send.at[i, 1], recv.at[i, 1], nx),
                   push(acc.at[:, 1 - y, :, 1], l1.at[1], send.at[i, 2], recv.at[i, 2], ny)))
    own.wait()
    gs.wait()
    gacc[...] += gl[0]
    g1 = push(gacc, gl.at[1], send.at[2, 2], recv.at[2, 2], nx)
    pl.when(s == 0)(give(o0, o1, 0))
    pl.when(s == 1)(give(o1, o0, 1))
    g1.wait()
    gacc[...] += gl[1]
    g2 = push(gacc, gl.at[2], send.at[2, 3], recv.at[2, 3], ny)
    g2.wait()
    gacc[...] += gl[2]
    g3 = [push(gacc, gl.at[3 + k], send.at[2, 4 + k], recv.at[2, 4 + k], nz[k]) for k in range(3)]
    p2 = []
    for i, (src, fin, acc, land, l1, l2, l3) in enumerate(sets):
        for c in p1[i]:
            c.wait()
        @pl.loop(0, 4)
        def _(zz):
            for a in range(2):
                add(acc, (zz, a, x, 0), l1[0, zz, a])
                add(acc, (zz, y, a, 1), l1[1, zz, a])
        p2.append((push(acc.at[:, 1 - y, x, 0], l2.at[0], send.at[i, 3], recv.at[i, 3], ny),
                   push(acc.at[:, y, 1 - x, 1], l2.at[1], send.at[i, 4], recv.at[i, 4], nx)))
    p3 = []
    for i, (src, fin, acc, land, l1, l2, l3) in enumerate(sets):
        for c in p2[i]:
            c.wait()
        @pl.loop(0, 4)
        def _(zz):
            add(acc, (zz, y, x, 0), l2[0, zz])
            add(acc, (zz, y, x, 1), l2[1, zz])
        p3.append([push(acc.at[lax.rem(z + k, 4), y, x], l3.at[k - 1], send.at[i, 4 + k], recv.at[i, 4 + k], nz[k - 1]) for k in range(1, 4)])
    for i, (src, fin, acc, land, l1, l2, l3) in enumerate(sets):
        for c in p3[i]:
            c.wait()
        total = acc[z, y, x].astype(f32)
        for k in range(3):
            total += l3[k].astype(f32)
        fin[...] = total
    for c in g3:
        c.wait()
    gout[...] = gacc[...] + gl[3] + gl[4] + gl[5]


def scatter(gw, gwd, out0, out1, gg):
    T = out0.shape[1]
    rows, low = FF // 16, FF // 32
    bulk = lambda r: [pltpu.VMEM((4, 2, 2, 2, r // 2, D), bf16)]
    scratch = []
    for shape in ((4, 2, 2, 2), (4, 2, 2, 2), (2, 4, 2), (2, 4), (3, 2)):
        for r in (rows, low):
            scratch.append(pltpu.VMEM((*shape, r // 2, D), bf16))
    scratch += [pltpu.VMEM((8, D), f32), pltpu.VMEM((6, 8, D), f32)]
    scratch += [pltpu.SemaphoreType.DMA((3, 8)), pltpu.SemaphoreType.DMA((3, 8)), pltpu.SemaphoreType.DMA((4,))]
    fw, fwd, out, gout = pl.pallas_call(
        scatter_kernel, in_specs=[HBM] * 5, out_specs=[V, V, HBM, V],
        out_shape=[sds(2, rows // 2, D), sds(2, low // 2, D), sds(D, 2 * T), sds(8, D)],
        scratch_shapes=scratch,
        compiler_params=pltpu.CompilerParams(collective_id=2, has_side_effects=True, vmem_limit_bytes=50 * 2**20), name="scatter",
    )(gw.reshape(2, 4, 2, 2, 2, rows // 2, D), gwd.reshape(2, 4, 2, 2, 2, low // 2, D), out0, out1, gg)
    return fw.reshape(rows, D), fwd.reshape(low, D), out, gout


def shards(sizes, stream_pair, norm_gains, first_proj, down_proj, doc_lengths, pad_mask):
    s, d = lax.axis_index("section"), lax.axis_index("dp")
    sections, groups = sizes
    stream = jnp.pad(jnp.transpose(stream_pair, (2, 0, 1)).reshape(D - 1, -1), ((0, 1), (0, 0)))
    w = jnp.transpose(first_proj[0])
    wd = jnp.transpose(down_proj)
    gain = jnp.broadcast_to(norm_gains[0][:, None], (D, 128))
    whole = stream.shape[1]
    T = whole // sections
    nb = T // SLOTS
    own_docs = lax.dynamic_slice_in_dim(doc_lengths, s * nb, nb, axis=0)
    ends = jnp.stack([jnp.sum(own_docs[:, : j + 1], axis=1) for j in range(own_docs.shape[1])], axis=1)
    mask = lax.dynamic_slice_in_dim(pad_mask, s * T, T, axis=0).astype(f32)
    mask = jnp.broadcast_to(mask[None], (8, T))
    own_kernels = (sections, groups) == (2, 16)
    if own_kernels:
        weights, wd_full, x, g, gains = gather(w, wd, stream, gain)
    else:
        weights = lax.all_gather(lax.all_gather(w, "dp", axis=0, tiled=True), "section")
        wd_full = lax.all_gather(wd, ("section", "dp"), axis=0, tiled=True)
        both = lax.all_gather(stream, "section")
        x, g = lax.dynamic_slice_in_dim(both, s * T, T, axis=2)
        gains = lax.all_gather(gain, "section")
    qkv, att, lse, h0, x1, h1 = run_attn_fwd(ends, x, gains[0], gains[1], mask, weights[0])
    out1, dy, gw1, gwd, gg1 = run_ffn(g, gains[1], mask, x1, h1, weights[1], wd_full)
    out0, gw0, gg0 = run_attn_bwd(ends, x, gains[0], mask, weights[0], qkv, att, lse, h0, dy)
    gw = jnp.stack([gw0, gw1])
    gg = jnp.stack([gg0, gg1])
    if own_kernels:
        gg = jnp.broadcast_to(jnp.sum(gg, axis=2)[:, None], (2, 8, D))
        first, down, out, gain_total = scatter(gw, gwd, out0, out1, gg)
        gain_total = gain_total[0]
    else:
        first = lax.psum_scatter(gw.astype(f32), "section", scatter_dimension=0)
        first = lax.psum_scatter(first, "dp", scatter_dimension=0, tiled=True)
        down = lax.psum_scatter(gwd.astype(f32), ("section", "dp"), scatter_dimension=0, tiled=True)
        outs = lax.all_gather(jnp.stack([out0, out1]), "section")
        out = jnp.concatenate([lax.dynamic_index_in_dim(outs[i], s, 0, False) for i in range(2)], axis=1)
        gain_total = lax.psum_scatter(lax.psum(jnp.sum(gg, axis=2), "dp"), "section", scatter_dimension=0)
    share = D // groups
    gain_share = lax.dynamic_slice_in_dim(gain_total, d * share, share, axis=0)
    layer_out = jnp.transpose(out[: D - 1].reshape(D - 1, 1, whole), (1, 2, 0))
    return layer_out, gain_share[None], jnp.transpose(first)[None], jnp.transpose(down)


def solution(mesh):
    placed = (
        P("section", "dp", None),
        P("section", None),
        P("section", None, "dp"),
        P(None, ("section", "dp")),
        P("dp", None),
        P("dp"),
    )
    return jax.shard_map(
        functools.partial(shards, (mesh.shape["section"], mesh.shape["dp"])),
        mesh=mesh,
        in_specs=placed,
        out_specs=(
            P("section", "dp", None),
            P("section", "dp"),
            P("section", None, "dp"),
            P(None, ("section", "dp")),
        ),
        check_vma=False,
    )
```

```python
import functools
import jax, jax.numpy as jnp
from jax import lax
from jax.experimental import pallas as pl
from jax.experimental.pallas import tpu as pltpu
from jax.sharding import PartitionSpec as P

HEADS, HEAD_DIM, FF, D, SLOTS = 12, 64, 3072, 768, 512
LONGEST = 256
EPS, MASKED = 1e-05, -1e30
VMEM_MOST = 63 * 2**20
f32, bf16 = jnp.float32, jnp.bfloat16
CHUNK = 768

def nn(a, b):
    return lax.dot_general(a, b, (((1,), (0,)), ((), ())), preferred_element_type=f32)
def nt(a, b):
    return lax.dot_general(a, b, (((1,), (1,)), ((), ())), preferred_element_type=f32)
def tn(a, b):
    return lax.dot_general(a, b, (((0,), (0,)), ((), ())), preferred_element_type=f32)

def last_row(shape):
    return lax.broadcasted_iota(jnp.int32, shape, 0) == shape[0] - 1

def expanded(x):
    return jnp.where(last_row(x.shape), -jnp.sum(x, axis=0, keepdims=True), x)

def inv_rms(x):
    return lax.rsqrt(jnp.mean(x * x, axis=0, keepdims=True) + EPS)

def bias_block(ends, live, first_key, keys, first_query, queries):
    shape = (keys, queries)
    kp = lax.broadcasted_iota(jnp.int32, shape, 0) + first_key
    qp = lax.broadcasted_iota(jnp.int32, shape, 1) + first_query
    kd = sum((kp >= e).astype(jnp.int32) for e in ends)
    qd = sum((qp >= e).astype(jnp.int32) for e in ends)
    seen = (kd == qd) & (kp <= qp) & ((live > 0.5) | (kp == qp))
    return jnp.where(seen, 0.0, MASKED)

def attn_fwd(ends_ref, x_ref, g0_ref, g1_ref, mask_ref, w_ref,
             qkv_ref, att_ref, lse_ref, h0_ref, x1_ref, h1_ref, bias_ref):
    T = x_ref.shape[1]
    nb = T // SLOTS
    @pl.loop(0, T // 256)
    def _(t):
        c = pl.ds(pl.multiple_of(t * 256, 256), 256)
        x = expanded(x_ref[:, c])
        h0_ref[:, c] = (x * inv_rms(x) * g0_ref[:, :1]).astype(bf16)
    for b in range(nb):
        ends = [ends_ref[b, j] for j in range(3)]
        marks = jnp.broadcast_to(mask_ref[:1, b * SLOTS:(b + 1) * SLOTS], (128, SLOTS)).T
        for qb in range(2):
            nk = 256 * (qb + 1)
            for q0 in (0, 128):
                bias_ref[b, :nk, qb * 256 + q0: qb * 256 + q0 + 128] = bias_block(ends, marks[:nk], 0, nk, qb * 256 + q0, 128)
    @pl.loop(0, 9)
    def _(m):
        r = pl.ds(pl.multiple_of(m * 256, 256), 256)
        qkv_ref[r, :] = nn(w_ref[r, :], h0_ref[...]).astype(bf16)
    for b in range(nb):
        cols = slice(b * SLOTS, (b + 1) * SLOTS)
        @pl.loop(0, HEADS // 2)
        def _(hp):
            for hh in range(2):
                h = hp * 2 + hh
                off = pl.multiple_of(h * HEAD_DIM, HEAD_DIM)
                q = qkv_ref[pl.ds(off, HEAD_DIM), cols] * bf16(HEAD_DIM ** -0.5)
                k = qkv_ref[pl.ds(off + D, HEAD_DIM), cols].T
                v = qkv_ref[pl.ds(off + 2 * D, HEAD_DIM), cols]
                for qb in range(2):
                    nk, lo = 256 * (qb + 1), qb * 256
                    s = nn(k[:nk], q[:, lo:lo + 256]) + bias_ref[b, :nk, lo:lo + 256]
                    mx = jnp.max(s, axis=0, keepdims=True)
                    p = jnp.exp(s - mx)
                    tot = jnp.sum(p, axis=0, keepdims=True)
                    lse_ref[pl.ds(h, 1), b * SLOTS + lo: b * SLOTS + lo + 256] = mx + jnp.log(tot)
                    low = (p * (1.0 / tot)).astype(bf16)
                    att_ref[pl.ds(off, HEAD_DIM), b * SLOTS + lo: b * SLOTS + lo + 256] = nn(v[:, :nk], low).astype(bf16)
    @pl.loop(0, T // 256)
    def _(t):
        c = pl.ds(pl.multiple_of(t * 256, 256), 256)
        x = expanded(x_ref[:, c])
        a = nn(w_ref[3 * D:, :], att_ref[:, c])
        x1 = expanded(jnp.where(last_row(x.shape), 0.0, x + (a - jnp.mean(a, axis=0, keepdims=True))))
        x1_ref[:, c] = x1
        h1_ref[:, c] = (x1 * inv_rms(x1) * g1_ref[:, :1]).astype(bf16)

C0 = 0.7978845608028654
def gelu_both(u):
    u2 = u * u
    inner = C0 * u * (1.0 + 0.044715 * u2)
    t = jnp.tanh(inner)
    half = 0.5 * (1.0 + t)
    slope = half + 0.5 * u * (1.0 - t * t) * (C0 * (1.0 + 3 * 0.044715 * u2))
    return u * half, slope

def norm_back(x, r, gain, dh):
    e = gain * dh
    dx = r * e - x * (r * r * r) * jnp.mean(x * e, axis=0, keepdims=True)
    return dx, dh * x * r

def lane_fold(v):
    return sum(v[:, i * 128:(i + 1) * 128] for i in range(v.shape[1] // 128))

def ffn(g_ref, g1_ref, mask_ref, x1_ref, h1_ref, w1_ref, wd_ref,
        out1_ref, dy_ref, gw1_ref, gwd_ref, gg_ref, dm_ref, z_ref, du_ref, u_ref, macc, hacc):
    T = g_ref.shape[1]
    nt_ = T // 256
    @pl.loop(0, nt_)
    def _(t):
        c = pl.ds(pl.multiple_of(t * 256, 256), 256)
        g = g_ref[:, c] * mask_ref[:1, c]
        dm_ref[:, c] = (g - jnp.mean(g, axis=0, keepdims=True)).astype(bf16)
    macc[...] = jnp.zeros_like(macc)
    hacc[...] = jnp.zeros_like(hacc)
    @pl.loop(0, FF // CHUNK)
    def _(p):
        base = p * CHUNK
        @pl.loop(0, CHUNK // 256)
        def _(m):
            r = pl.ds(pl.multiple_of(base + m * 256, 256), 256)
            rl = pl.ds(pl.multiple_of(m * 256, 256), 256)
            for n in range(T // 512):
                cs = slice(n * 512, (n + 1) * 512)
                z, slope = gelu_both(nn(w1_ref[r, :], h1_ref[:, cs]))
                z_ref[rl, cs] = z.astype(bf16)
                du_ref[rl, cs] = (nn(wd_ref[r, :], dm_ref[:, cs]) * slope).astype(bf16)
        rows = pl.ds(pl.multiple_of(base, CHUNK), CHUNK)
        @pl.loop(0, 3)
        def _(m):
            o = pl.ds(pl.multiple_of(m * 256, 256), 256)
            macc[o, :] += tn(wd_ref[rows, o], z_ref[...])
            hacc[o, :] += tn(w1_ref[rows, o], du_ref[...])
            r = pl.ds(pl.multiple_of(base + m * 256, 256), 256)
            gw1_ref[r, :] = nt(du_ref[o, :], h1_ref[...]).astype(gw1_ref.dtype)
            gwd_ref[r, :] = nt(z_ref[o, :], dm_ref[...]).astype(gwd_ref.dtype)
    gg_ref[...] = jnp.zeros_like(gg_ref)
    @pl.loop(0, nt_)
    def _(t):
        c = pl.ds(pl.multiple_of(t * 256, 256), 256)
        x1, m = x1_ref[:, c], macc[:, c]
        out1_ref[:, c] = x1 + (m - jnp.mean(m, axis=0, keepdims=True))
        g = g_ref[:, c] * mask_ref[:1, c]
        dx, gg = norm_back(x1, inv_rms(x1), g1_ref[:, :1], hacc[:, c])
        gg_ref[...] += lane_fold(gg)
        dy_ref[:, c] = g + dx - dx[D - 1:, :]

def attn_bwd(ends_ref, x_ref, g0_ref, mask_ref, w_ref, qkv_ref, att_ref, lse_ref, h0_ref, dy_ref,
             out0_ref, gw_ref, gg_ref, da_ref, dat_ref, dqkv_ref, bias_ref):
    T = x_ref.shape[1]
    nb = T // SLOTS
    for b in range(nb):
        ends = [ends_ref[b, j] for j in range(3)]
        marks = jnp.broadcast_to(mask_ref[:1, b * SLOTS:(b + 1) * SLOTS], (128, SLOTS)).T
        for qb in range(2):
            nk = 256 * (qb + 1)
            for q0 in (0, 128):
                bias_ref[b, :nk, qb * 256 + q0: qb * 256 + q0 + 128] = bias_block(ends, marks[:nk], 0, nk, qb * 256 + q0, 128)
    @pl.loop(0, T // 256)
    def _(t):
        c = pl.ds(pl.multiple_of(t * 256, 256), 256)
        dy = dy_ref[:, c]
        da_ref[:, c] = (dy - jnp.mean(dy, axis=0, keepdims=True)).astype(bf16)
    @pl.loop(0, 3)
    def _(m):
        o = pl.ds(pl.multiple_of(m * 256, 256), 256)
        r = pl.ds(pl.multiple_of(3 * D + m * 256, 256), 256)
        gw_ref[r, :] = nt(da_ref[o, :], att_ref[...]).astype(gw_ref.dtype)
        dat_ref[o, :] = tn(w_ref[3 * D:, o], da_ref[...]).astype(bf16)
    for b in range(nb):
        cols = slice(b * SLOTS, (b + 1) * SLOTS)
        @pl.loop(0, HEADS)
        def _(h):
            off = pl.multiple_of(h * HEAD_DIM, HEAD_DIM)
            q = qkv_ref[pl.ds(off, HEAD_DIM), cols] * bf16(HEAD_DIM ** -0.5)
            kt = qkv_ref[pl.ds(off + D, HEAD_DIM), cols]
            k = kt.T
            v = qkv_ref[pl.ds(off + 2 * D, HEAD_DIM), cols].T
            d = dat_ref[pl.ds(off, HEAD_DIM), cols]
            dks, dvs = [], []
            for qb in range(2):
                nk, lo = 256 * (qb + 1), qb * 256
                s = nn(k[:nk], q[:, lo:lo + 256]) + bias_ref[b, :nk, lo:lo + 256]
                p = jnp.exp(s - lse_ref[pl.ds(h, 1), b * SLOTS + lo: b * SLOTS + lo + 256])
                dp = nn(v[:nk], d[:, lo:lo + 256])
                ds = (p * (dp - jnp.sum(p * dp, axis=0, keepdims=True))).astype(bf16)
                low = p.astype(bf16)
                dqkv_ref[pl.ds(off, HEAD_DIM), b * SLOTS + lo: b * SLOTS + lo + 256] = (nn(kt[:, :nk], ds) * HEAD_DIM ** -0.5).astype(bf16)
                dks.append(nt(q[:, lo:lo + 256], ds))
                dvs.append(nt(d[:, lo:lo + 256], low))
            for at, parts in ((D, dks), (2 * D, dvs)):
                dqkv_ref[pl.ds(off + at, HEAD_DIM), b * SLOTS: b * SLOTS + 256] = (parts[0] + parts[1][:, :256]).astype(bf16)
                dqkv_ref[pl.ds(off + at, HEAD_DIM), b * SLOTS + 256: (b + 1) * SLOTS] = parts[1][:, 256:].astype(bf16)
    @pl.loop(0, 9)
    def _(m):
        r = pl.ds(pl.multiple_of(m * 256, 256), 256)
        gw_ref[r, :] = nt(dqkv_ref[r, :], h0_ref[...]).astype(gw_ref.dtype)
    gg_ref[...] = jnp.zeros_like(gg_ref)
    @pl.loop(0, T // 256)
    def _(t):
        c = pl.ds(pl.multiple_of(t * 256, 256), 256)
        x = expanded(x_ref[:, c])
        dh = tn(w_ref[:3 * D, :], dqkv_ref[:, c])
        dx, gg = norm_back(x, inv_rms(x), g0_ref[:, :1], dh)
        gg_ref[...] += lane_fold(gg)
        out0_ref[:, c] = dy_ref[:, c] + dx - dx[D - 1:, :]

V = pl.BlockSpec(memory_space=pltpu.VMEM)
S = pl.BlockSpec(memory_space=pltpu.SMEM)
def sds(*shape, dtype=f32):
    return jax.ShapeDtypeStruct(shape, dtype)
PARAMS = pltpu.CompilerParams(vmem_limit_bytes=60 * 2**20)

def run_attn_fwd(ends, x, g0, g1, mask, w):
    T = x.shape[1]
    return pl.pallas_call(attn_fwd, in_specs=[S] + [V] * 5, out_specs=[V] * 6,
        out_shape=[sds(3 * D, T, dtype=bf16), sds(D, T, dtype=bf16), sds(16, T), sds(D, T, dtype=bf16), sds(D, T), sds(D, T, dtype=bf16)],
        scratch_shapes=[pltpu.VMEM((T // SLOTS, SLOTS, SLOTS), f32)], compiler_params=PARAMS, name="attn_fwd")(ends, x, g0, g1, mask, w)

def run_ffn(g, g1, mask, x1, h1, w1, wd, gdt=bf16):
    T = g.shape[1]
    return pl.pallas_call(ffn, in_specs=[V] * 7, out_specs=[V] * 5,
        out_shape=[sds(D, T), sds(D, T), sds(FF, D, dtype=gdt), sds(FF, D, dtype=gdt), sds(D, 128)],
        scratch_shapes=[pltpu.VMEM((D, T), bf16), pltpu.VMEM((CHUNK, T), bf16), pltpu.VMEM((CHUNK, T), bf16), pltpu.VMEM((8, 128), f32), pltpu.VMEM((D, T), f32), pltpu.VMEM((D, T), f32)],
        compiler_params=PARAMS, name="ffn")(g, g1, mask, x1, h1, w1, wd)

def run_attn_bwd(ends, x, g0, mask, w, qkv, att, lse, h0, dy, gdt=bf16):
    T = x.shape[1]
    return pl.pallas_call(attn_bwd, in_specs=[S] + [V] * 9, out_specs=[V] * 3,
        out_shape=[sds(D, T), sds(FF, D, dtype=gdt), sds(D, 128)],
        scratch_shapes=[pltpu.VMEM((D, T), bf16), pltpu.VMEM((D, T), bf16), pltpu.VMEM((3 * D, T), bf16), pltpu.VMEM((T // SLOTS, SLOTS, SLOTS), f32)],
        compiler_params=PARAMS, name="attn_bwd")(ends, x, g0, mask, w, qkv, att, lse, h0, dy)


MESH = pl.DeviceIdType.MESH
HBM = pl.BlockSpec(memory_space=pl.ANY)


def push(src, dst, send, recv, device):
    copy = pltpu.make_async_remote_copy(
        src_ref=src, dst_ref=dst, send_sem=send, recv_sem=recv, device_id=device, device_id_type=MESH
    )
    copy.start()
    return copy


DIST = (0, 1, 3, 2)
TILE = 256
SCALE = HEAD_DIM ** -0.5
KIND_A, KIND_D, KIND_W = 0, 1, 2
SETS = 12
PLANES = (3, 0, 1, 2)


def wide(v):
    return v.astype(f32)


def square(v):
    return v.reshape(-1, D)


def at_step(k):
    return (1 - k // 2) * k + (k // 2) * (5 - k)


def layer_kernel(
    len_ref, mask_ref, gain_ref, stream, w_ref, wd_ref,
    out, first, down, gain_out, spill_x, spill_q,
    fa, fw, fd, X, G, xt, gt, QKV, ATT, H0, H1, DM, MACC, HACC, BIAS, LSE, MK, GR, GCOL, GG, GV, GL, GT,
    STG, ACC, L1, L2, L3W, L3A, L3D, FIN, FIND,
    zs, zr, ps, pr, ss, sr, p1s, p1r, p2s, p2r, p3s, rw, ra, rd, i_s, i_r, local, gs, gr,
):
    s, d = lax.axis_index("section"), lax.axis_index("dp")
    x, y, z, xy = lax.rem(d, 2), lax.rem(d // 2, 2), d // 4, lax.rem(d, 4)
    t = 1 - s
    over_y, over_x = (1 - y) * 2 + x, y * 2 + 1 - x
    xy1, xy2, xy3 = t * over_y + s * over_x, s * over_y + t * over_x, 3 - xy
    sib, n1, n2 = (t, d), (s, z * 4 + xy1), (s, z * 4 + xy2)
    T = X.shape[1]
    nb = T // SLOTS
    tiles = T // TILE
    col = lambda i: pl.ds(pl.multiple_of(i * TILE, TILE), TILE)
    at_plane = lambda p: (s, p * 4 + xy)

    def plane(i):
        return lax.rem(z + 4 - DIST[i], 4)

    def wait_recv(dst, sem):
        pltpu.make_async_remote_copy(
            src_ref=dst, dst_ref=dst, send_sem=sem, recv_sem=sem, device_id=sib, device_id_type=MESH
        ).wait_recv()

    def wait_send(src, sem):
        pltpu.make_async_remote_copy(
            src_ref=src, dst_ref=src, send_sem=sem, recv_sem=sem, device_id=sib, device_id_type=MESH
        ).wait_send()

    def move(src, dst, sem):
        pltpu.make_async_copy(src, dst, sem).start()

    def moved(src, dst, sem):
        pltpu.make_async_copy(src, dst, sem).wait()

    def slab(kind, zz, q, h):
        return fd.at[:, zz, q, h] if kind == KIND_D else (fa, None, fw)[kind].at[zz, q, h]

    def group(kind, zz, h):
        return fd.at[:, zz, :, h] if kind == KIND_D else (fa, None, fw)[kind].at[zz, :, h]

    def Z(kind, i):
        own = slab(kind, z, xy, s)
        push(own, own, zs.at[kind, i], zr.at[kind, i], at_plane(lax.rem(z + DIST[i], 4)))

    def A(kind, i):
        here = slab(kind, plane(i), xy, s)
        if i:
            wait_recv(here, zr.at[kind, i])
        if 0 < i < 3:
            Z(kind, i + 1)
        elif i == 3 and kind < 2:
            Z(kind + 1, 1)
        push(here, here, ps.at[kind, i, 0], pr.at[kind, i, 0], n1)
        push(here, here, ps.at[kind, i, 1], pr.at[kind, i, 1], n2)

    def B(kind, i):
        here = slab(kind, plane(i), xy1, s)
        wait_recv(here, pr.at[kind, i, 0])
        push(here, here, ps.at[kind, i, 2], pr.at[kind, i, 2], n2)

    def C(kind, i):
        zz = plane(i)
        wait_recv(slab(kind, zz, xy2, s), pr.at[kind, i, 1])
        wait_recv(slab(kind, zz, xy3, s), pr.at[kind, i, 2])
        here = group(kind, zz, s)
        push(here, here, ps.at[kind, i, 3], pr.at[kind, i, 3], sib)

    def E(kind, i):
        wait_recv(group(kind, plane(i), t), pr.at[kind, i, 3])

    def sent(kind):
        for i in range(4):
            zz = plane(i)
            if i:
                wait_send(slab(kind, z, xy, s), zs.at[kind, i])
            wait_send(slab(kind, zz, xy, s), ps.at[kind, i, 0])
            wait_send(slab(kind, zz, xy, s), ps.at[kind, i, 1])
            wait_send(slab(kind, zz, xy1, s), ps.at[kind, i, 2])
            wait_send(group(kind, zz, s), ps.at[kind, i, 3])

    def to_sibling(j):
        push(STG.at[j % 2 if isinstance(j, int) else lax.rem(j, 2), :, t], ACC.at[j], ss.at[j], sr.at[j], sib)

    def staged_free(j):
        wait_send(STG.at[0, :, t], ss.at[j])

    def R1(j):
        wait_recv(ACC.at[j], sr.at[j])
        for q in range(4):
            ACC[j, q] = (wide(ACC[j, q]) + wide(STG[j % 2, q, s])).astype(bf16)
        push(ACC.at[j, xy2], L1.at[j, 0], p1s.at[j, 0], p1r.at[j, 0], n2)
        push(ACC.at[j, xy3], L1.at[j, 1], p1s.at[j, 1], p1r.at[j, 1], n2)

    def R2(j):
        wait_recv(L1.at[j, 0], p1r.at[j, 0])
        wait_recv(L1.at[j, 1], p1r.at[j, 1])
        ACC[j, xy] = (wide(ACC[j, xy]) + wide(L1[j, 0])).astype(bf16)
        ACC[j, xy1] = (wide(ACC[j, xy1]) + wide(L1[j, 1])).astype(bf16)
        push(ACC.at[j, xy1], L2.at[j], p2s.at[j], p2r.at[j], n1)

    def ends_of(j):
        if j >= 8:
            p = PLANES[j - 8]
            return [(z != p, ACC.at[j, xy], L3A.at[z], p3s.at[j, 0], ra.at[z], p)]
        k = j // 2
        p = plane(k)
        if j % 2 == 0:
            return [(None, ACC.at[j, xy], L3W.at[k - 1], p3s.at[j, 0], rw.at[k - 1], p)] if k else []
        made = []
        for sub in range(2):
            to = 2 * lax.rem(p, 2) + sub
            made.append((z != to, ACC.at[j, xy, sub], L3D.at[p // 2, z], p3s.at[j, sub], rd.at[p // 2, z], to))
        return made

    def guarded(cond, act):
        act() if cond is None else pl.when(cond)(act)

    def R3(j):
        wait_recv(L2.at[j], p2r.at[j])
        ACC[j, xy] = (wide(ACC[j, xy]) + wide(L2[j])).astype(bf16)
        for cond, src, dst, ssem, rsem, to in ends_of(j):
            guarded(cond, lambda src=src, dst=dst, ssem=ssem, rsem=rsem, to=to: push(src, dst, ssem, rsem, at_plane(to)) and None)

    def scattered(j):
        wait_send(ACC.at[j, xy2], p1s.at[j, 0])
        wait_send(ACC.at[j, xy3], p1s.at[j, 1])
        wait_send(ACC.at[j, xy1], p2s.at[j])
        for cond, src, dst, ssem, rsem, to in ends_of(j):
            guarded(cond, lambda src=src, ssem=ssem: wait_send(src, ssem))

    barrier = pltpu.get_barrier_semaphore()
    partners = [sib, n1, n2, *(at_plane(lax.rem(z + r, 4)) for r in (1, 2, 3))]
    for device in partners:
        pl.semaphore_signal(barrier, inc=1, device_id=device, device_id_type=MESH)
    pl.semaphore_wait(barrier, len(partners))

    mine, other = pl.ds(pl.multiple_of(s * T, T), T), pl.ds(pl.multiple_of(t * T, T), T)
    top = pl.ds(0, D - 8)

    def rows_of(part):
        return stream.at[top, 0, part], stream.at[pl.ds(D - 9, 8), 0, part]

    @pl.when(s == 0)
    def _():
        push(w_ref.at[1], fa.at[z, xy, 1], i_s.at[0], i_r.at[0], sib)
        move(w_ref.at[0], fa.at[z, xy, 0], local.at[0])

    @pl.when(s == 1)
    def _():
        push(w_ref.at[0], fw.at[z, xy, 0], i_s.at[0], i_r.at[0], sib)
        move(w_ref.at[1], fw.at[z, xy, 1], local.at[0])

    push(wd_ref.at[t], fd.at[s, z, xy, t], i_s.at[1], i_r.at[1], sib)
    move(wd_ref.at[s], fd.at[s, z, xy, s], local.at[1])
    push(gain_ref, GR.at[s], i_s.at[2], i_r.at[2], sib)
    move(gain_ref, GR.at[s], local.at[2])

    def stream_in(keep, tail):
        def go():
            a, b = rows_of(mine)
            move(a, keep.at[top], local.at[3])
            move(b, tail, local.at[4])
        return go

    def stream_out(give, tail):
        def go():
            a, b = rows_of(other)
            push(a, give.at[top], i_s.at[3], i_r.at[3], sib)
            push(b, tail, i_s.at[4], i_r.at[4], sib)
        return go

    pl.when(s == 0)(stream_in(X, xt))
    pl.when(s == 1)(stream_in(G, gt))

    @pl.when(s == 0)
    def _():
        moved(w_ref.at[0], fa.at[z, xy, 0], local.at[0])
        wait_send(w_ref.at[1], i_s.at[0])

    @pl.when(s == 1)
    def _():
        wait_recv(fa.at[z, xy, 1], i_r.at[0])

    Z(KIND_A, 1)
    A(KIND_A, 0)
    pl.when(s == 0)(stream_out(X, xt))
    pl.when(s == 1)(stream_out(G, gt))

    def lengths(b):
        return [len_ref[s * nb + b, j] for j in range(4)]

    shifts, ends = [], []
    for b in range(nb):
        size = lengths(b)
        stops = [size[0], size[0] + size[1], size[0] + size[1] + size[2]]
        starts = [0, *stops]
        shifts.append(sum(jnp.where(size[j] == LONGEST, starts[j], 0) for j in range(1, 4)))
        ends.append(stops)

    moved(gain_ref, GR.at[s], local.at[2])
    wait_recv(GR.at[t], i_r.at[2])
    for j in range(2):
        GCOL[j] = jnp.broadcast_to(GR[j], (128, D)).T

    def turn(ref, tail, b):
        cols = slice(b * SLOTS, (b + 1) * SLOTS)
        amount = lax.rem(SLOTS - shifts[b], SLOTS)
        ref[D - 8:, cols] = jnp.concatenate([tail[1:, cols], jnp.zeros((1, SLOTS), f32)], axis=0)

        @pl.loop(0, 8)
        def _(i):
            r = pl.ds(pl.multiple_of(i * 96, 96), 96)
            ref[r, cols] = pltpu.roll(ref[r, cols], amount, 1)

    def x_arrived():
        @pl.when(s == 0)
        def _():
            a, b = rows_of(mine)
            moved(a, X.at[top], local.at[3])
            moved(b, xt, local.at[4])

        @pl.when(s == 1)
        def _():
            wait_recv(X.at[top], i_r.at[3])
            wait_recv(xt, i_r.at[4])

    def g_arrived():
        @pl.when(s == 1)
        def _():
            a, b = rows_of(mine)
            moved(a, G.at[top], local.at[3])
            moved(b, gt, local.at[4])

        @pl.when(s == 0)
        def _():
            wait_recv(G.at[top], i_r.at[3])
            wait_recv(gt, i_r.at[4])

    def masks():
        for b in range(nb):
            cols = slice(b * SLOTS, (b + 1) * SLOTS)
            amount = lax.rem(SLOTS - shifts[b], SLOTS)
            live = wide(mask_ref[:, pl.ds(pl.multiple_of(s * T + b * SLOTS, SLOTS), SLOTS)])
            MK[:, cols] = pltpu.roll(jnp.broadcast_to(live, (8, SLOTS)), amount, 1)
            marks = jnp.broadcast_to(MK[:1, cols], (128, SLOTS)).T
            for qb in range(2):
                for half in range(2):
                    shape = (TILE, 128)
                    kp = lax.broadcasted_iota(jnp.int32, shape, 0) + qb * TILE
                    qp = lax.broadcasted_iota(jnp.int32, shape, 1) + qb * TILE + half * 128

                    def doc(p):
                        first_place = p + shifts[b]
                        first_place = first_place - jnp.where(first_place >= SLOTS, SLOTS, 0)
                        return sum((first_place >= e).astype(jnp.int32) for e in ends[b])

                    seen = (doc(kp) == doc(qp)) & (kp <= qp)
                    seen = seen & ((marks[qb * TILE:(qb + 1) * TILE] > 0.5) | (kp == qp))
                    BIAS[b, qb, :, half * 128:(half + 1) * 128] = jnp.where(seen, 0.0, MASKED)

    def normed_in():
        @pl.loop(0, tiles)
        def _(i):
            c = col(i)
            v = expanded(X[:, c])
            X[D - 8:, c] = v[D - 8:]
            H0[:, c] = (v * inv_rms(v) * GCOL[0, :, :1]).astype(bf16)

    def cotangent():
        @pl.loop(0, tiles)
        def _(i):
            c = col(i)
            v = G[:, c] * MK[:1, c]
            G[:, c] = v
            DM[:, c] = (v - jnp.mean(v, axis=0, keepdims=True)).astype(bf16)

    masks()
    B(KIND_A, 0)
    x_arrived()
    turn(X, xt, 0)
    A(KIND_A, 1)
    turn(X, xt, 1)
    C(KIND_A, 0)
    normed_in()
    move(X, spill_x, local.at[5])
    B(KIND_A, 1)
    A(KIND_A, 2)

    @pl.when(s == 0)
    def _():
        wait_recv(fw.at[z, xy, 0], i_r.at[0])

    @pl.when(s == 1)
    def _():
        moved(w_ref.at[1], fw.at[z, xy, 1], local.at[0])
        wait_send(w_ref.at[0], i_s.at[0])

    moved(wd_ref.at[s], fd.at[s, z, xy, s], local.at[1])
    wait_recv(fd.at[t, z, xy, s], i_r.at[1])
    C(KIND_A, 1)
    B(KIND_A, 2)
    g_arrived()
    turn(G, gt, 0)
    A(KIND_A, 3)
    turn(G, gt, 1)
    C(KIND_A, 2)
    cotangent()
    B(KIND_A, 3)
    A(KIND_D, 0)
    C(KIND_A, 3)
    for i in range(4):
        E(KIND_A, i)

    def ticks(index, table):
        for at, steps in table.items():
            @pl.when(index == at)
            def _(steps=steps):
                for act, *args in steps:
                    act(*args)

    @pl.loop(0, 3)
    def _(p):
        rows = pl.ds(pl.multiple_of(p * D, D), D)
        QKV[rows, :] = nn(square(fa[p]), H0[...]).astype(bf16)
        ticks(p, {0: [(B, KIND_D, 0)], 2: [(A, KIND_D, 1)]})

    units = [(h, qb) for h in range(4) for qb in range(2)]

    def spots(i):
        b = i // 3
        def spot(u):
            head = lax.rem(i, 3) * 4 + u[0]
            return head, pl.multiple_of(head * HEAD_DIM, HEAD_DIM), pl.ds(pl.multiple_of(b * SLOTS + u[1] * TILE, TILE), TILE)
        return b, spot

    def three(off, c):
        return [QKV[pl.ds(off + j * D, HEAD_DIM), c] for j in range(3)]

    @pl.loop(0, 3 * nb)
    def _(i):
        b, spot = spots(i)
        scores, probs = {}, {}
        for u in units:
            head, off, c = spot(u)
            q, k, v = three(off, c)
            scores[u] = nn(k.T, q * bf16(SCALE))
        for u in units:
            head, off, c = spot(u)
            v = scores[u] + BIAS[b, u[1]]
            highest = jnp.max(v, axis=0, keepdims=True)
            p = jnp.exp(v - highest)
            total = jnp.sum(p, axis=0, keepdims=True)
            LSE[pl.ds(head, 1), c] = highest + jnp.log(total)
            probs[u] = (p * (1.0 / total)).astype(bf16)
        for u in units:
            head, off, c = spot(u)
            ATT[pl.ds(off, HEAD_DIM), c] = nn(QKV[pl.ds(off + 2 * D, HEAD_DIM), c], probs[u]).astype(bf16)
        ticks(i, {0: [(C, KIND_D, 0)], 1: [(B, KIND_D, 1)], 3: [(A, KIND_D, 2), (C, KIND_D, 1)], 5: [(B, KIND_D, 2)]})

    move(QKV, spill_q, local.at[6])
    moved(X, spill_x, local.at[5])

    @pl.loop(0, tiles)
    def _(i):
        c = col(i)
        a = nn(square(fa[3]), ATT[:, c])
        v = X[:, c] + (a - jnp.mean(a, axis=0, keepdims=True))
        v = expanded(jnp.where(last_row(v.shape), 0.0, v))
        X[:, c] = v
        H1[:, c] = (v * inv_rms(v) * GCOL[1, :, :1]).astype(bf16)
        ticks(i, {1: [(A, KIND_D, 3)], 2: [(C, KIND_D, 2)], 3: [(B, KIND_D, 3)]})

    MACC[...] = jnp.zeros_like(MACC)
    HACC[...] = jnp.zeros_like(HACC)
    moved(QKV, spill_q, local.at[6])
    A(KIND_W, 0)
    C(KIND_D, 3)
    for i in range(4):
        E(KIND_D, i)
    B(KIND_W, 0)
    A(KIND_W, 1)
    C(KIND_W, 0)
    B(KIND_W, 1)
    E(KIND_W, 0)
    ZT, DU = QKV.at[pl.ds(0, D)], QKV.at[pl.ds(D, D)]

    def stage_rows(slot, left, right, by_plane):
        for m in range(2):
            v = nt(left(m), right).astype(bf16)
            if by_plane:
                for a in range(2):
                    for h in range(2):
                        for sub in range(2):
                            lo = a * 192 + h * 96 + sub * 48
                            STG[slot, 2 * m + a, h, sub] = v[lo:lo + 48]
            else:
                for q in range(4):
                    for h in range(2):
                        STG[slot, q, h, m] = v[q * 96 + h * 48:q * 96 + h * 48 + 48]

    FFN_TICKS = {
        (0, "a1"): [(A, KIND_W, 2)], (0, "a2"): [(C, KIND_W, 1)], (0, "a3"): [(B, KIND_W, 2)],
        (0, "w"): [(A, KIND_W, 3)], (0, "d"): [(C, KIND_W, 2)],
        (0, "t0"): [(B, KIND_W, 3), (R1, 0)], (0, "t1"): [(R1, 1), (E, KIND_W, 1)],
        (1, "a0"): [(C, KIND_W, 3)],
        (1, "t0"): [(R1, 2), (E, KIND_W, 2)], (1, "t1"): [(R2, 0), (R1, 3)],
        (2, "a2"): [(R2, 1)], (2, "w"): [(R3, 0)],
        (2, "t0"): [(R1, 4)], (2, "t1"): [(R1, 5), (E, KIND_W, 3)],
        (3, "a0"): [(R3, 1)], (3, "a1"): [(R2, 2)], (3, "w"): [(R3, 2)], (3, "d"): [(R2, 3)],
        (3, "t0"): [(R1, 6)], (3, "t1"): [(R1, 7)],
    }

    @pl.loop(0, 4)
    def _(k):
        p = lax.rem(z + 4 - at_step(k), 4)

        def tick(name):
            ticks(k, {kk: steps for (kk, n), steps in FFN_TICKS.items() if n == name})

        def down_rows():
            return square(fd[p // 2, pl.ds(2 * lax.rem(p, 2), 2)])

        @pl.loop(0, tiles)
        def _(i):
            c = col(i)
            act, slope = gelu_both(nn(square(fw[p]), H1[:, c]))
            ZT[:, c] = act.astype(bf16)
            DU[:, c] = (nn(down_rows(), DM[:, c]) * slope).astype(bf16)
            for a in range(4):
                ticks(i * 8 + k, {a * 8 + kk: steps for (kk, n), steps in FFN_TICKS.items() if n == f"a{a}"})

        @pl.when(k > 0)
        def _():
            staged_free(2 * k - 2)
        stage_rows(0, lambda m: DU[m * 384:(m + 1) * 384, :], H1[...], True)
        to_sibling(2 * k)
        tick("w")

        @pl.when(k > 0)
        def _():
            staged_free(2 * k - 1)
        stage_rows(1, lambda m: ZT[m * 384:(m + 1) * 384, :], DM[...], False)
        to_sibling(2 * k + 1)
        tick("d")
        for half in range(2):
            c = slice(half * SLOTS, (half + 1) * SLOTS)
            MACC[:, c] += tn(down_rows(), ZT[:, c])
        tick("t0")
        for half in range(2):
            c = slice(half * SLOTS, (half + 1) * SLOTS)
            HACC[:, c] += tn(square(fw[p]), DU[:, c])
        tick("t1")

    move(spill_q, QKV, local.at[6])
    GG[...] = jnp.zeros_like(GG)

    @pl.loop(0, tiles)
    def _(i):
        c = col(i)
        v, m = X[:, c], MACC[:, c]
        MACC[:, c] = v + (m - jnp.mean(m, axis=0, keepdims=True))
        dx, part = norm_back(v, inv_rms(v), GCOL[1, :, :1], HACC[:, c])
        GG[...] += lane_fold(part)
        G[:, c] = G[:, c] + dx - dx[D - 1:, :]
        ticks(i, {0: [(R3, 3)], 2: [(R2, 4)]})
    GV[1] = jnp.sum(GG[...].T, axis=0, keepdims=True)

    @pl.when(s == 1)
    def _():
        move(MACC, out.at[:, mine], local.at[7])

    @pl.when(s == 0)
    def _():
        push(MACC, out.at[:, mine], i_s.at[5], i_r.at[5], sib)

    move(spill_x, HACC, local.at[5])

    @pl.loop(0, tiles)
    def _(i):
        c = col(i)
        v = G[:, c]
        DM[:, c] = (v - jnp.mean(v, axis=0, keepdims=True)).astype(bf16)

    staged_free(6)
    stage_rows(0, lambda m: DM[m * 384:(m + 1) * 384, :], ATT[...], True)
    to_sibling(8)
    R3(4)
    for half in range(2):
        c = slice(half * SLOTS, (half + 1) * SLOTS)
        H1[:, c] = tn(square(fa[3]), DM[:, c]).astype(bf16)
    R1(8)
    moved(spill_q, QKV, local.at[6])

    @pl.loop(0, 3 * nb)
    def _(i):
        b, spot = spots(i)
        scores, dprobs, probs, grads = {}, {}, {}, {}
        for u in units:
            head, off, c = spot(u)
            q, k, v = three(off, c)
            scores[u] = nn(k.T, q * bf16(SCALE))
            dprobs[u] = nn(v.T, H1[pl.ds(off, HEAD_DIM), c])
        for u in units:
            head, off, c = spot(u)
            p = jnp.exp(scores[u] + BIAS[b, u[1]] - LSE[pl.ds(head, 1), c])
            dp = dprobs[u]
            grads[u] = (p * (dp - jnp.sum(p * dp, axis=0, keepdims=True))).astype(bf16)
            probs[u] = p.astype(bf16)
        for u in units:
            head, off, c = spot(u)
            q, k, _ = three(off, c)
            QKV[pl.ds(off, HEAD_DIM), c] = (nn(k, grads[u]) * SCALE).astype(bf16)
            QKV[pl.ds(off + D, HEAD_DIM), c] = nt(q * bf16(SCALE), grads[u]).astype(bf16)
            QKV[pl.ds(off + 2 * D, HEAD_DIM), c] = nt(H1[pl.ds(off, HEAD_DIM), c], probs[u]).astype(bf16)
        ticks(i, {1: [(R2, 5)], 3: [(R3, 5)], 4: [(R2, 6)]})

    staged_free(7)
    stage_rows(1, lambda m: QKV[m * 384:(m + 1) * 384, :], H0[...], True)
    to_sibling(9)
    R3(6)
    R2(7)
    staged_free(8)
    stage_rows(0, lambda m: QKV[D + m * 384:D + (m + 1) * 384, :], H0[...], True)
    to_sibling(10)
    R1(9)
    staged_free(9)
    stage_rows(1, lambda m: QKV[2 * D + m * 384:2 * D + (m + 1) * 384, :], H0[...], True)
    to_sibling(11)
    R1(10)
    moved(spill_x, HACC, local.at[5])
    GG[...] = jnp.zeros_like(GG)

    @pl.loop(0, tiles)
    def _(i):
        c = col(i)
        v = HACC[:, c]
        dh = tn(square(fa[:3]), QKV[:, c])
        dx, part = norm_back(v, inv_rms(v), GCOL[0, :, :1], dh)
        GG[...] += lane_fold(part)
        G[:, c] = G[:, c] + dx - dx[D - 1:, :]
        ticks(i, {0: [(R1, 11)], 1: [(R3, 7)], 3: [(R2, 8)]})
    GV[0] = jnp.sum(GG[...].T, axis=0, keepdims=True)

    @pl.when(s == 0)
    def _():
        move(G, out.at[:, mine], local.at[8])

    @pl.when(s == 1)
    def _():
        push(G, out.at[:, mine], i_s.at[5], i_r.at[5], sib)

    push(GV.at[t], GL.at[0], gs.at[0], gr.at[0], sib)
    R3(8)
    R2(9)
    wait_recv(GL.at[0], gr.at[0])
    GT[0] = GV[s] + GL[0]
    push(GT.at[0], GL.at[1], gs.at[1], gr.at[1], n2)
    R3(9)
    R2(10)
    wait_recv(GL.at[1], gr.at[1])
    GT[1] = GT[0] + GL[1]
    push(GT.at[1], GL.at[2], gs.at[2], gr.at[2], n1)
    R3(10)
    R2(11)
    wait_recv(GL.at[2], gr.at[2])
    GT[2] = GT[1] + GL[2]
    for r in range(3):
        push(GT.at[2], GL.at[3 + r], gs.at[3 + r], gr.at[3 + r], at_plane(lax.rem(z + 1 + r, 4)))
    R3(11)

    def total_of(v, parts):
        v = wide(v)
        for part in parts:
            v = v + wide(part)
        return v

    for k in range(3):
        wait_recv(L3W.at[k], rw.at[k])
    FIN[1] = total_of(ACC[0, xy], [L3W[k] for k in range(3)])
    for sec in range(2):
        for r in range(3):
            zz = lax.rem(z + 1 + r, 4)
            wait_recv(L3D.at[sec, zz], rd.at[sec, zz])
        far = lax.rem(z + 4 - (2 * sec + z // 2), 4)
        FIND[sec] = total_of(ACC[2 * at_step(far) + 1, xy, lax.rem(z, 2)], [L3D[sec, lax.rem(z + 1 + r, 4)] for r in range(3)])
    move(FIND.at[s], down.at[s], local.at[9])
    push(FIND.at[t], down.at[s], i_s.at[6], i_r.at[6], sib)

    @pl.when(s == 1)
    def _():
        move(FIN.at[1], first.at[1], local.at[10])

    @pl.when(s == 0)
    def _():
        push(FIN.at[1], first.at[0], i_s.at[7], i_r.at[7], sib)

    for r in range(3):
        wait_recv(GL.at[3 + r], gr.at[3 + r])
    GT[3] = GT[2] + GL[3] + GL[4] + GL[5]
    gain_out[...] = GT[3]
    for r in range(3):
        zz = lax.rem(z + 1 + r, 4)
        wait_recv(L3A.at[zz], ra.at[zz])
    FIN[0] = total_of(ACC[8 + lax.rem(z + 1, 4), xy], [L3A[lax.rem(z + 1 + r, 4)] for r in range(3)])

    @pl.when(s == 0)
    def _():
        move(FIN.at[0], first.at[0], local.at[10])

    @pl.when(s == 1)
    def _():
        push(FIN.at[0], first.at[1], i_s.at[7], i_r.at[7], sib)

    @pl.when(s == 0)
    def _():
        moved(FIN.at[0], first.at[0], local.at[10])
        wait_send(FIN.at[1], i_s.at[7])
        wait_recv(first.at[1], i_r.at[7])
        wait_send(MACC, i_s.at[5])
        moved(G, out.at[:, mine], local.at[8])

    @pl.when(s == 1)
    def _():
        moved(FIN.at[1], first.at[1], local.at[10])
        wait_send(FIN.at[0], i_s.at[7])
        wait_recv(first.at[0], i_r.at[7])
        moved(MACC, out.at[:, mine], local.at[7])
        wait_send(G, i_s.at[5])

    wait_recv(out.at[:, other], i_r.at[5])
    moved(FIND.at[s], down.at[s], local.at[9])
    wait_send(FIND.at[t], i_s.at[6])
    wait_recv(down.at[t], i_r.at[6])
    wait_send(wd_ref.at[t], i_s.at[1])
    wait_send(gain_ref, i_s.at[2])
    a, b = rows_of(other)
    wait_send(a, i_s.at[3])
    wait_send(b, i_s.at[4])
    for n in range(6):
        wait_send(GT.at[0], gs.at[n])
    for kind in range(3):
        sent(kind)
    staged_free(10)
    staged_free(11)
    for j in range(SETS):
        scattered(j)


def finish_kernel(len_ref, pre, out, a, b, ins, outs):
    n = pre.shape[1] // SLOTS
    cols = lambda i: pl.ds(i * SLOTS, SLOTS)
    load = lambda i: pltpu.make_async_copy(pre.at[:, cols(i)], a.at[i % 2], ins.at[i % 2])
    save = lambda i: pltpu.make_async_copy(b.at[i % 2], out.at[:, 0, cols(i)], outs.at[i % 2])
    load(0).start()
    for i in range(n):
        load(i).wait()
        if i + 1 < n:
            load(i + 1).start()
        start, shift = 0, 0
        for j in range(4):
            shift = shift + jnp.where(len_ref[i, j] == LONGEST, start, 0)
            start = start + len_ref[i, j]
        if i >= 2:
            save(i - 2).wait()
        b[i % 2] = pltpu.roll(a[i % 2], shift, 1)[:D - 1]
        save(i).start()
    for i in range(max(n - 2, 0), n):
        save(i).wait()


def layer(lengths, mask, gain, stream, w, wd):
    T = stream.shape[2] // 2
    dma = lambda *shape: pltpu.SemaphoreType.DMA(shape)
    bulk = lambda *shape: pltpu.VMEM(shape, bf16)
    full = lambda *shape: pltpu.VMEM(shape, f32)
    scratch = [
        bulk(4, 4, 2, 96, D), bulk(4, 4, 2, 96, D), bulk(2, 4, 4, 2, 48, D),
        full(D, T), full(D, T), full(8, T), full(8, T),
        bulk(3 * D, T), bulk(D, T), bulk(D, T), bulk(D, T), bulk(D, T),
        full(D, T), full(D, T), full(T // SLOTS, 2, TILE, TILE), full(16, T), full(8, T),
        full(2, 1, D), full(2, D, 128), full(D, 128), full(2, 1, D), full(6, 1, D), full(4, 1, D),
        bulk(2, 4, 2, 2, 48, D), bulk(SETS, 4, 2, 48, D), bulk(SETS, 2, 2, 48, D), bulk(SETS, 2, 48, D),
        bulk(3, 2, 48, D), bulk(4, 2, 48, D), bulk(2, 4, 48, D), full(2, 2, 48, D), full(2, 48, D),
        dma(3, 4), dma(3, 4), dma(3, 4, 4), dma(3, 4, 4),
        dma(SETS), dma(SETS), dma(SETS, 2), dma(SETS, 2), dma(SETS), dma(SETS),
        dma(SETS, 2), dma(3), dma(4), dma(2, 4),
        dma(8), dma(8), dma(11), dma(6), dma(6),
    ]
    out, first, down, gains, _, _ = pl.pallas_call(
        layer_kernel,
        in_specs=[S, V, HBM, HBM, HBM, HBM],
        out_specs=[HBM, HBM, HBM, V, HBM, HBM],
        out_shape=[
            sds(D, 2 * T), sds(2, 2, 48, D), sds(2, 48, D), sds(1, D), sds(D, T), sds(3 * D, T, dtype=bf16),
        ],
        scratch_shapes=scratch,
        compiler_params=pltpu.CompilerParams(collective_id=1, has_side_effects=True, vmem_limit_bytes=VMEM_MOST),
        name="layer",
    )(lengths, mask, gain, stream, w.reshape(2, 96, D), wd.reshape(2, 48, D))
    final = pl.pallas_call(
        finish_kernel,
        in_specs=[S, HBM],
        out_specs=HBM,
        out_shape=sds(D - 1, 1, 2 * T),
        scratch_shapes=[full(2, D, SLOTS), full(2, D - 1, SLOTS), dma(2), dma(2)],
        compiler_params=pltpu.CompilerParams(vmem_limit_bytes=32 * 2**20),
        name="finish",
    )(lengths, out)
    return final, first.reshape(192, D), down.reshape(96, D), gains


def separate(own, stream, w, wd, gain, doc_lengths, pad_mask, sections, groups):
    s, d = own
    stream = jnp.pad(stream[:, 0], ((0, 1), (0, 0)))
    gain = jnp.broadcast_to(gain[0][:, None], (D, 128))
    T = stream.shape[1] // sections
    nb = T // SLOTS
    own_docs = lax.dynamic_slice_in_dim(doc_lengths, s * nb, nb, axis=0)
    ends = jnp.stack([jnp.sum(own_docs[:, : j + 1], axis=1) for j in range(own_docs.shape[1])], axis=1)
    mask = lax.dynamic_slice_in_dim(pad_mask, s * T, T, axis=0).astype(f32)
    mask = jnp.broadcast_to(mask[None], (8, T))
    weights = lax.all_gather(lax.all_gather(w, "dp", axis=0, tiled=True), "section")
    wd_full = lax.all_gather(wd, ("section", "dp"), axis=0, tiled=True)
    both = lax.all_gather(stream, "section")
    x, g = lax.dynamic_slice_in_dim(both, s * T, T, axis=2)
    gains = lax.all_gather(gain, "section")
    qkv, att, lse, h0, x1, h1 = run_attn_fwd(ends, x, gains[0], gains[1], mask, weights[0])
    out1, dy, gw1, gwd, gg1 = run_ffn(g, gains[1], mask, x1, h1, weights[1], wd_full)
    out0, gw0, gg0 = run_attn_bwd(ends, x, gains[0], mask, weights[0], qkv, att, lse, h0, dy)
    gw = jnp.stack([gw0, gw1])
    gg = jnp.stack([gg0, gg1])
    first = lax.psum_scatter(gw.astype(f32), "section", scatter_dimension=0)
    first = lax.psum_scatter(first, "dp", scatter_dimension=0, tiled=True)
    down = lax.psum_scatter(gwd.astype(f32), ("section", "dp"), scatter_dimension=0, tiled=True)
    outs = lax.all_gather(jnp.stack([out0, out1]), "section")
    out = jnp.concatenate([lax.dynamic_index_in_dim(outs[i], s, 0, False) for i in range(2)], axis=1)
    gain_total = lax.psum_scatter(lax.psum(jnp.sum(gg, axis=2), "dp"), "section", scatter_dimension=0)
    return out[: D - 1][:, None], first, down, gain_total[None]


def shards(sizes, stream_pair, norm_gains, first_proj, down_proj, doc_lengths, pad_mask):
    own = lax.axis_index("section"), lax.axis_index("dp")
    sections, groups = sizes
    stream = jnp.transpose(stream_pair, (2, 0, 1))
    w = jnp.transpose(first_proj[0])
    wd = jnp.transpose(down_proj)
    if sizes == (2, 16) and stream.shape[2] == 4 * SLOTS:
        out, first, down, gain_total = layer(doc_lengths, pad_mask[None], norm_gains, stream, w, wd)
    else:
        out, first, down, gain_total = separate(
            own, stream, w, wd, norm_gains, doc_lengths, pad_mask, sections, groups
        )
    share = D // groups
    gain_share = lax.dynamic_slice_in_dim(gain_total, own[1] * share, share, axis=1)
    return jnp.transpose(out, (1, 2, 0)), gain_share, jnp.transpose(first)[None], jnp.transpose(down)


def solution(mesh):
    placed = (
        P("section", "dp", None),
        P("section", None),
        P("section", None, "dp"),
        P(None, ("section", "dp")),
        P("dp", None),
        P("dp"),
    )
    return jax.shard_map(
        functools.partial(shards, (mesh.shape["section"], mesh.shape["dp"])),
        mesh=mesh,
        in_specs=placed,
        out_specs=(
            P("section", "dp", None),
            P("section", "dp"),
            P("section", None, "dp"),
            P(None, ("section", "dp")),
        ),
        check_vma=False,
    )
```

```python
import functools
import jax, jax.numpy as jnp
from jax import lax
from jax.experimental import pallas as pl
from jax.experimental.pallas import tpu as pltpu
from jax.sharding import PartitionSpec as P

HEADS, HEAD_DIM, FF, D, SLOTS = 12, 64, 3072, 768, 512
LONGEST = 256
EPS, MASKED = 1e-05, -1e30
VMEM_MOST = 63 * 2**20
f32, bf16 = jnp.float32, jnp.bfloat16
CHUNK = 768

def nn(a, b):
    return lax.dot_general(a, b, (((1,), (0,)), ((), ())), preferred_element_type=f32)
def nt(a, b):
    return lax.dot_general(a, b, (((1,), (1,)), ((), ())), preferred_element_type=f32)
def tn(a, b):
    return lax.dot_general(a, b, (((0,), (0,)), ((), ())), preferred_element_type=f32)

def last_row(shape):
    return lax.broadcasted_iota(jnp.int32, shape, 0) == shape[0] - 1

def expanded(x):
    return jnp.where(last_row(x.shape), -jnp.sum(x, axis=0, keepdims=True), x)

def inv_rms(x):
    return lax.rsqrt(jnp.mean(x * x, axis=0, keepdims=True) + EPS)

def bias_block(ends, live, first_key, keys, first_query, queries):
    shape = (keys, queries)
    kp = lax.broadcasted_iota(jnp.int32, shape, 0) + first_key
    qp = lax.broadcasted_iota(jnp.int32, shape, 1) + first_query
    kd = sum((kp >= e).astype(jnp.int32) for e in ends)
    qd = sum((qp >= e).astype(jnp.int32) for e in ends)
    seen = (kd == qd) & (kp <= qp) & ((live > 0.5) | (kp == qp))
    return jnp.where(seen, 0.0, MASKED)

def attn_fwd(ends_ref, x_ref, g0_ref, g1_ref, mask_ref, w_ref,
             qkv_ref, att_ref, lse_ref, h0_ref, x1_ref, h1_ref, bias_ref):
    T = x_ref.shape[1]
    nb = T // SLOTS
    @pl.loop(0, T // 256)
    def _(t):
        c = pl.ds(pl.multiple_of(t * 256, 256), 256)
        x = expanded(x_ref[:, c])
        h0_ref[:, c] = (x * inv_rms(x) * g0_ref[:, :1]).astype(bf16)
    for b in range(nb):
        ends = [ends_ref[b, j] for j in range(3)]
        marks = jnp.broadcast_to(mask_ref[:1, b * SLOTS:(b + 1) * SLOTS], (128, SLOTS)).T
        for qb in range(2):
            nk = 256 * (qb + 1)
            for q0 in (0, 128):
                bias_ref[b, :nk, qb * 256 + q0: qb * 256 + q0 + 128] = bias_block(ends, marks[:nk], 0, nk, qb * 256 + q0, 128)
    @pl.loop(0, 9)
    def _(m):
        r = pl.ds(pl.multiple_of(m * 256, 256), 256)
        qkv_ref[r, :] = nn(w_ref[r, :], h0_ref[...]).astype(bf16)
    for b in range(nb):
        cols = slice(b * SLOTS, (b + 1) * SLOTS)
        @pl.loop(0, HEADS // 2)
        def _(hp):
            for hh in range(2):
                h = hp * 2 + hh
                off = pl.multiple_of(h * HEAD_DIM, HEAD_DIM)
                q = qkv_ref[pl.ds(off, HEAD_DIM), cols] * bf16(HEAD_DIM ** -0.5)
                k = qkv_ref[pl.ds(off + D, HEAD_DIM), cols].T
                v = qkv_ref[pl.ds(off + 2 * D, HEAD_DIM), cols]
                for qb in range(2):
                    nk, lo = 256 * (qb + 1), qb * 256
                    s = nn(k[:nk], q[:, lo:lo + 256]) + bias_ref[b, :nk, lo:lo + 256]
                    mx = jnp.max(s, axis=0, keepdims=True)
                    p = jnp.exp(s - mx)
                    tot = jnp.sum(p, axis=0, keepdims=True)
                    lse_ref[pl.ds(h, 1), b * SLOTS + lo: b * SLOTS + lo + 256] = mx + jnp.log(tot)
                    low = (p * (1.0 / tot)).astype(bf16)
                    att_ref[pl.ds(off, HEAD_DIM), b * SLOTS + lo: b * SLOTS + lo + 256] = nn(v[:, :nk], low).astype(bf16)
    @pl.loop(0, T // 256)
    def _(t):
        c = pl.ds(pl.multiple_of(t * 256, 256), 256)
        x = expanded(x_ref[:, c])
        a = nn(w_ref[3 * D:, :], att_ref[:, c])
        x1 = expanded(jnp.where(last_row(x.shape), 0.0, x + (a - jnp.mean(a, axis=0, keepdims=True))))
        x1_ref[:, c] = x1
        h1_ref[:, c] = (x1 * inv_rms(x1) * g1_ref[:, :1]).astype(bf16)

C0 = 0.7978845608028654
def gelu_both(u):
    u2 = u * u
    inner = C0 * u * (1.0 + 0.044715 * u2)
    t = jnp.tanh(inner)
    half = 0.5 * (1.0 + t)
    slope = half + 0.5 * u * (1.0 - t * t) * (C0 * (1.0 + 3 * 0.044715 * u2))
    return u * half, slope

def norm_back(x, r, gain, dh):
    e = gain * dh
    dx = r * e - x * (r * r * r) * jnp.mean(x * e, axis=0, keepdims=True)
    return dx, dh * x * r

def lane_fold(v):
    return sum(v[:, i * 128:(i + 1) * 128] for i in range(v.shape[1] // 128))

def ffn(g_ref, g1_ref, mask_ref, x1_ref, h1_ref, w1_ref, wd_ref,
        out1_ref, dy_ref, gw1_ref, gwd_ref, gg_ref, dm_ref, z_ref, du_ref, u_ref, macc, hacc):
    T = g_ref.shape[1]
    nt_ = T // 256
    @pl.loop(0, nt_)
    def _(t):
        c = pl.ds(pl.multiple_of(t * 256, 256), 256)
        g = g_ref[:, c] * mask_ref[:1, c]
        dm_ref[:, c] = (g - jnp.mean(g, axis=0, keepdims=True)).astype(bf16)
    macc[...] = jnp.zeros_like(macc)
    hacc[...] = jnp.zeros_like(hacc)
    @pl.loop(0, FF // CHUNK)
    def _(p):
        base = p * CHUNK
        @pl.loop(0, CHUNK // 256)
        def _(m):
            r = pl.ds(pl.multiple_of(base + m * 256, 256), 256)
            rl = pl.ds(pl.multiple_of(m * 256, 256), 256)
            for n in range(T // 512):
                cs = slice(n * 512, (n + 1) * 512)
                z, slope = gelu_both(nn(w1_ref[r, :], h1_ref[:, cs]))
                z_ref[rl, cs] = z.astype(bf16)
                du_ref[rl, cs] = (nn(wd_ref[r, :], dm_ref[:, cs]) * slope).astype(bf16)
        rows = pl.ds(pl.multiple_of(base, CHUNK), CHUNK)
        @pl.loop(0, 3)
        def _(m):
            o = pl.ds(pl.multiple_of(m * 256, 256), 256)
            macc[o, :] += tn(wd_ref[rows, o], z_ref[...])
            hacc[o, :] += tn(w1_ref[rows, o], du_ref[...])
            r = pl.ds(pl.multiple_of(base + m * 256, 256), 256)
            gw1_ref[r, :] = nt(du_ref[o, :], h1_ref[...]).astype(gw1_ref.dtype)
            gwd_ref[r, :] = nt(z_ref[o, :], dm_ref[...]).astype(gwd_ref.dtype)
    gg_ref[...] = jnp.zeros_like(gg_ref)
    @pl.loop(0, nt_)
    def _(t):
        c = pl.ds(pl.multiple_of(t * 256, 256), 256)
        x1, m = x1_ref[:, c], macc[:, c]
        out1_ref[:, c] = x1 + (m - jnp.mean(m, axis=0, keepdims=True))
        g = g_ref[:, c] * mask_ref[:1, c]
        dx, gg = norm_back(x1, inv_rms(x1), g1_ref[:, :1], hacc[:, c])
        gg_ref[...] += lane_fold(gg)
        dy_ref[:, c] = g + dx - dx[D - 1:, :]

def attn_bwd(ends_ref, x_ref, g0_ref, mask_ref, w_ref, qkv_ref, att_ref, lse_ref, h0_ref, dy_ref,
             out0_ref, gw_ref, gg_ref, da_ref, dat_ref, dqkv_ref, bias_ref):
    T = x_ref.shape[1]
    nb = T // SLOTS
    for b in range(nb):
        ends = [ends_ref[b, j] for j in range(3)]
        marks = jnp.broadcast_to(mask_ref[:1, b * SLOTS:(b + 1) * SLOTS], (128, SLOTS)).T
        for qb in range(2):
            nk = 256 * (qb + 1)
            for q0 in (0, 128):
                bias_ref[b, :nk, qb * 256 + q0: qb * 256 + q0 + 128] = bias_block(ends, marks[:nk], 0, nk, qb * 256 + q0, 128)
    @pl.loop(0, T // 256)
    def _(t):
        c = pl.ds(pl.multiple_of(t * 256, 256), 256)
        dy = dy_ref[:, c]
        da_ref[:, c] = (dy - jnp.mean(dy, axis=0, keepdims=True)).astype(bf16)
    @pl.loop(0, 3)
    def _(m):
        o = pl.ds(pl.multiple_of(m * 256, 256), 256)
        r = pl.ds(pl.multiple_of(3 * D + m * 256, 256), 256)
        gw_ref[r, :] = nt(da_ref[o, :], att_ref[...]).astype(gw_ref.dtype)
        dat_ref[o, :] = tn(w_ref[3 * D:, o], da_ref[...]).astype(bf16)
    for b in range(nb):
        cols = slice(b * SLOTS, (b + 1) * SLOTS)
        @pl.loop(0, HEADS)
        def _(h):
            off = pl.multiple_of(h * HEAD_DIM, HEAD_DIM)
            q = qkv_ref[pl.ds(off, HEAD_DIM), cols] * bf16(HEAD_DIM ** -0.5)
            kt = qkv_ref[pl.ds(off + D, HEAD_DIM), cols]
            k = kt.T
            v = qkv_ref[pl.ds(off + 2 * D, HEAD_DIM), cols].T
            d = dat_ref[pl.ds(off, HEAD_DIM), cols]
            dks, dvs = [], []
            for qb in range(2):
                nk, lo = 256 * (qb + 1), qb * 256
                s = nn(k[:nk], q[:, lo:lo + 256]) + bias_ref[b, :nk, lo:lo + 256]
                p = jnp.exp(s - lse_ref[pl.ds(h, 1), b * SLOTS + lo: b * SLOTS + lo + 256])
                dp = nn(v[:nk], d[:, lo:lo + 256])
                ds = (p * (dp - jnp.sum(p * dp, axis=0, keepdims=True))).astype(bf16)
                low = p.astype(bf16)
                dqkv_ref[pl.ds(off, HEAD_DIM), b * SLOTS + lo: b * SLOTS + lo + 256] = (nn(kt[:, :nk], ds) * HEAD_DIM ** -0.5).astype(bf16)
                dks.append(nt(q[:, lo:lo + 256], ds))
                dvs.append(nt(d[:, lo:lo + 256], low))
            for at, parts in ((D, dks), (2 * D, dvs)):
                dqkv_ref[pl.ds(off + at, HEAD_DIM), b * SLOTS: b * SLOTS + 256] = (parts[0] + parts[1][:, :256]).astype(bf16)
                dqkv_ref[pl.ds(off + at, HEAD_DIM), b * SLOTS + 256: (b + 1) * SLOTS] = parts[1][:, 256:].astype(bf16)
    @pl.loop(0, 9)
    def _(m):
        r = pl.ds(pl.multiple_of(m * 256, 256), 256)
        gw_ref[r, :] = nt(dqkv_ref[r, :], h0_ref[...]).astype(gw_ref.dtype)
    gg_ref[...] = jnp.zeros_like(gg_ref)
    @pl.loop(0, T // 256)
    def _(t):
        c = pl.ds(pl.multiple_of(t * 256, 256), 256)
        x = expanded(x_ref[:, c])
        dh = tn(w_ref[:3 * D, :], dqkv_ref[:, c])
        dx, gg = norm_back(x, inv_rms(x), g0_ref[:, :1], dh)
        gg_ref[...] += lane_fold(gg)
        out0_ref[:, c] = dy_ref[:, c] + dx - dx[D - 1:, :]

V = pl.BlockSpec(memory_space=pltpu.VMEM)
S = pl.BlockSpec(memory_space=pltpu.SMEM)
def sds(*shape, dtype=f32):
    return jax.ShapeDtypeStruct(shape, dtype)
PARAMS = pltpu.CompilerParams(vmem_limit_bytes=60 * 2**20)

def run_attn_fwd(ends, x, g0, g1, mask, w):
    T = x.shape[1]
    return pl.pallas_call(attn_fwd, in_specs=[S] + [V] * 5, out_specs=[V] * 6,
        out_shape=[sds(3 * D, T, dtype=bf16), sds(D, T, dtype=bf16), sds(16, T), sds(D, T, dtype=bf16), sds(D, T), sds(D, T, dtype=bf16)],
        scratch_shapes=[pltpu.VMEM((T // SLOTS, SLOTS, SLOTS), f32)], compiler_params=PARAMS, name="attn_fwd")(ends, x, g0, g1, mask, w)

def run_ffn(g, g1, mask, x1, h1, w1, wd, gdt=bf16):
    T = g.shape[1]
    return pl.pallas_call(ffn, in_specs=[V] * 7, out_specs=[V] * 5,
        out_shape=[sds(D, T), sds(D, T), sds(FF, D, dtype=gdt), sds(FF, D, dtype=gdt), sds(D, 128)],
        scratch_shapes=[pltpu.VMEM((D, T), bf16), pltpu.VMEM((CHUNK, T), bf16), pltpu.VMEM((CHUNK, T), bf16), pltpu.VMEM((8, 128), f32), pltpu.VMEM((D, T), f32), pltpu.VMEM((D, T), f32)],
        compiler_params=PARAMS, name="ffn")(g, g1, mask, x1, h1, w1, wd)

def run_attn_bwd(ends, x, g0, mask, w, qkv, att, lse, h0, dy, gdt=bf16):
    T = x.shape[1]
    return pl.pallas_call(attn_bwd, in_specs=[S] + [V] * 9, out_specs=[V] * 3,
        out_shape=[sds(D, T), sds(FF, D, dtype=gdt), sds(D, 128)],
        scratch_shapes=[pltpu.VMEM((D, T), bf16), pltpu.VMEM((D, T), bf16), pltpu.VMEM((3 * D, T), bf16), pltpu.VMEM((T // SLOTS, SLOTS, SLOTS), f32)],
        compiler_params=PARAMS, name="attn_bwd")(ends, x, g0, mask, w, qkv, att, lse, h0, dy)


MESH = pl.DeviceIdType.MESH
HBM = pl.BlockSpec(memory_space=pl.ANY)


def push(src, dst, send, recv, device):
    copy = pltpu.make_async_remote_copy(
        src_ref=src, dst_ref=dst, send_sem=send, recv_sem=recv, device_id=device, device_id_type=MESH
    )
    copy.start()
    return copy


DIST = (0, 1, 3, 2)
CHUNKS = (0, 2, 1, 3)
TILE = 256
SCALE = HEAD_DIM ** -0.5
KIND_A, KIND_D, KIND_W = 0, 1, 2
SETS = 12
PLANES = (3, 0, 1, 2)


def wide(v):
    return v.astype(f32)


def square(v):
    return v.reshape(-1, D)


def at_step(k):
    return lax.rem(2 * k, 3) + 3 * (k // 3)


def layer_kernel(
    len_ref, mask_ref, gain_ref, stream, w_ref, wd_ref,
    out, first, down, gain_out, spill_x, spill_q,
    fa, fw, fd, X, G, xt, gt, QKV, ATT, H0, H1, DM, MACC, HACC, BIAS, LSE, MK, GR, GCOL, GG, GV, GL, GT,
    STG, STGD, ACC, L1, L2, L3W, L3A, L3D,
    zs, zr, ps, pr, ss, sr, p1s, p1r, p2s, p2r, p3s, rw, ra, rd, i_s, i_r, local, gs, gr, gss, gsr,
):
    s, d = lax.axis_index("section"), lax.axis_index("dp")
    x, y, z, xy = lax.rem(d, 2), lax.rem(d // 2, 2), d // 4, lax.rem(d, 4)
    t = 1 - s
    over_y, over_x = (1 - y) * 2 + x, y * 2 + 1 - x
    xy1, xy2, xy3 = t * over_y + s * over_x, s * over_y + t * over_x, 3 - xy
    sib, n1, n2 = (t, d), (s, z * 4 + xy1), (s, z * 4 + xy2)
    T = X.shape[1]
    nb = T // SLOTS
    tiles = T // TILE
    col = lambda i: pl.ds(pl.multiple_of(i * TILE, TILE), TILE)
    at_plane = lambda p: (s, p * 4 + xy)

    def plane(i, kind=KIND_W):
        if kind == KIND_D:
            return 2 * lax.rem(z + i // 2, 2) + i % 2
        return lax.rem(z + 4 - (DIST if kind == KIND_A else CHUNKS)[i], 4)

    def wait_recv(dst, sem):
        pltpu.make_async_remote_copy(
            src_ref=dst, dst_ref=dst, send_sem=sem, recv_sem=sem, device_id=sib, device_id_type=MESH
        ).wait_recv()

    def wait_send(src, sem):
        pltpu.make_async_remote_copy(
            src_ref=src, dst_ref=src, send_sem=sem, recv_sem=sem, device_id=sib, device_id_type=MESH
        ).wait_send()

    def move(src, dst, sem):
        pltpu.make_async_copy(src, dst, sem).start()

    def moved(src, dst, sem):
        pltpu.make_async_copy(src, dst, sem).wait()

    def slab(kind, zz, q, h):
        return fd.at[:, zz, q, h] if kind == KIND_D else (fa, None, fw)[kind].at[zz, q, h]

    def group(kind, zz, h):
        return fd.at[:, zz, :, h] if kind == KIND_D else (fa, None, fw)[kind].at[zz, :, h]

    def Z(kind, far):
        own = slab(kind, z, xy, s)
        push(own, own, zs.at[kind, far], zr.at[kind, far], at_plane(lax.rem(z + far, 4)))

    def A(kind, i):
        zz = plane(i, kind)
        here = slab(kind, zz, xy, s)
        if kind == KIND_D:
            @pl.when(zz != z)
            def _():
                wait_recv(here, zr.at[kind, lax.rem(z + 4 - zz, 4)])
        elif i:
            wait_recv(here, zr.at[kind, (DIST if kind == KIND_A else CHUNKS)[i]])
        if kind == KIND_A and i in (1, 2):
            Z(kind, DIST[i + 1])
        elif kind == KIND_A and i == 3:
            for far in (1, 2, 3):
                Z(KIND_D, far)
        elif kind == KIND_D and i == 1:
            Z(KIND_W, 2)
        elif kind == KIND_W and i == 1:
            Z(KIND_W, 1)
            Z(KIND_W, 3)
        push(here, here, ps.at[kind, i, 0], pr.at[kind, i, 0], n1)
        push(here, here, ps.at[kind, i, 1], pr.at[kind, i, 1], n2)

    def B(kind, i):
        here = slab(kind, plane(i, kind), xy1, s)
        wait_recv(here, pr.at[kind, i, 0])
        push(here, here, ps.at[kind, i, 2], pr.at[kind, i, 2], n2)

    def C(kind, i):
        zz = plane(i, kind)
        wait_recv(slab(kind, zz, xy2, s), pr.at[kind, i, 1])
        wait_recv(slab(kind, zz, xy3, s), pr.at[kind, i, 2])
        here = group(kind, zz, s)
        push(here, here, ps.at[kind, i, 3], pr.at[kind, i, 3], sib)

    def E(kind, i):
        wait_recv(group(kind, plane(i, kind), t), pr.at[kind, i, 3])

    def sent(kind):
        for i in range(4):
            zz = plane(i, kind)
            if i:
                wait_send(slab(kind, z, xy, s), zs.at[kind, i])
            wait_send(slab(kind, zz, xy, s), ps.at[kind, i, 0])
            wait_send(slab(kind, zz, xy, s), ps.at[kind, i, 1])
            wait_send(slab(kind, zz, xy1, s), ps.at[kind, i, 2])
            wait_send(group(kind, zz, s), ps.at[kind, i, 3])

    def to_sibling(j, slot, down_set=False):
        if down_set:
            for sub in range(2):
                push(STGD.at[sub, :, t], ACC.at[j, :, sub], ss.at[j, sub], sr.at[j, sub], sib)
        else:
            push(STG.at[slot, :, t], ACC.at[j], ss.at[j, 0], sr.at[j, 0], sib)

    def staged_free(j, down_set=False):
        if down_set:
            for sub in range(2):
                wait_send(STGD.at[sub, :, t], ss.at[j, sub])
        else:
            wait_send(STG.at[0, :, t], ss.at[j, 0])

    def slot_of(j):
        return j // 2 % 2 if j < 8 else j % 2

    def R1(j):
        if j < 8 and j % 2:
            for sub in range(2):
                wait_recv(ACC.at[j, :, sub], sr.at[j, sub])
                for q in range(4):
                    ACC[j, q, sub] = (wide(ACC[j, q, sub]) + wide(STGD[sub, q, s])).astype(bf16)
        else:
            wait_recv(ACC.at[j], sr.at[j, 0])
            for q in range(4):
                ACC[j, q] = (wide(ACC[j, q]) + wide(STG[slot_of(j), q, s])).astype(bf16)
        push(ACC.at[j, xy2], L1.at[j, 0], p1s.at[j, 0], p1r.at[j, 0], n2)
        push(ACC.at[j, xy3], L1.at[j, 1], p1s.at[j, 1], p1r.at[j, 1], n2)

    def R2(j):
        wait_recv(L1.at[j, 0], p1r.at[j, 0])
        wait_recv(L1.at[j, 1], p1r.at[j, 1])
        ACC[j, xy] = (wide(ACC[j, xy]) + wide(L1[j, 0])).astype(bf16)
        ACC[j, xy1] = (wide(ACC[j, xy1]) + wide(L1[j, 1])).astype(bf16)
        push(ACC.at[j, xy1], L2.at[j], p2s.at[j], p2r.at[j], n1)

    def ends_of(j):
        if j >= 8:
            p = PLANES[j - 8]
            return [(z != p, ACC.at[j, xy], L3A.at[z], p3s.at[j, 0], ra.at[z], p)]
        k = j // 2
        p = plane(k)
        if j % 2 == 0:
            return [(None, ACC.at[j, xy], L3W.at[k - 1], p3s.at[j, 0], rw.at[k - 1], p)] if k else []
        made = []
        for sub in range(2):
            to = 2 * lax.rem(p, 2) + sub
            made.append((z != to, ACC.at[j, xy, sub], L3D.at[p // 2, z], p3s.at[j, sub], rd.at[p // 2, z], to))
        return made

    def guarded(cond, act):
        act() if cond is None else pl.when(cond)(act)

    def R3(j):
        wait_recv(L2.at[j], p2r.at[j])
        ACC[j, xy] = (wide(ACC[j, xy]) + wide(L2[j])).astype(bf16)
        for cond, src, dst, ssem, rsem, to in ends_of(j):
            guarded(cond, lambda src=src, dst=dst, ssem=ssem, rsem=rsem, to=to: push(src, dst, ssem, rsem, at_plane(to)) and None)

    def scattered(j):
        wait_send(ACC.at[j, xy2], p1s.at[j, 0])
        wait_send(ACC.at[j, xy3], p1s.at[j, 1])
        wait_send(ACC.at[j, xy1], p2s.at[j])
        for cond, src, dst, ssem, rsem, to in ends_of(j):
            guarded(cond, lambda src=src, ssem=ssem: wait_send(src, ssem))

    QKV_SETS = pl.ds(9, 3)

    def G1(n):
        q = (lax.rem(y + 1 - n % 2, 2)) * 2 + lax.rem(x + 1 - n // 2, 2)
        slot = (n + 1) % 2
        wait_recv(ACC.at[QKV_SETS, q], gsr.at[n])
        for part in range(3):
            ACC[9 + part, q] = (wide(ACC[9 + part, q]) + wide(STG[slot, part, s])).astype(bf16)
        if n == 0:
            push(ACC.at[QKV_SETS, xy3], L1.at[QKV_SETS, 1], p1s.at[9, 1], p1r.at[9, 1], n2)
        elif n < 3:
            @pl.when(s == n - 1)
            def _():
                push(ACC.at[QKV_SETS, xy2], L1.at[QKV_SETS, 0], p1s.at[9, 0], p1r.at[9, 0], n2)

    def G2():
        wait_recv(L1.at[QKV_SETS, 1], p1r.at[9, 1])
        for j in range(9, 12):
            ACC[j, xy1] = (wide(ACC[j, xy1]) + wide(L1[j, 1])).astype(bf16)
        push(ACC.at[QKV_SETS, xy1], L2.at[QKV_SETS], p2s.at[9], p2r.at[9], n1)

    def G3():
        wait_recv(L1.at[QKV_SETS, 0], p1r.at[9, 0])
        wait_recv(L2.at[QKV_SETS], p2r.at[9])
        for j in range(9, 12):
            ACC[j, xy] = (wide(ACC[j, xy]) + wide(L1[j, 0]) + wide(L2[j])).astype(bf16)
            for cond, src, dst, ssem, rsem, to in ends_of(j):
                guarded(cond, lambda src=src, dst=dst, ssem=ssem, rsem=rsem, to=to: push(src, dst, ssem, rsem, at_plane(to)) and None)

    def G_sent():
        wait_send(ACC.at[QKV_SETS, xy3], p1s.at[9, 1])
        wait_send(ACC.at[QKV_SETS, xy2], p1s.at[9, 0])
        wait_send(ACC.at[QKV_SETS, xy1], p2s.at[9])
        for j in range(9, 12):
            for cond, src, dst, ssem, rsem, to in ends_of(j):
                guarded(cond, lambda src=src, ssem=ssem: wait_send(src, ssem))

    barrier = pltpu.get_barrier_semaphore()
    partners = [sib, n1, n2, *(at_plane(lax.rem(z + r, 4)) for r in (1, 2, 3))]
    for device in partners:
        pl.semaphore_signal(barrier, inc=1, device_id=device, device_id_type=MESH)
    pl.semaphore_wait(barrier, len(partners))

    mine, other = pl.ds(pl.multiple_of(s * T, T), T), pl.ds(pl.multiple_of(t * T, T), T)
    top = pl.ds(0, D - 8)

    def rows_of(part):
        return stream.at[top, 0, part], stream.at[pl.ds(D - 9, 8), 0, part]

    @pl.when(s == 0)
    def _():
        push(w_ref.at[1], fa.at[z, xy, 1], i_s.at[0], i_r.at[0], sib)
        move(w_ref.at[0], fa.at[z, xy, 0], local.at[0])

    @pl.when(s == 1)
    def _():
        push(w_ref.at[0], fw.at[z, xy, 0], i_s.at[0], i_r.at[0], sib)
        move(w_ref.at[1], fw.at[z, xy, 1], local.at[0])

    push(wd_ref.at[t], fd.at[s, z, xy, t], i_s.at[1], i_r.at[1], sib)
    move(wd_ref.at[s], fd.at[s, z, xy, s], local.at[1])
    push(gain_ref, GR.at[s], i_s.at[2], i_r.at[2], sib)
    move(gain_ref, GR.at[s], local.at[2])

    def stream_in(keep, tail):
        def go():
            a, b = rows_of(mine)
            move(a, keep.at[top], local.at[3])
            move(b, tail, local.at[4])
        return go

    def stream_out(give, tail):
        def go():
            a, b = rows_of(other)
            push(a, give.at[top], i_s.at[3], i_r.at[3], sib)
            push(b, tail, i_s.at[4], i_r.at[4], sib)
        return go

    pl.when(s == 0)(stream_in(X, xt))
    pl.when(s == 1)(stream_in(G, gt))

    @pl.when(s == 0)
    def _():
        moved(w_ref.at[0], fa.at[z, xy, 0], local.at[0])
        wait_send(w_ref.at[1], i_s.at[0])

    @pl.when(s == 1)
    def _():
        wait_recv(fa.at[z, xy, 1], i_r.at[0])

    Z(KIND_A, DIST[1])
    A(KIND_A, 0)
    pl.when(s == 0)(stream_out(X, xt))
    pl.when(s == 1)(stream_out(G, gt))

    def lengths(b):
        return [len_ref[s * nb + b, j] for j in range(4)]

    shifts, ends = [], []
    for b in range(nb):
        size = lengths(b)
        stops = [size[0], size[0] + size[1], size[0] + size[1] + size[2]]
        starts = [0, *stops]
        shifts.append(sum(jnp.where(size[j] == LONGEST, starts[j], 0) for j in range(1, 4)))
        ends.append(stops)

    moved(gain_ref, GR.at[s], local.at[2])
    wait_recv(GR.at[t], i_r.at[2])
    for j in range(2):
        GCOL[j] = jnp.broadcast_to(GR[j], (128, D)).T

    def turn(ref, tail, b):
        cols = slice(b * SLOTS, (b + 1) * SLOTS)
        amount = lax.rem(SLOTS - shifts[b], SLOTS)
        ref[D - 8:, cols] = jnp.concatenate([tail[1:, cols], jnp.zeros((1, SLOTS), f32)], axis=0)

        @pl.loop(0, 8)
        def _(i):
            r = pl.ds(pl.multiple_of(i * 96, 96), 96)
            ref[r, cols] = pltpu.roll(ref[r, cols], amount, 1)

    def x_arrived():
        @pl.when(s == 0)
        def _():
            a, b = rows_of(mine)
            moved(a, X.at[top], local.at[3])
            moved(b, xt, local.at[4])

        @pl.when(s == 1)
        def _():
            wait_recv(X.at[top], i_r.at[3])
            wait_recv(xt, i_r.at[4])

    def g_arrived():
        @pl.when(s == 1)
        def _():
            a, b = rows_of(mine)
            moved(a, G.at[top], local.at[3])
            moved(b, gt, local.at[4])

        @pl.when(s == 0)
        def _():
            wait_recv(G.at[top], i_r.at[3])
            wait_recv(gt, i_r.at[4])

    def masks():
        for b in range(nb):
            cols = slice(b * SLOTS, (b + 1) * SLOTS)
            amount = lax.rem(SLOTS - shifts[b], SLOTS)
            live = wide(mask_ref[:, pl.ds(pl.multiple_of(s * T + b * SLOTS, SLOTS), SLOTS)])
            MK[:, cols] = pltpu.roll(jnp.broadcast_to(live, (8, SLOTS)), amount, 1)
            marks = jnp.broadcast_to(MK[:1, cols], (128, SLOTS)).T
            for qb in range(2):
                for half in range(2):
                    shape = (TILE, 128)
                    kp = lax.broadcasted_iota(jnp.int32, shape, 0) + qb * TILE
                    qp = lax.broadcasted_iota(jnp.int32, shape, 1) + qb * TILE + half * 128

                    def doc(p):
                        first_place = p + shifts[b]
                        first_place = first_place - jnp.where(first_place >= SLOTS, SLOTS, 0)
                        return sum((first_place >= e).astype(jnp.int32) for e in ends[b])

                    seen = (doc(kp) == doc(qp)) & (kp <= qp)
                    seen = seen & ((marks[qb * TILE:(qb + 1) * TILE] > 0.5) | (kp == qp))
                    BIAS[b, qb, :, half * 128:(half + 1) * 128] = jnp.where(seen, 0.0, MASKED)

    def normed_in():
        @pl.loop(0, tiles)
        def _(i):
            c = col(i)
            v = expanded(X[:, c])
            X[D - 8:, c] = v[D - 8:]
            H0[:, c] = (v * inv_rms(v) * GCOL[0, :, :1]).astype(bf16)

    def cotangent():
        @pl.loop(0, tiles)
        def _(i):
            c = col(i)
            v = G[:, c] * MK[:1, c]
            G[:, c] = v
            DM[:, c] = (v - jnp.mean(v, axis=0, keepdims=True)).astype(bf16)

    masks()
    A(KIND_A, 1)
    B(KIND_A, 0)
    x_arrived()
    turn(X, xt, 0)
    A(KIND_A, 2)
    B(KIND_A, 1)
    turn(X, xt, 1)
    C(KIND_A, 0)
    normed_in()
    move(X, spill_x, local.at[5])

    @pl.when(s == 0)
    def _():
        wait_recv(fw.at[z, xy, 0], i_r.at[0])

    @pl.when(s == 1)
    def _():
        moved(w_ref.at[1], fw.at[z, xy, 1], local.at[0])
        wait_send(w_ref.at[0], i_s.at[0])

    moved(wd_ref.at[s], fd.at[s, z, xy, s], local.at[1])
    wait_recv(fd.at[t, z, xy, s], i_r.at[1])
    A(KIND_A, 3)
    B(KIND_A, 2)
    g_arrived()
    turn(G, gt, 0)
    C(KIND_A, 1)
    A(KIND_D, 0)
    B(KIND_A, 3)
    turn(G, gt, 1)
    C(KIND_A, 2)
    cotangent()
    C(KIND_A, 3)
    for i in range(4):
        E(KIND_A, i)
    A(KIND_D, 1)
    B(KIND_D, 0)

    def ticks(index, table):
        for at, steps in table.items():
            @pl.when(index == at)
            def _(steps=steps):
                for act, *args in steps:
                    act(*args)

    @pl.loop(0, 3)
    def _(p):
        rows = pl.ds(pl.multiple_of(p * D, D), D)
        QKV[rows, :] = nn(square(fa[p]), H0[...]).astype(bf16)
        ticks(p, {1: [(A, KIND_W, 0), (B, KIND_D, 1)], 2: [(C, KIND_D, 0)]})

    units = [(h, qb) for h in range(4) for qb in range(2)]

    def spots(i):
        b = i // 3
        def spot(u):
            head = lax.rem(i, 3) * 4 + u[0]
            return head, pl.multiple_of(head * HEAD_DIM, HEAD_DIM), pl.ds(pl.multiple_of(b * SLOTS + u[1] * TILE, TILE), TILE)
        return b, spot

    def three(off, c):
        return [QKV[pl.ds(off + j * D, HEAD_DIM), c] for j in range(3)]

    @pl.loop(0, 3 * nb)
    def _(i):
        b, spot = spots(i)
        scores, probs = {}, {}
        for u in units:
            head, off, c = spot(u)
            q, k, v = three(off, c)
            scores[u] = nn(k.T, q * bf16(SCALE))
        for u in units:
            head, off, c = spot(u)
            v = scores[u] + BIAS[b, u[1]]
            highest = jnp.max(v, axis=0, keepdims=True)
            p = jnp.exp(v - highest)
            total = jnp.sum(p, axis=0, keepdims=True)
            LSE[pl.ds(head, 1), c] = highest + jnp.log(total)
            probs[u] = (p * (1.0 / total)).astype(bf16)
        for u in units:
            head, off, c = spot(u)
            ATT[pl.ds(off, HEAD_DIM), c] = nn(QKV[pl.ds(off + 2 * D, HEAD_DIM), c], probs[u]).astype(bf16)
        ticks(i, {1: [(A, KIND_W, 1), (B, KIND_W, 0), (C, KIND_D, 1)], 3: [(A, KIND_D, 2), (B, KIND_W, 1)], 5: [(C, KIND_W, 0)]})

    move(QKV, spill_q, local.at[6])
    moved(X, spill_x, local.at[5])

    @pl.loop(0, tiles)
    def _(i):
        c = col(i)
        a = nn(square(fa[3]), ATT[:, c])
        v = X[:, c] + (a - jnp.mean(a, axis=0, keepdims=True))
        v = expanded(jnp.where(last_row(v.shape), 0.0, v))
        X[:, c] = v
        H1[:, c] = (v * inv_rms(v) * GCOL[1, :, :1]).astype(bf16)
        ticks(i, {0: [(A, KIND_D, 3), (B, KIND_D, 2)], 2: [(C, KIND_W, 1)]})

    MACC[...] = jnp.zeros_like(MACC)
    HACC[...] = jnp.zeros_like(HACC)
    moved(QKV, spill_q, local.at[6])
    A(KIND_W, 2)
    B(KIND_D, 3)
    E(KIND_D, 0)
    E(KIND_D, 1)
    E(KIND_W, 0)
    ZT, DU = QKV.at[pl.ds(0, D)], QKV.at[pl.ds(D, D)]

    def stage_rows(slot, left, right, by_plane):
        v = nt(left, right).astype(bf16)
        if by_plane:
            STG[slot] = v.reshape(4, 2, 2, 48, D)
        else:
            STGD[...] = v.reshape(2, 4, 2, 48, D)

    FFN_TICKS = {
        (0, "a"): [(A, KIND_W, 3), (B, KIND_W, 2), (C, KIND_D, 2)],
        (0, "w"): [(C, KIND_D, 3)], (0, "d"): [(B, KIND_W, 3), (C, KIND_W, 2)],
        (0, "t0"): [(R1, 0)], (0, "t1"): [(R1, 1), (E, KIND_W, 1)],
        (1, "a"): [(C, KIND_W, 3)], (1, "t0"): [(R1, 2)],
        (1, "t1"): [(R1, 3), (R2, 0), (E, KIND_D, 2), (E, KIND_D, 3), (E, KIND_W, 2)],
        (2, "a"): [(R2, 1)], (2, "d"): [(R3, 0)], (2, "t0"): [(R1, 4), (R2, 2)],
        (2, "t1"): [(R1, 5), (R3, 1), (E, KIND_W, 3)],
        (3, "a"): [(R2, 3)], (3, "d"): [(R3, 2)], (3, "t0"): [(R1, 6), (R2, 4)], (3, "t1"): [(R1, 7), (R3, 3)],
    }

    @pl.loop(0, 4)
    def _(k):
        p = lax.rem(z + 4 - at_step(k), 4)

        def tick(name):
            ticks(k, {kk: steps for (kk, n), steps in FFN_TICKS.items() if n == name})

        def down_rows():
            return square(fd[p // 2, pl.ds(2 * lax.rem(p, 2), 2)])

        for i in range(tiles):
            c = slice(i * TILE, (i + 1) * TILE)
            act, slope = gelu_both(nn(square(fw[p]), H1[:, c]))
            ZT[:, c] = act.astype(bf16)
            DU[:, c] = (nn(down_rows(), DM[:, c]) * slope).astype(bf16)
        tick("a")

        slot = lax.rem(k, 2)

        @pl.when(k > 1)
        def _():
            staged_free(2 * k - 4)
        stage_rows(slot, DU[...], H1[...], True)
        to_sibling(2 * k, slot)
        tick("w")

        @pl.when(k > 0)
        def _():
            staged_free(2 * k - 1, True)
        stage_rows(0, ZT[...], DM[...], False)
        to_sibling(2 * k + 1, 0, True)
        tick("d")
        MACC[...] += tn(down_rows(), ZT[...])
        tick("t0")
        HACC[...] += tn(square(fw[p]), DU[...])
        tick("t1")

    move(spill_q, QKV, local.at[6])
    GG[...] = jnp.zeros_like(GG)

    @pl.loop(0, tiles)
    def _(i):
        c = col(i)
        v, m = X[:, c], MACC[:, c]
        MACC[:, c] = v + (m - jnp.mean(m, axis=0, keepdims=True))
        dx, part = norm_back(v, inv_rms(v), GCOL[1, :, :1], HACC[:, c])
        GG[...] += lane_fold(part)
        G[:, c] = G[:, c] + dx - dx[D - 1:, :]
        ticks(i, {2: [(R2, 5)]})
    GV[1] = jnp.sum(GG[...].T, axis=0, keepdims=True)

    @pl.when(s == 1)
    def _():
        move(MACC, out.at[:, mine], local.at[7])

    @pl.when(s == 0)
    def _():
        push(MACC, out.at[:, mine], i_s.at[5], i_r.at[5], sib)

    move(spill_x, HACC, local.at[5])

    @pl.loop(0, tiles)
    def _(i):
        c = col(i)
        v = G[:, c]
        DM[:, c] = (v - jnp.mean(v, axis=0, keepdims=True)).astype(bf16)

    staged_free(4)
    staged_free(6)
    staged_free(7, True)
    stage_rows(0, DM[...], ATT[...], True)
    to_sibling(8, 0)
    H1[...] = tn(square(fa[3]), DM[...]).astype(bf16)
    R1(8)
    moved(spill_q, QKV, local.at[6])

    GROUP_TICKS = {
        (0, "0"): [(R3, 4)], (0, "1"): [(R2, 6)], (0, "g"): [(R3, 5)],
        (1, "0"): [(R2, 7), (G1, 0)], (1, "1"): [(R3, 6)], (1, "g"): [(R2, 8)],
        (2, "0"): [(R3, 7), (G1, 1)], (2, "g"): [(R3, 8)],
        (3, "0"): [(G1, 2), (G2,)],
    }

    @pl.loop(0, 4)
    def _(n):
        q = lax.rem(y + 1 - lax.rem(n, 2), 2) * 2 + lax.rem(x + 1 - n // 2, 2)

        def tick(name):
            ticks(n, {nn_: steps for (nn_, name_), steps in GROUP_TICKS.items() if name_ == name})

        for b in range(nb):
            picks = [(h, qb) for h in range(3) for qb in range(2)]
            spot = lambda u: (q * 3 + u[0], pl.multiple_of((q * 3 + u[0]) * HEAD_DIM, HEAD_DIM), slice(b * SLOTS + u[1] * TILE, b * SLOTS + (u[1] + 1) * TILE))
            scores, dprobs, probs, grads = {}, {}, {}, {}
            for u in picks:
                head, off, c = spot(u)
                qq, kk, vv = three(off, c)
                scores[u] = nn(kk.T, qq * bf16(SCALE))
                dprobs[u] = nn(vv.T, H1[pl.ds(off, HEAD_DIM), c])
            for u in picks:
                head, off, c = spot(u)
                p = jnp.exp(scores[u] + BIAS[b, u[1]] - LSE[pl.ds(head, 1), c])
                dp = dprobs[u]
                grads[u] = (p * (dp - jnp.sum(p * dp, axis=0, keepdims=True))).astype(bf16)
                probs[u] = p.astype(bf16)
            for u in picks:
                head, off, c = spot(u)
                qq, kk, _ = three(off, c)
                QKV[pl.ds(off, HEAD_DIM), c] = (nn(kk, grads[u]) * SCALE).astype(bf16)
                QKV[pl.ds(off + D, HEAD_DIM), c] = nt(qq * bf16(SCALE), grads[u]).astype(bf16)
                QKV[pl.ds(off + 2 * D, HEAD_DIM), c] = nt(H1[pl.ds(off, HEAD_DIM), c], probs[u]).astype(bf16)
            tick(str(b))
        slot = lax.rem(n + 1, 2)

        @pl.when(n == 1)
        def _():
            staged_free(8)

        @pl.when(n > 1)
        def _():
            wait_send(STG.at[0, pl.ds(0, 3), t], gss.at[n - 2])
        rows = lambda part: QKV[pl.ds(pl.multiple_of(part * D + q * 192, 64), 192), :]
        v = nt(jnp.concatenate([rows(0), rows(1), rows(2)], axis=0), H0[...]).astype(bf16)
        STG[slot, 0:3] = v.reshape(3, 2, 2, 48, D)
        push(STG.at[slot, pl.ds(0, 3), t], ACC.at[QKV_SETS, q], gss.at[n], gsr.at[n], sib)
        tick("g")

    moved(spill_x, HACC, local.at[5])

    @pl.when(s == 1)
    def _():
        moved(MACC, out.at[:, mine], local.at[7])

    @pl.when(s == 0)
    def _():
        wait_send(MACC, i_s.at[5])

    G1(3)
    MACC[...] = tn(square(fa[:3]), QKV[...])
    G3()
    GG[...] = jnp.zeros_like(GG)

    @pl.loop(0, tiles)
    def _(i):
        c = col(i)
        v = HACC[:, c]
        dx, part = norm_back(v, inv_rms(v), GCOL[0, :, :1], MACC[:, c])
        GG[...] += lane_fold(part)
        G[:, c] = G[:, c] + dx - dx[D - 1:, :]
    GV[0] = jnp.sum(GG[...].T, axis=0, keepdims=True)

    @pl.when(s == 0)
    def _():
        move(G, out.at[:, mine], local.at[8])

    @pl.when(s == 1)
    def _():
        push(G, out.at[:, mine], i_s.at[5], i_r.at[5], sib)

    push(GV.at[t], GL.at[0], gs.at[0], gr.at[0], sib)
    wait_recv(GL.at[0], gr.at[0])
    GT[0] = GV[s] + GL[0]
    push(GT.at[0], GL.at[1], gs.at[1], gr.at[1], n2)
    wait_recv(GL.at[1], gr.at[1])
    GT[1] = GT[0] + GL[1]
    push(GT.at[1], GL.at[2], gs.at[2], gr.at[2], n1)
    wait_recv(GL.at[2], gr.at[2])
    GT[2] = GT[1] + GL[2]
    for r in range(3):
        push(GT.at[2], GL.at[3 + r], gs.at[3 + r], gr.at[3 + r], at_plane(lax.rem(z + 1 + r, 4)))

    def total_of(v, parts):
        v = wide(v)
        for part in parts:
            v = v + wide(part)
        return square(v)

    whole = lambda i: HACC.at[pl.ds(i * 96, 96), pl.ds(0, D)]
    lower = lambda i: HACC.at[pl.ds(pl.multiple_of(192 + 48 * i, 16), 48), pl.ds(0, D)]

    for k in range(3):
        wait_recv(L3W.at[k], rw.at[k])
    whole(1)[...] = total_of(ACC[0, xy], [L3W[k] for k in range(3)])
    for sec in range(2):
        for r in range(3):
            zz = lax.rem(z + 1 + r, 4)
            wait_recv(L3D.at[sec, zz], rd.at[sec, zz])
        far = lax.rem(z + 4 - (2 * sec + z // 2), 4)
        lower(sec)[...] = total_of(ACC[2 * at_step(far) + 1, xy, lax.rem(z, 2)], [L3D[sec, lax.rem(z + 1 + r, 4)] for r in range(3)])
    move(lower(s), down.at[s], local.at[9])
    push(lower(t), down.at[s], i_s.at[6], i_r.at[6], sib)

    @pl.when(s == 1)
    def _():
        move(whole(1), first.at[1], local.at[10])

    @pl.when(s == 0)
    def _():
        push(whole(1), first.at[0], i_s.at[7], i_r.at[7], sib)

    for r in range(3):
        wait_recv(GL.at[3 + r], gr.at[3 + r])
    GT[3] = GT[2] + GL[3] + GL[4] + GL[5]
    gain_out[...] = GT[3]
    for r in range(3):
        zz = lax.rem(z + 1 + r, 4)
        wait_recv(L3A.at[zz], ra.at[zz])
    whole(0)[...] = total_of(ACC[8 + lax.rem(z + 1, 4), xy], [L3A[lax.rem(z + 1 + r, 4)] for r in range(3)])

    @pl.when(s == 0)
    def _():
        move(whole(0), first.at[0], local.at[10])

    @pl.when(s == 1)
    def _():
        push(whole(0), first.at[1], i_s.at[7], i_r.at[7], sib)

    @pl.when(s == 0)
    def _():
        moved(whole(0), first.at[0], local.at[10])
        wait_send(whole(1), i_s.at[7])
        wait_recv(first.at[1], i_r.at[7])
        moved(G, out.at[:, mine], local.at[8])

    @pl.when(s == 1)
    def _():
        moved(whole(1), first.at[1], local.at[10])
        wait_send(whole(0), i_s.at[7])
        wait_recv(first.at[0], i_r.at[7])
        wait_send(G, i_s.at[5])

    wait_recv(out.at[:, other], i_r.at[5])
    moved(lower(s), down.at[s], local.at[9])
    wait_send(lower(t), i_s.at[6])
    wait_recv(down.at[t], i_r.at[6])
    wait_send(wd_ref.at[t], i_s.at[1])
    wait_send(gain_ref, i_s.at[2])
    a, b = rows_of(other)
    wait_send(a, i_s.at[3])
    wait_send(b, i_s.at[4])
    for n in range(6):
        wait_send(GT.at[0], gs.at[n])
    for kind in range(3):
        sent(kind)
    wait_send(STG.at[0, pl.ds(0, 3), t], gss.at[2])
    wait_send(STG.at[0, pl.ds(0, 3), t], gss.at[3])
    for j in range(9):
        scattered(j)
    G_sent()


def finish_kernel(len_ref, pre, out, a, b, ins, outs):
    n = pre.shape[1] // SLOTS
    cols = lambda i: pl.ds(i * SLOTS, SLOTS)
    load = lambda i: pltpu.make_async_copy(pre.at[:, cols(i)], a.at[i % 2], ins.at[i % 2])
    save = lambda i: pltpu.make_async_copy(b.at[i % 2], out.at[:, 0, cols(i)], outs.at[i % 2])
    load(0).start()
    for i in range(n):
        load(i).wait()
        if i + 1 < n:
            load(i + 1).start()
        start, shift = 0, 0
        for j in range(4):
            shift = shift + jnp.where(len_ref[i, j] == LONGEST, start, 0)
            start = start + len_ref[i, j]
        if i >= 2:
            save(i - 2).wait()
        b[i % 2] = pltpu.roll(a[i % 2], shift, 1)[:D - 1]
        save(i).start()
    for i in range(max(n - 2, 0), n):
        save(i).wait()


def layer(lengths, mask, gain, stream, w, wd):
    T = stream.shape[2] // 2
    dma = lambda *shape: pltpu.SemaphoreType.DMA(shape)
    bulk = lambda *shape: pltpu.VMEM(shape, bf16)
    full = lambda *shape: pltpu.VMEM(shape, f32)
    scratch = [
        bulk(4, 4, 2, 96, D), bulk(4, 4, 2, 96, D), bulk(2, 4, 4, 2, 48, D),
        full(D, T), full(D, T), full(8, T), full(8, T),
        bulk(3 * D, T), bulk(D, T), bulk(D, T), bulk(D, T), bulk(D, T),
        full(D, T), full(D, T), full(T // SLOTS, 2, TILE, TILE), full(16, T), full(8, T),
        full(2, 1, D), full(2, D, 128), full(D, 128), full(2, 1, D), full(6, 1, D), full(4, 1, D),
        bulk(2, 4, 2, 2, 48, D), bulk(2, 4, 2, 48, D), bulk(SETS, 4, 2, 48, D), bulk(SETS, 2, 2, 48, D), bulk(SETS, 2, 48, D),
        bulk(3, 2, 48, D), bulk(4, 2, 48, D), bulk(2, 4, 48, D),
        dma(3, 4), dma(3, 4), dma(3, 4, 4), dma(3, 4, 4),
        dma(SETS, 2), dma(SETS, 2), dma(SETS, 2), dma(SETS, 2), dma(SETS), dma(SETS),
        dma(SETS, 2), dma(3), dma(4), dma(2, 4),
        dma(8), dma(8), dma(11), dma(6), dma(6), dma(4), dma(4),
    ]
    out, first, down, gains, _, _ = pl.pallas_call(
        layer_kernel,
        in_specs=[S, V, HBM, HBM, HBM, HBM],
        out_specs=[HBM, HBM, HBM, V, HBM, HBM],
        out_shape=[
            sds(D, 2 * T), sds(2, 96, D), sds(2, 48, D), sds(1, D), sds(D, T), sds(3 * D, T, dtype=bf16),
        ],
        scratch_shapes=scratch,
        compiler_params=pltpu.CompilerParams(collective_id=1, has_side_effects=True, vmem_limit_bytes=VMEM_MOST),
        name="layer",
    )(lengths, mask, gain, stream, w.reshape(2, 96, D), wd.reshape(2, 48, D))
    final = pl.pallas_call(
        finish_kernel,
        in_specs=[S, HBM],
        out_specs=HBM,
        out_shape=sds(D - 1, 1, 2 * T),
        scratch_shapes=[full(2, D, SLOTS), full(2, D - 1, SLOTS), dma(2), dma(2)],
        compiler_params=pltpu.CompilerParams(vmem_limit_bytes=32 * 2**20),
        name="finish",
    )(lengths, out)
    return final, first.reshape(192, D), down.reshape(96, D), gains


def separate(own, stream, w, wd, gain, doc_lengths, pad_mask, sections, groups):
    s, d = own
    stream = jnp.pad(stream[:, 0], ((0, 1), (0, 0)))
    gain = jnp.broadcast_to(gain[0][:, None], (D, 128))
    T = stream.shape[1] // sections
    nb = T // SLOTS
    own_docs = lax.dynamic_slice_in_dim(doc_lengths, s * nb, nb, axis=0)
    ends = jnp.stack([jnp.sum(own_docs[:, : j + 1], axis=1) for j in range(own_docs.shape[1])], axis=1)
    mask = lax.dynamic_slice_in_dim(pad_mask, s * T, T, axis=0).astype(f32)
    mask = jnp.broadcast_to(mask[None], (8, T))
    weights = lax.all_gather(lax.all_gather(w, "dp", axis=0, tiled=True), "section")
    wd_full = lax.all_gather(wd, ("section", "dp"), axis=0, tiled=True)
    both = lax.all_gather(stream, "section")
    x, g = lax.dynamic_slice_in_dim(both, s * T, T, axis=2)
    gains = lax.all_gather(gain, "section")
    qkv, att, lse, h0, x1, h1 = run_attn_fwd(ends, x, gains[0], gains[1], mask, weights[0])
    out1, dy, gw1, gwd, gg1 = run_ffn(g, gains[1], mask, x1, h1, weights[1], wd_full)
    out0, gw0, gg0 = run_attn_bwd(ends, x, gains[0], mask, weights[0], qkv, att, lse, h0, dy)
    gw = jnp.stack([gw0, gw1])
    gg = jnp.stack([gg0, gg1])
    first = lax.psum_scatter(gw.astype(f32), "section", scatter_dimension=0)
    first = lax.psum_scatter(first, "dp", scatter_dimension=0, tiled=True)
    down = lax.psum_scatter(gwd.astype(f32), ("section", "dp"), scatter_dimension=0, tiled=True)
    outs = lax.all_gather(jnp.stack([out0, out1]), "section")
    out = jnp.concatenate([lax.dynamic_index_in_dim(outs[i], s, 0, False) for i in range(2)], axis=1)
    gain_total = lax.psum_scatter(lax.psum(jnp.sum(gg, axis=2), "dp"), "section", scatter_dimension=0)
    return out[: D - 1][:, None], first, down, gain_total[None]


def shards(sizes, stream_pair, norm_gains, first_proj, down_proj, doc_lengths, pad_mask):
    own = lax.axis_index("section"), lax.axis_index("dp")
    sections, groups = sizes
    stream = jnp.transpose(stream_pair, (2, 0, 1))
    w = jnp.transpose(first_proj[0])
    wd = jnp.transpose(down_proj)
    if sizes == (2, 16) and stream.shape[2] == 4 * SLOTS:
        out, first, down, gain_total = layer(doc_lengths, pad_mask[None], norm_gains, stream, w, wd)
    else:
        out, first, down, gain_total = separate(
            own, stream, w, wd, norm_gains, doc_lengths, pad_mask, sections, groups
        )
    share = D // groups
    gain_share = lax.dynamic_slice_in_dim(gain_total, own[1] * share, share, axis=1)
    return jnp.transpose(out, (1, 2, 0)), gain_share, jnp.transpose(first)[None], jnp.transpose(down)


def solution(mesh):
    placed = (
        P("section", "dp", None),
        P("section", None),
        P("section", None, "dp"),
        P(None, ("section", "dp")),
        P("dp", None),
        P("dp"),
    )
    return jax.shard_map(
        functools.partial(shards, (mesh.shape["section"], mesh.shape["dp"])),
        mesh=mesh,
        in_specs=placed,
        out_specs=(
            P("section", "dp", None),
            P("section", "dp"),
            P("section", None, "dp"),
            P(None, ("section", "dp")),
        ),
        check_vma=False,
    )
```

```python
import functools
import jax, jax.numpy as jnp
from jax import lax
from jax.experimental import pallas as pl
from jax.experimental.pallas import tpu as pltpu
from jax.sharding import PartitionSpec as P

HEADS, HEAD_DIM, FF, D, SLOTS = 12, 64, 3072, 768, 512
LONGEST = 256
EPS, MASKED = 1e-05, -1e30
VMEM_MOST = 63 * 2**20
f32, bf16 = jnp.float32, jnp.bfloat16
CHUNK = 768

def nn(a, b):
    return lax.dot_general(a, b, (((1,), (0,)), ((), ())), preferred_element_type=f32)
def nt(a, b):
    return lax.dot_general(a, b, (((1,), (1,)), ((), ())), preferred_element_type=f32)
def tn(a, b):
    return lax.dot_general(a, b, (((0,), (0,)), ((), ())), preferred_element_type=f32)

def last_row(shape):
    return lax.broadcasted_iota(jnp.int32, shape, 0) == shape[0] - 1

def expanded(x):
    return jnp.where(last_row(x.shape), -jnp.sum(x, axis=0, keepdims=True), x)

def inv_rms(x):
    return lax.rsqrt(jnp.mean(x * x, axis=0, keepdims=True) + EPS)

def bias_block(ends, live, first_key, keys, first_query, queries):
    shape = (keys, queries)
    kp = lax.broadcasted_iota(jnp.int32, shape, 0) + first_key
    qp = lax.broadcasted_iota(jnp.int32, shape, 1) + first_query
    kd = sum((kp >= e).astype(jnp.int32) for e in ends)
    qd = sum((qp >= e).astype(jnp.int32) for e in ends)
    seen = (kd == qd) & (kp <= qp) & ((live > 0.5) | (kp == qp))
    return jnp.where(seen, 0.0, MASKED)

def attn_fwd(ends_ref, x_ref, g0_ref, g1_ref, mask_ref, w_ref,
             qkv_ref, att_ref, lse_ref, h0_ref, x1_ref, h1_ref, bias_ref):
    T = x_ref.shape[1]
    nb = T // SLOTS
    @pl.loop(0, T // 256)
    def _(t):
        c = pl.ds(pl.multiple_of(t * 256, 256), 256)
        x = expanded(x_ref[:, c])
        h0_ref[:, c] = (x * inv_rms(x) * g0_ref[:, :1]).astype(bf16)
    for b in range(nb):
        ends = [ends_ref[b, j] for j in range(3)]
        marks = jnp.broadcast_to(mask_ref[:1, b * SLOTS:(b + 1) * SLOTS], (128, SLOTS)).T
        for qb in range(2):
            nk = 256 * (qb + 1)
            for q0 in (0, 128):
                bias_ref[b, :nk, qb * 256 + q0: qb * 256 + q0 + 128] = bias_block(ends, marks[:nk], 0, nk, qb * 256 + q0, 128)
    @pl.loop(0, 9)
    def _(m):
        r = pl.ds(pl.multiple_of(m * 256, 256), 256)
        qkv_ref[r, :] = nn(w_ref[r, :], h0_ref[...]).astype(bf16)
    for b in range(nb):
        cols = slice(b * SLOTS, (b + 1) * SLOTS)
        @pl.loop(0, HEADS // 2)
        def _(hp):
            for hh in range(2):
                h = hp * 2 + hh
                off = pl.multiple_of(h * HEAD_DIM, HEAD_DIM)
                q = qkv_ref[pl.ds(off, HEAD_DIM), cols] * bf16(HEAD_DIM ** -0.5)
                k = qkv_ref[pl.ds(off + D, HEAD_DIM), cols].T
                v = qkv_ref[pl.ds(off + 2 * D, HEAD_DIM), cols]
                for qb in range(2):
                    nk, lo = 256 * (qb + 1), qb * 256
                    s = nn(k[:nk], q[:, lo:lo + 256]) + bias_ref[b, :nk, lo:lo + 256]
                    mx = jnp.max(s, axis=0, keepdims=True)
                    p = jnp.exp(s - mx)
                    tot = jnp.sum(p, axis=0, keepdims=True)
                    lse_ref[pl.ds(h, 1), b * SLOTS + lo: b * SLOTS + lo + 256] = mx + jnp.log(tot)
                    low = (p * (1.0 / tot)).astype(bf16)
                    att_ref[pl.ds(off, HEAD_DIM), b * SLOTS + lo: b * SLOTS + lo + 256] = nn(v[:, :nk], low).astype(bf16)
    @pl.loop(0, T // 256)
    def _(t):
        c = pl.ds(pl.multiple_of(t * 256, 256), 256)
        x = expanded(x_ref[:, c])
        a = nn(w_ref[3 * D:, :], att_ref[:, c])
        x1 = expanded(jnp.where(last_row(x.shape), 0.0, x + (a - jnp.mean(a, axis=0, keepdims=True))))
        x1_ref[:, c] = x1
        h1_ref[:, c] = (x1 * inv_rms(x1) * g1_ref[:, :1]).astype(bf16)

C0 = 0.7978845608028654
def gelu_both(u):
    u2 = u * u
    inner = C0 * u * (1.0 + 0.044715 * u2)
    t = jnp.tanh(inner)
    half = 0.5 * (1.0 + t)
    slope = half + 0.5 * u * (1.0 - t * t) * (C0 * (1.0 + 3 * 0.044715 * u2))
    return u * half, slope

def norm_back(x, r, gain, dh):
    e = gain * dh
    dx = r * e - x * (r * r * r) * jnp.mean(x * e, axis=0, keepdims=True)
    return dx, dh * x * r

def lane_fold(v):
    return sum(v[:, i * 128:(i + 1) * 128] for i in range(v.shape[1] // 128))

def ffn(g_ref, g1_ref, mask_ref, x1_ref, h1_ref, w1_ref, wd_ref,
        out1_ref, dy_ref, gw1_ref, gwd_ref, gg_ref, dm_ref, z_ref, du_ref, u_ref, macc, hacc):
    T = g_ref.shape[1]
    nt_ = T // 256
    @pl.loop(0, nt_)
    def _(t):
        c = pl.ds(pl.multiple_of(t * 256, 256), 256)
        g = g_ref[:, c] * mask_ref[:1, c]
        dm_ref[:, c] = (g - jnp.mean(g, axis=0, keepdims=True)).astype(bf16)
    macc[...] = jnp.zeros_like(macc)
    hacc[...] = jnp.zeros_like(hacc)
    @pl.loop(0, FF // CHUNK)
    def _(p):
        base = p * CHUNK
        @pl.loop(0, CHUNK // 256)
        def _(m):
            r = pl.ds(pl.multiple_of(base + m * 256, 256), 256)
            rl = pl.ds(pl.multiple_of(m * 256, 256), 256)
            for n in range(T // 512):
                cs = slice(n * 512, (n + 1) * 512)
                z, slope = gelu_both(nn(w1_ref[r, :], h1_ref[:, cs]))
                z_ref[rl, cs] = z.astype(bf16)
                du_ref[rl, cs] = (nn(wd_ref[r, :], dm_ref[:, cs]) * slope).astype(bf16)
        rows = pl.ds(pl.multiple_of(base, CHUNK), CHUNK)
        @pl.loop(0, 3)
        def _(m):
            o = pl.ds(pl.multiple_of(m * 256, 256), 256)
            macc[o, :] += tn(wd_ref[rows, o], z_ref[...])
            hacc[o, :] += tn(w1_ref[rows, o], du_ref[...])
            r = pl.ds(pl.multiple_of(base + m * 256, 256), 256)
            gw1_ref[r, :] = nt(du_ref[o, :], h1_ref[...]).astype(gw1_ref.dtype)
            gwd_ref[r, :] = nt(z_ref[o, :], dm_ref[...]).astype(gwd_ref.dtype)
    gg_ref[...] = jnp.zeros_like(gg_ref)
    @pl.loop(0, nt_)
    def _(t):
        c = pl.ds(pl.multiple_of(t * 256, 256), 256)
        x1, m = x1_ref[:, c], macc[:, c]
        out1_ref[:, c] = x1 + (m - jnp.mean(m, axis=0, keepdims=True))
        g = g_ref[:, c] * mask_ref[:1, c]
        dx, gg = norm_back(x1, inv_rms(x1), g1_ref[:, :1], hacc[:, c])
        gg_ref[...] += lane_fold(gg)
        dy_ref[:, c] = g + dx - dx[D - 1:, :]

def attn_bwd(ends_ref, x_ref, g0_ref, mask_ref, w_ref, qkv_ref, att_ref, lse_ref, h0_ref, dy_ref,
             out0_ref, gw_ref, gg_ref, da_ref, dat_ref, dqkv_ref, bias_ref):
    T = x_ref.shape[1]
    nb = T // SLOTS
    for b in range(nb):
        ends = [ends_ref[b, j] for j in range(3)]
        marks = jnp.broadcast_to(mask_ref[:1, b * SLOTS:(b + 1) * SLOTS], (128, SLOTS)).T
        for qb in range(2):
            nk = 256 * (qb + 1)
            for q0 in (0, 128):
                bias_ref[b, :nk, qb * 256 + q0: qb * 256 + q0 + 128] = bias_block(ends, marks[:nk], 0, nk, qb * 256 + q0, 128)
    @pl.loop(0, T // 256)
    def _(t):
        c = pl.ds(pl.multiple_of(t * 256, 256), 256)
        dy = dy_ref[:, c]
        da_ref[:, c] = (dy - jnp.mean(dy, axis=0, keepdims=True)).astype(bf16)
    @pl.loop(0, 3)
    def _(m):
        o = pl.ds(pl.multiple_of(m * 256, 256), 256)
        r = pl.ds(pl.multiple_of(3 * D + m * 256, 256), 256)
        gw_ref[r, :] = nt(da_ref[o, :], att_ref[...]).astype(gw_ref.dtype)
        dat_ref[o, :] = tn(w_ref[3 * D:, o], da_ref[...]).astype(bf16)
    for b in range(nb):
        cols = slice(b * SLOTS, (b + 1) * SLOTS)
        @pl.loop(0, HEADS)
        def _(h):
            off = pl.multiple_of(h * HEAD_DIM, HEAD_DIM)
            q = qkv_ref[pl.ds(off, HEAD_DIM), cols] * bf16(HEAD_DIM ** -0.5)
            kt = qkv_ref[pl.ds(off + D, HEAD_DIM), cols]
            k = kt.T
            v = qkv_ref[pl.ds(off + 2 * D, HEAD_DIM), cols].T
            d = dat_ref[pl.ds(off, HEAD_DIM), cols]
            dks, dvs = [], []
            for qb in range(2):
                nk, lo = 256 * (qb + 1), qb * 256
                s = nn(k[:nk], q[:, lo:lo + 256]) + bias_ref[b, :nk, lo:lo + 256]
                p = jnp.exp(s - lse_ref[pl.ds(h, 1), b * SLOTS + lo: b * SLOTS + lo + 256])
                dp = nn(v[:nk], d[:, lo:lo + 256])
                ds = (p * (dp - jnp.sum(p * dp, axis=0, keepdims=True))).astype(bf16)
                low = p.astype(bf16)
                dqkv_ref[pl.ds(off, HEAD_DIM), b * SLOTS + lo: b * SLOTS + lo + 256] = (nn(kt[:, :nk], ds) * HEAD_DIM ** -0.5).astype(bf16)
                dks.append(nt(q[:, lo:lo + 256], ds))
                dvs.append(nt(d[:, lo:lo + 256], low))
            for at, parts in ((D, dks), (2 * D, dvs)):
                dqkv_ref[pl.ds(off + at, HEAD_DIM), b * SLOTS: b * SLOTS + 256] = (parts[0] + parts[1][:, :256]).astype(bf16)
                dqkv_ref[pl.ds(off + at, HEAD_DIM), b * SLOTS + 256: (b + 1) * SLOTS] = parts[1][:, 256:].astype(bf16)
    @pl.loop(0, 9)
    def _(m):
        r = pl.ds(pl.multiple_of(m * 256, 256), 256)
        gw_ref[r, :] = nt(dqkv_ref[r, :], h0_ref[...]).astype(gw_ref.dtype)
    gg_ref[...] = jnp.zeros_like(gg_ref)
    @pl.loop(0, T // 256)
    def _(t):
        c = pl.ds(pl.multiple_of(t * 256, 256), 256)
        x = expanded(x_ref[:, c])
        dh = tn(w_ref[:3 * D, :], dqkv_ref[:, c])
        dx, gg = norm_back(x, inv_rms(x), g0_ref[:, :1], dh)
        gg_ref[...] += lane_fold(gg)
        out0_ref[:, c] = dy_ref[:, c] + dx - dx[D - 1:, :]

V = pl.BlockSpec(memory_space=pltpu.VMEM)
S = pl.BlockSpec(memory_space=pltpu.SMEM)
def sds(*shape, dtype=f32):
    return jax.ShapeDtypeStruct(shape, dtype)
PARAMS = pltpu.CompilerParams(vmem_limit_bytes=60 * 2**20)

def run_attn_fwd(ends, x, g0, g1, mask, w):
    T = x.shape[1]
    return pl.pallas_call(attn_fwd, in_specs=[S] + [V] * 5, out_specs=[V] * 6,
        out_shape=[sds(3 * D, T, dtype=bf16), sds(D, T, dtype=bf16), sds(16, T), sds(D, T, dtype=bf16), sds(D, T), sds(D, T, dtype=bf16)],
        scratch_shapes=[pltpu.VMEM((T // SLOTS, SLOTS, SLOTS), f32)], compiler_params=PARAMS, name="attn_fwd")(ends, x, g0, g1, mask, w)

def run_ffn(g, g1, mask, x1, h1, w1, wd, gdt=bf16):
    T = g.shape[1]
    return pl.pallas_call(ffn, in_specs=[V] * 7, out_specs=[V] * 5,
        out_shape=[sds(D, T), sds(D, T), sds(FF, D, dtype=gdt), sds(FF, D, dtype=gdt), sds(D, 128)],
        scratch_shapes=[pltpu.VMEM((D, T), bf16), pltpu.VMEM((CHUNK, T), bf16), pltpu.VMEM((CHUNK, T), bf16), pltpu.VMEM((8, 128), f32), pltpu.VMEM((D, T), f32), pltpu.VMEM((D, T), f32)],
        compiler_params=PARAMS, name="ffn")(g, g1, mask, x1, h1, w1, wd)

def run_attn_bwd(ends, x, g0, mask, w, qkv, att, lse, h0, dy, gdt=bf16):
    T = x.shape[1]
    return pl.pallas_call(attn_bwd, in_specs=[S] + [V] * 9, out_specs=[V] * 3,
        out_shape=[sds(D, T), sds(FF, D, dtype=gdt), sds(D, 128)],
        scratch_shapes=[pltpu.VMEM((D, T), bf16), pltpu.VMEM((D, T), bf16), pltpu.VMEM((3 * D, T), bf16), pltpu.VMEM((T // SLOTS, SLOTS, SLOTS), f32)],
        compiler_params=PARAMS, name="attn_bwd")(ends, x, g0, mask, w, qkv, att, lse, h0, dy)


MESH = pl.DeviceIdType.MESH
HBM = pl.BlockSpec(memory_space=pl.ANY)


def push(src, dst, send, recv, device):
    copy = pltpu.make_async_remote_copy(
        src_ref=src, dst_ref=dst, send_sem=send, recv_sem=recv, device_id=device, device_id_type=MESH
    )
    copy.start()
    return copy


DIST = (0, 1, 3, 2)
CHUNKS = (0, 2, 1, 3)
FAR_KIND = -1
FAR_SETS = ()
TILE = 256
SCALE = HEAD_DIM ** -0.5
KIND_A, KIND_D, KIND_W = 0, 1, 2
SETS = 12
PLANES = (3, 0, 1, 2)


def wide(v):
    return v.astype(f32)


def square(v):
    return v.reshape(-1, D)


def at_step(k):
    return lax.rem(2 * k, 3) + 3 * (k // 3)


def layer_kernel(
    len_ref, mask_ref, gain_ref, stream, w_ref, wd_ref,
    out, first, down, gain_out, spill_x, spill_q,
    fa, fw, fd, X, G, xt, gt, QKV, ATT, H0, H1, DM, MACC, HACC, BIAS, LSE, MK, GR, GCOL, GG, GV, GL, GT,
    STG, STGD, ACC, L1, L2, L3W, L3A, L3D,
    zs, zr, ps, pr, ss, sr, p1s, p1r, p2s, p2r, p3s, rw, ra, rd, i_s, i_r, local, gs, gr, gss, gsr, vs, vr,
):
    s, d = lax.axis_index("section"), lax.axis_index("dp")
    x, y, z, xy = lax.rem(d, 2), lax.rem(d // 2, 2), d // 4, lax.rem(d, 4)
    t = 1 - s
    over_y, over_x = (1 - y) * 2 + x, y * 2 + 1 - x
    xy1, xy2, xy3 = t * over_y + s * over_x, s * over_y + t * over_x, 3 - xy
    sib, n1, n2 = (t, d), (s, z * 4 + xy1), (s, z * 4 + xy2)
    T = X.shape[1]
    nb = T // SLOTS
    tiles = T // TILE
    col = lambda i: pl.ds(pl.multiple_of(i * TILE, TILE), TILE)
    at_plane = lambda p: (s, p * 4 + xy)

    def plane(i, kind=KIND_W):
        if kind == KIND_D:
            return 2 * lax.rem(z + i // 2, 2) + i % 2
        return lax.rem(z + 4 - (DIST if kind == KIND_A else CHUNKS)[i], 4)

    def wait_recv(dst, sem):
        pltpu.make_async_remote_copy(
            src_ref=dst, dst_ref=dst, send_sem=sem, recv_sem=sem, device_id=sib, device_id_type=MESH
        ).wait_recv()

    def wait_send(src, sem):
        pltpu.make_async_remote_copy(
            src_ref=src, dst_ref=src, send_sem=sem, recv_sem=sem, device_id=sib, device_id_type=MESH
        ).wait_send()

    def move(src, dst, sem):
        pltpu.make_async_copy(src, dst, sem).start()

    def moved(src, dst, sem):
        pltpu.make_async_copy(src, dst, sem).wait()

    def slab(kind, zz, q, h):
        return fd.at[:, zz, q, h] if kind == KIND_D else (fa, None, fw)[kind].at[zz, q, h]

    def group(kind, zz, h):
        return fd.at[:, zz, :, h] if kind == KIND_D else (fa, None, fw)[kind].at[zz, :, h]

    def Z(kind, far):
        own = slab(kind, z, xy, s)
        push(own, own, zs.at[kind, far], zr.at[kind, far], at_plane(lax.rem(z + far, 4)))

    def A(kind, i):
        zz = plane(i, kind)
        here = slab(kind, zz, xy, s)
        if kind == KIND_D:
            @pl.when(zz != z)
            def _():
                wait_recv(here, zr.at[kind, lax.rem(z + 4 - zz, 4)])
        elif i:
            wait_recv(here, zr.at[kind, (DIST if kind == KIND_A else CHUNKS)[i]])
        if kind == KIND_A and i in (1, 2):
            Z(kind, DIST[i + 1])
        elif kind == KIND_A and i == 3:
            for far in (1, 2, 3):
                Z(KIND_D, far)
        elif kind == KIND_D and i == 1:
            Z(KIND_W, 2)
        elif kind == KIND_W and i == 1:
            Z(KIND_W, 1)
            Z(KIND_W, 3)
        push(here, here, ps.at[kind, i, 0], pr.at[kind, i, 0], n1)
        push(here, here, ps.at[kind, i, 1], pr.at[kind, i, 1], n2)

    def B(kind, i):
        if kind == FAR_KIND and i:
            return
        here = slab(kind, plane(i, kind), xy1, s)
        wait_recv(here, pr.at[kind, i, 0])
        push(here, here, ps.at[kind, i, 2], pr.at[kind, i, 2], n2)

    def C(kind, i):
        zz = plane(i, kind)
        wait_recv(slab(kind, zz, xy2, s), pr.at[kind, i, 1])
        if kind == FAR_KIND and i:
            wait_recv(slab(kind, zz, xy1, s), pr.at[kind, i, 0])
            wait_recv(slab(kind, zz, xy3, s), vr.at[CHUNKS[i]])
        else:
            wait_recv(slab(kind, zz, xy3, s), pr.at[kind, i, 2])
        if kind == FAR_KIND and i == 0:
            far_slab = slab(kind, z, xy3, s)
            for far in (2, 1, 3):
                push(far_slab, far_slab, vs.at[far], vr.at[far], at_plane(lax.rem(z + far, 4)))
        here = group(kind, zz, s)
        push(here, here, ps.at[kind, i, 3], pr.at[kind, i, 3], sib)

    def E(kind, i):
        wait_recv(group(kind, plane(i, kind), t), pr.at[kind, i, 3])

    def sent(kind):
        for i in range(4):
            zz = plane(i, kind)
            if i:
                wait_send(slab(kind, z, xy, s), zs.at[kind, i])
            wait_send(slab(kind, zz, xy, s), ps.at[kind, i, 0])
            wait_send(slab(kind, zz, xy, s), ps.at[kind, i, 1])
            if kind == FAR_KIND and i:
                wait_send(slab(kind, z, xy3, s), vs.at[i])
            else:
                wait_send(slab(kind, zz, xy1, s), ps.at[kind, i, 2])
            wait_send(group(kind, zz, s), ps.at[kind, i, 3])

    def to_sibling(j, slot, down_set=False):
        if down_set:
            for sub in range(2):
                push(STGD.at[sub, :, t], ACC.at[j, :, sub], ss.at[j, sub], sr.at[j, sub], sib)
        else:
            push(STG.at[slot, :, t], ACC.at[j], ss.at[j, 0], sr.at[j, 0], sib)

    def staged_free(j, down_set=False):
        if down_set:
            for sub in range(2):
                wait_send(STGD.at[sub, :, t], ss.at[j, sub])
        else:
            wait_send(STG.at[0, :, t], ss.at[j, 0])

    def slot_of(j):
        return j // 2 % 2 if j < 8 else j % 2

    def R1(j):
        if j < 8 and j % 2:
            for sub in range(2):
                wait_recv(ACC.at[j, :, sub], sr.at[j, sub])
                for q in range(4):
                    ACC[j, q, sub] = (wide(ACC[j, q, sub]) + wide(STGD[sub, q, s])).astype(bf16)
        else:
            wait_recv(ACC.at[j], sr.at[j, 0])
            for q in range(4):
                ACC[j, q] = (wide(ACC[j, q]) + wide(STG[slot_of(j), q, s])).astype(bf16)
        push(ACC.at[j, xy2], L1.at[j, 0], p1s.at[j, 0], p1r.at[j, 0], n2)
        if j in FAR_SETS:
            push(ACC.at[j, xy3], L1.at[j, 1], p1s.at[j, 1], p1r.at[j, 1], at_plane(plane(j // 2)))
        elif j or not FAR_SETS:
            push(ACC.at[j, xy3], L1.at[j, 1], p1s.at[j, 1], p1r.at[j, 1], n2)

    def RD():
        if not FAR_SETS:
            return
        v = wide(ACC[0, xy3])
        for j in FAR_SETS:
            wait_recv(L1.at[j, 1], p1r.at[j, 1])
            v = v + wide(L1[j, 1])
        ACC[0, xy3] = v.astype(bf16)
        push(ACC.at[0, xy3], L1.at[0, 1], p1s.at[0, 1], p1r.at[0, 1], n2)

    def R2(j):
        wait_recv(L1.at[j, 0], p1r.at[j, 0])
        ACC[j, xy] = (wide(ACC[j, xy]) + wide(L1[j, 0])).astype(bf16)
        if j not in FAR_SETS:
            wait_recv(L1.at[j, 1], p1r.at[j, 1])
            ACC[j, xy1] = (wide(ACC[j, xy1]) + wide(L1[j, 1])).astype(bf16)
        push(ACC.at[j, xy1], L2.at[j], p2s.at[j], p2r.at[j], n1)

    def ends_of(j):
        if j >= 8:
            p = PLANES[j - 8]
            return [(z != p, ACC.at[j, xy], L3A.at[z], p3s.at[j, 0], ra.at[z], p)]
        k = j // 2
        p = plane(k)
        if j % 2 == 0:
            return [(None, ACC.at[j, xy], L3W.at[k - 1], p3s.at[j, 0], rw.at[k - 1], p)] if k else []
        made = []
        for sub in range(2):
            to = 2 * lax.rem(p, 2) + sub
            made.append((z != to, ACC.at[j, xy, sub], L3D.at[p // 2, z], p3s.at[j, sub], rd.at[p // 2, z], to))
        return made

    def guarded(cond, act):
        act() if cond is None else pl.when(cond)(act)

    def R3(j):
        wait_recv(L2.at[j], p2r.at[j])
        ACC[j, xy] = (wide(ACC[j, xy]) + wide(L2[j])).astype(bf16)
        for cond, src, dst, ssem, rsem, to in ends_of(j):
            guarded(cond, lambda src=src, dst=dst, ssem=ssem, rsem=rsem, to=to: push(src, dst, ssem, rsem, at_plane(to)) and None)

    def scattered(j):
        wait_send(ACC.at[j, xy2], p1s.at[j, 0])
        wait_send(ACC.at[j, xy3], p1s.at[j, 1])
        wait_send(ACC.at[j, xy1], p2s.at[j])
        for cond, src, dst, ssem, rsem, to in ends_of(j):
            guarded(cond, lambda src=src, ssem=ssem: wait_send(src, ssem))

    QKV_SETS = pl.ds(9, 3)

    def G1(n):
        q = (lax.rem(y + 1 - n % 2, 2)) * 2 + lax.rem(x + 1 - n // 2, 2)
        slot = (n + 1) % 2
        wait_recv(ACC.at[QKV_SETS, q], gsr.at[n])
        for part in range(3):
            ACC[9 + part, q] = (wide(ACC[9 + part, q]) + wide(STG[slot, part, s])).astype(bf16)
        if n == 0:
            push(ACC.at[QKV_SETS, xy3], L1.at[QKV_SETS, 1], p1s.at[9, 1], p1r.at[9, 1], n2)
        elif n < 3:
            @pl.when(s == n - 1)
            def _():
                push(ACC.at[QKV_SETS, xy2], L1.at[QKV_SETS, 0], p1s.at[9, 0], p1r.at[9, 0], n2)

    def G2():
        wait_recv(L1.at[QKV_SETS, 1], p1r.at[9, 1])
        for j in range(9, 12):
            ACC[j, xy1] = (wide(ACC[j, xy1]) + wide(L1[j, 1])).astype(bf16)
        push(ACC.at[QKV_SETS, xy1], L2.at[QKV_SETS], p2s.at[9], p2r.at[9], n1)

    def G3():
        wait_recv(L1.at[QKV_SETS, 0], p1r.at[9, 0])
        wait_recv(L2.at[QKV_SETS], p2r.at[9])
        for j in range(9, 12):
            ACC[j, xy] = (wide(ACC[j, xy]) + wide(L1[j, 0]) + wide(L2[j])).astype(bf16)
            for cond, src, dst, ssem, rsem, to in ends_of(j):
                guarded(cond, lambda src=src, dst=dst, ssem=ssem, rsem=rsem, to=to: push(src, dst, ssem, rsem, at_plane(to)) and None)

    def G_sent():
        wait_send(ACC.at[QKV_SETS, xy3], p1s.at[9, 1])
        wait_send(ACC.at[QKV_SETS, xy2], p1s.at[9, 0])
        wait_send(ACC.at[QKV_SETS, xy1], p2s.at[9])
        for j in range(9, 12):
            for cond, src, dst, ssem, rsem, to in ends_of(j):
                guarded(cond, lambda src=src, ssem=ssem: wait_send(src, ssem))

    barrier = pltpu.get_barrier_semaphore()
    partners = [sib, n1, n2, *(at_plane(lax.rem(z + r, 4)) for r in (1, 2, 3))]
    for device in partners:
        pl.semaphore_signal(barrier, inc=1, device_id=device, device_id_type=MESH)
    pl.semaphore_wait(barrier, len(partners))

    mine, other = pl.ds(pl.multiple_of(s * T, T), T), pl.ds(pl.multiple_of(t * T, T), T)
    top = pl.ds(0, D - 8)

    def rows_of(part):
        return stream.at[top, 0, part], stream.at[pl.ds(D - 9, 8), 0, part]

    @pl.when(s == 0)
    def _():
        push(w_ref.at[1], fa.at[z, xy, 1], i_s.at[0], i_r.at[0], sib)
        move(w_ref.at[0], fa.at[z, xy, 0], local.at[0])

    @pl.when(s == 1)
    def _():
        push(w_ref.at[0], fw.at[z, xy, 0], i_s.at[0], i_r.at[0], sib)
        move(w_ref.at[1], fw.at[z, xy, 1], local.at[0])

    push(wd_ref.at[t], fd.at[s, z, xy, t], i_s.at[1], i_r.at[1], sib)
    move(wd_ref.at[s], fd.at[s, z, xy, s], local.at[1])
    push(gain_ref, GR.at[s], i_s.at[2], i_r.at[2], sib)
    move(gain_ref, GR.at[s], local.at[2])

    def stream_in(keep, tail):
        def go():
            a, b = rows_of(mine)
            move(a, keep.at[top], local.at[3])
            move(b, tail, local.at[4])
        return go

    def stream_out(give, tail):
        def go():
            a, b = rows_of(other)
            push(a, give.at[top], i_s.at[3], i_r.at[3], sib)
            push(b, tail, i_s.at[4], i_r.at[4], sib)
        return go

    pl.when(s == 0)(stream_in(X, xt))
    pl.when(s == 1)(stream_in(G, gt))

    @pl.when(s == 0)
    def _():
        moved(w_ref.at[0], fa.at[z, xy, 0], local.at[0])
        wait_send(w_ref.at[1], i_s.at[0])

    @pl.when(s == 1)
    def _():
        wait_recv(fa.at[z, xy, 1], i_r.at[0])

    Z(KIND_A, DIST[1])
    A(KIND_A, 0)
    pl.when(s == 0)(stream_out(X, xt))
    pl.when(s == 1)(stream_out(G, gt))

    def lengths(b):
        return [len_ref[s * nb + b, j] for j in range(4)]

    shifts, ends = [], []
    for b in range(nb):
        size = lengths(b)
        stops = [size[0], size[0] + size[1], size[0] + size[1] + size[2]]
        starts = [0, *stops]
        shifts.append(sum(jnp.where(size[j] == LONGEST, starts[j], 0) for j in range(1, 4)))
        ends.append(stops)

    moved(gain_ref, GR.at[s], local.at[2])
    wait_recv(GR.at[t], i_r.at[2])
    for j in range(2):
        GCOL[j] = jnp.broadcast_to(GR[j], (128, D)).T

    def turn(ref, tail, b):
        cols = slice(b * SLOTS, (b + 1) * SLOTS)
        amount = lax.rem(SLOTS - shifts[b], SLOTS)
        ref[D - 8:, cols] = jnp.concatenate([tail[1:, cols], jnp.zeros((1, SLOTS), f32)], axis=0)

        @pl.loop(0, 8)
        def _(i):
            r = pl.ds(pl.multiple_of(i * 96, 96), 96)
            ref[r, cols] = pltpu.roll(ref[r, cols], amount, 1)

    def x_arrived():
        @pl.when(s == 0)
        def _():
            a, b = rows_of(mine)
            moved(a, X.at[top], local.at[3])
            moved(b, xt, local.at[4])

        @pl.when(s == 1)
        def _():
            wait_recv(X.at[top], i_r.at[3])
            wait_recv(xt, i_r.at[4])

    def g_arrived():
        @pl.when(s == 1)
        def _():
            a, b = rows_of(mine)
            moved(a, G.at[top], local.at[3])
            moved(b, gt, local.at[4])

        @pl.when(s == 0)
        def _():
            wait_recv(G.at[top], i_r.at[3])
            wait_recv(gt, i_r.at[4])

    def masks():
        for b in range(nb):
            cols = slice(b * SLOTS, (b + 1) * SLOTS)
            amount = lax.rem(SLOTS - shifts[b], SLOTS)
            live = wide(mask_ref[:, pl.ds(pl.multiple_of(s * T + b * SLOTS, SLOTS), SLOTS)])
            MK[:, cols] = pltpu.roll(jnp.broadcast_to(live, (8, SLOTS)), amount, 1)
            marks = jnp.broadcast_to(MK[:1, cols], (128, SLOTS)).T
            for qb in range(2):
                for half in range(2):
                    shape = (TILE, 128)
                    kp = lax.broadcasted_iota(jnp.int32, shape, 0) + qb * TILE
                    qp = lax.broadcasted_iota(jnp.int32, shape, 1) + qb * TILE + half * 128

                    def doc(p):
                        first_place = p + shifts[b]
                        first_place = first_place - jnp.where(first_place >= SLOTS, SLOTS, 0)
                        return sum((first_place >= e).astype(jnp.int32) for e in ends[b])

                    seen = (doc(kp) == doc(qp)) & (kp <= qp)
                    seen = seen & ((marks[qb * TILE:(qb + 1) * TILE] > 0.5) | (kp == qp))
                    BIAS[b, qb, :, half * 128:(half + 1) * 128] = jnp.where(seen, 0.0, MASKED)

    def normed_in():
        @pl.loop(0, tiles)
        def _(i):
            c = col(i)
            v = expanded(X[:, c])
            X[D - 8:, c] = v[D - 8:]
            H0[:, c] = (v * inv_rms(v) * GCOL[0, :, :1]).astype(bf16)

    def cotangent():
        @pl.loop(0, tiles)
        def _(i):
            c = col(i)
            v = G[:, c] * MK[:1, c]
            G[:, c] = v
            DM[:, c] = (v - jnp.mean(v, axis=0, keepdims=True)).astype(bf16)

    masks()
    A(KIND_A, 1)
    B(KIND_A, 0)
    x_arrived()
    turn(X, xt, 0)
    A(KIND_A, 2)
    B(KIND_A, 1)
    turn(X, xt, 1)
    C(KIND_A, 0)
    normed_in()
    move(X, spill_x, local.at[5])

    @pl.when(s == 0)
    def _():
        wait_recv(fw.at[z, xy, 0], i_r.at[0])

    @pl.when(s == 1)
    def _():
        moved(w_ref.at[1], fw.at[z, xy, 1], local.at[0])
        wait_send(w_ref.at[0], i_s.at[0])

    moved(wd_ref.at[s], fd.at[s, z, xy, s], local.at[1])
    wait_recv(fd.at[t, z, xy, s], i_r.at[1])
    A(KIND_A, 3)
    B(KIND_A, 2)
    g_arrived()
    turn(G, gt, 0)
    C(KIND_A, 1)
    A(KIND_D, 0)
    B(KIND_A, 3)
    turn(G, gt, 1)
    C(KIND_A, 2)
    cotangent()
    C(KIND_A, 3)
    for i in range(4):
        E(KIND_A, i)
    A(KIND_D, 1)
    B(KIND_D, 0)

    def ticks(index, table):
        for at, steps in table.items():
            @pl.when(index == at)
            def _(steps=steps):
                for act, *args in steps:
                    act(*args)

    @pl.loop(0, 3)
    def _(p):
        rows = pl.ds(pl.multiple_of(p * D, D), D)
        QKV[rows, :] = nn(square(fa[p]), H0[...]).astype(bf16)
        ticks(p, {1: [(A, KIND_W, 0), (B, KIND_D, 1)], 2: [(C, KIND_D, 0)]})

    units = [(h, qb) for h in range(4) for qb in range(2)]

    def spots(i):
        b = i // 3
        def spot(u):
            head = lax.rem(i, 3) * 4 + u[0]
            return head, pl.multiple_of(head * HEAD_DIM, HEAD_DIM), pl.ds(pl.multiple_of(b * SLOTS + u[1] * TILE, TILE), TILE)
        return b, spot

    def three(off, c):
        return [QKV[pl.ds(off + j * D, HEAD_DIM), c] for j in range(3)]

    @pl.loop(0, 3 * nb)
    def _(i):
        b, spot = spots(i)
        scores, probs = {}, {}
        for u in units:
            head, off, c = spot(u)
            q, k, v = three(off, c)
            scores[u] = nn(k.T, q * bf16(SCALE))
        for u in units:
            head, off, c = spot(u)
            v = scores[u] + BIAS[b, u[1]]
            highest = jnp.max(v, axis=0, keepdims=True)
            p = jnp.exp(v - highest)
            total = jnp.sum(p, axis=0, keepdims=True)
            LSE[pl.ds(head, 1), c] = highest + jnp.log(total)
            probs[u] = (p * (1.0 / total)).astype(bf16)
        for u in units:
            head, off, c = spot(u)
            ATT[pl.ds(off, HEAD_DIM), c] = nn(QKV[pl.ds(off + 2 * D, HEAD_DIM), c], probs[u]).astype(bf16)
        ticks(i, {1: [(A, KIND_W, 1), (B, KIND_W, 0), (C, KIND_D, 1)], 3: [(A, KIND_D, 2), (B, KIND_W, 1)], 5: [(C, KIND_W, 0)]})

    move(QKV, spill_q, local.at[6])
    moved(X, spill_x, local.at[5])

    @pl.loop(0, tiles)
    def _(i):
        c = col(i)
        a = nn(square(fa[3]), ATT[:, c])
        v = X[:, c] + (a - jnp.mean(a, axis=0, keepdims=True))
        v = expanded(jnp.where(last_row(v.shape), 0.0, v))
        X[:, c] = v
        H1[:, c] = (v * inv_rms(v) * GCOL[1, :, :1]).astype(bf16)
        ticks(i, {0: [(A, KIND_D, 3), (B, KIND_D, 2)], 2: [(C, KIND_W, 1)]})

    A(KIND_W, 2)
    B(KIND_D, 3)
    MACC[...] = jnp.zeros_like(MACC)
    HACC[...] = jnp.zeros_like(HACC)
    moved(QKV, spill_q, local.at[6])
    E(KIND_D, 0)
    E(KIND_D, 1)
    E(KIND_W, 0)
    ZT, DU = QKV.at[pl.ds(0, D)], QKV.at[pl.ds(D, D)]

    def stage_rows(slot, left, right, by_plane):
        v = nt(left, right).astype(bf16)
        if by_plane:
            STG[slot] = v.reshape(4, 2, 2, 48, D)
        else:
            STGD[...] = v.reshape(2, 4, 2, 48, D)

    FFN_TICKS = {
        (0, "a"): [(A, KIND_W, 3), (B, KIND_W, 2), (C, KIND_D, 2)],
        (0, "w"): [(C, KIND_D, 3)], (0, "d"): [(B, KIND_W, 3), (C, KIND_W, 2)],
        (0, "t0"): [(R1, 0)], (0, "t1"): [(R1, 1), (E, KIND_W, 1)],
        (1, "a"): [(C, KIND_W, 3)], (1, "t0"): [(R1, 2)],
        (1, "t1"): [(R1, 3), (R2, 0), (E, KIND_D, 2), (E, KIND_D, 3), (E, KIND_W, 2)],
        (2, "a"): [(R2, 1)], (2, "d"): [(R3, 0)], (2, "t0"): [(R1, 4), (R2, 2)],
        (2, "t1"): [(R1, 5), (R3, 1), (E, KIND_W, 3)],
        (3, "a"): [(R2, 3)], (3, "d"): [(R3, 2)], (3, "t0"): [(R1, 6), (R2, 4)], (3, "t1"): [(R1, 7), (R3, 3)],
    }

    @pl.loop(0, 4)
    def _(k):
        p = lax.rem(z + 4 - at_step(k), 4)

        def tick(name):
            ticks(k, {kk: steps for (kk, n), steps in FFN_TICKS.items() if n == name})

        def down_rows():
            return square(fd[p // 2, pl.ds(2 * lax.rem(p, 2), 2)])

        for i in range(tiles):
            c = slice(i * TILE, (i + 1) * TILE)
            before, back = nn(square(fw[p]), H1[:, c]), nn(down_rows(), DM[:, c])
            act, slope = gelu_both(before)
            ZT[:, c] = act.astype(bf16)
            DU[:, c] = (back * slope).astype(bf16)
        tick("a")

        slot = lax.rem(k, 2)

        @pl.when(k > 1)
        def _():
            staged_free(2 * k - 4)
        stage_rows(slot, DU[...], H1[...], True)
        to_sibling(2 * k, slot)
        tick("w")

        @pl.when(k > 0)
        def _():
            staged_free(2 * k - 1, True)
        stage_rows(0, ZT[...], DM[...], False)
        to_sibling(2 * k + 1, 0, True)
        tick("d")
        MACC[...] += tn(down_rows(), ZT[...])
        tick("t0")
        HACC[...] += tn(square(fw[p]), DU[...])
        tick("t1")

    move(spill_q, QKV, local.at[6])
    GG[...] = jnp.zeros_like(GG)

    @pl.loop(0, tiles)
    def _(i):
        c = col(i)
        v, m = X[:, c], MACC[:, c]
        MACC[:, c] = v + (m - jnp.mean(m, axis=0, keepdims=True))
        dx, part = norm_back(v, inv_rms(v), GCOL[1, :, :1], HACC[:, c])
        GG[...] += lane_fold(part)
        G[:, c] = G[:, c] + dx - dx[D - 1:, :]
        ticks(i, {2: [(R2, 5)]})
    GV[1] = jnp.sum(GG[...].T, axis=0, keepdims=True)

    @pl.when(s == 1)
    def _():
        move(MACC, out.at[:, mine], local.at[7])

    @pl.when(s == 0)
    def _():
        push(MACC, out.at[:, mine], i_s.at[5], i_r.at[5], sib)

    move(spill_x, HACC, local.at[5])

    @pl.loop(0, tiles)
    def _(i):
        c = col(i)
        v = G[:, c]
        DM[:, c] = (v - jnp.mean(v, axis=0, keepdims=True)).astype(bf16)

    staged_free(4)
    staged_free(6)
    staged_free(7, True)
    stage_rows(0, DM[...], ATT[...], True)
    to_sibling(8, 0)
    H1[...] = tn(square(fa[3]), DM[...]).astype(bf16)
    R1(8)
    moved(spill_q, QKV, local.at[6])

    GROUP_TICKS = {
        (0, "0"): [(R3, 4)], (0, "1"): [(R2, 6)], (0, "g"): [(R3, 5)],
        (1, "0"): [(R2, 7), (G1, 0)], (1, "1"): [(R3, 6)], (1, "g"): [(R2, 8)],
        (2, "0"): [(R3, 7), (G1, 1)], (2, "g"): [(R3, 8)],
        (3, "0"): [(G1, 2), (G2,)],
    }

    @pl.loop(0, 4)
    def _(n):
        q = lax.rem(y + 1 - lax.rem(n, 2), 2) * 2 + lax.rem(x + 1 - n // 2, 2)

        def tick(name):
            ticks(n, {nn_: steps for (nn_, name_), steps in GROUP_TICKS.items() if name_ == name})

        for b in range(nb):
            picks = [(h, qb) for h in range(3) for qb in range(2)]
            spot = lambda u: (q * 3 + u[0], pl.multiple_of((q * 3 + u[0]) * HEAD_DIM, HEAD_DIM), slice(b * SLOTS + u[1] * TILE, b * SLOTS + (u[1] + 1) * TILE))
            scores, dprobs, probs, grads = {}, {}, {}, {}
            for u in picks:
                head, off, c = spot(u)
                qq, kk, vv = three(off, c)
                scores[u] = nn(kk.T, qq * bf16(SCALE))
                dprobs[u] = nn(vv.T, H1[pl.ds(off, HEAD_DIM), c])
            for u in picks:
                head, off, c = spot(u)
                p = jnp.exp(scores[u] + BIAS[b, u[1]] - LSE[pl.ds(head, 1), c])
                dp = dprobs[u]
                grads[u] = (p * (dp - jnp.sum(p * dp, axis=0, keepdims=True))).astype(bf16)
                probs[u] = p.astype(bf16)
            for u in picks:
                head, off, c = spot(u)
                qq, kk, _ = three(off, c)
                QKV[pl.ds(off, HEAD_DIM), c] = (nn(kk, grads[u]) * SCALE).astype(bf16)
                QKV[pl.ds(off + D, HEAD_DIM), c] = nt(qq * bf16(SCALE), grads[u]).astype(bf16)
                QKV[pl.ds(off + 2 * D, HEAD_DIM), c] = nt(H1[pl.ds(off, HEAD_DIM), c], probs[u]).astype(bf16)
            tick(str(b))
        slot = lax.rem(n + 1, 2)

        @pl.when(n == 1)
        def _():
            staged_free(8)

        @pl.when(n > 1)
        def _():
            wait_send(STG.at[0, pl.ds(0, 3), t], gss.at[n - 2])
        rows = lambda part: QKV[pl.ds(pl.multiple_of(part * D + q * 192, 64), 192), :]
        v = nt(jnp.concatenate([rows(0), rows(1), rows(2)], axis=0), H0[...]).astype(bf16)
        STG[slot, 0:3] = v.reshape(3, 2, 2, 48, D)
        push(STG.at[slot, pl.ds(0, 3), t], ACC.at[QKV_SETS, q], gss.at[n], gsr.at[n], sib)
        tick("g")

    moved(spill_x, HACC, local.at[5])

    @pl.when(s == 1)
    def _():
        moved(MACC, out.at[:, mine], local.at[7])

    @pl.when(s == 0)
    def _():
        wait_send(MACC, i_s.at[5])

    G1(3)
    MACC[...] = tn(square(fa[:3]), QKV[...])
    G3()
    GG[...] = jnp.zeros_like(GG)

    @pl.loop(0, tiles)
    def _(i):
        c = col(i)
        v = HACC[:, c]
        dx, part = norm_back(v, inv_rms(v), GCOL[0, :, :1], MACC[:, c])
        GG[...] += lane_fold(part)
        G[:, c] = G[:, c] + dx - dx[D - 1:, :]
    GV[0] = jnp.sum(GG[...].T, axis=0, keepdims=True)

    @pl.when(s == 0)
    def _():
        move(G, out.at[:, mine], local.at[8])

    @pl.when(s == 1)
    def _():
        push(G, out.at[:, mine], i_s.at[5], i_r.at[5], sib)

    push(GV.at[t], GL.at[0], gs.at[0], gr.at[0], sib)
    wait_recv(GL.at[0], gr.at[0])
    GT[0] = GV[s] + GL[0]
    push(GT.at[0], GL.at[1], gs.at[1], gr.at[1], n2)
    wait_recv(GL.at[1], gr.at[1])
    GT[1] = GT[0] + GL[1]
    push(GT.at[1], GL.at[2], gs.at[2], gr.at[2], n1)
    wait_recv(GL.at[2], gr.at[2])
    GT[2] = GT[1] + GL[2]
    for r in range(3):
        push(GT.at[2], GL.at[3 + r], gs.at[3 + r], gr.at[3 + r], at_plane(lax.rem(z + 1 + r, 4)))

    def total_of(v, parts):
        v = wide(v)
        for part in parts:
            v = v + wide(part)
        return square(v)

    whole = lambda i: HACC.at[pl.ds(i * 96, 96), pl.ds(0, D)]
    lower = lambda i: HACC.at[pl.ds(pl.multiple_of(192 + 48 * i, 16), 48), pl.ds(0, D)]

    for k in range(3):
        wait_recv(L3W.at[k], rw.at[k])
    whole(1)[...] = total_of(ACC[0, xy], [L3W[k] for k in range(3)])
    for sec in range(2):
        for r in range(3):
            zz = lax.rem(z + 1 + r, 4)
            wait_recv(L3D.at[sec, zz], rd.at[sec, zz])
        far = lax.rem(z + 4 - (2 * sec + z // 2), 4)
        lower(sec)[...] = total_of(ACC[2 * at_step(far) + 1, xy, lax.rem(z, 2)], [L3D[sec, lax.rem(z + 1 + r, 4)] for r in range(3)])
    move(lower(s), down.at[s], local.at[9])
    push(lower(t), down.at[s], i_s.at[6], i_r.at[6], sib)

    @pl.when(s == 1)
    def _():
        move(whole(1), first.at[1], local.at[10])

    @pl.when(s == 0)
    def _():
        push(whole(1), first.at[0], i_s.at[7], i_r.at[7], sib)

    for r in range(3):
        wait_recv(GL.at[3 + r], gr.at[3 + r])
    GT[3] = GT[2] + GL[3] + GL[4] + GL[5]
    gain_out[...] = GT[3]
    for r in range(3):
        zz = lax.rem(z + 1 + r, 4)
        wait_recv(L3A.at[zz], ra.at[zz])
    whole(0)[...] = total_of(ACC[8 + lax.rem(z + 1, 4), xy], [L3A[lax.rem(z + 1 + r, 4)] for r in range(3)])

    @pl.when(s == 0)
    def _():
        move(whole(0), first.at[0], local.at[10])

    @pl.when(s == 1)
    def _():
        push(whole(0), first.at[1], i_s.at[7], i_r.at[7], sib)

    @pl.when(s == 0)
    def _():
        moved(whole(0), first.at[0], local.at[10])
        wait_send(whole(1), i_s.at[7])
        wait_recv(first.at[1], i_r.at[7])
        moved(G, out.at[:, mine], local.at[8])

    @pl.when(s == 1)
    def _():
        moved(whole(1), first.at[1], local.at[10])
        wait_send(whole(0), i_s.at[7])
        wait_recv(first.at[0], i_r.at[7])
        wait_send(G, i_s.at[5])

    wait_recv(out.at[:, other], i_r.at[5])
    moved(lower(s), down.at[s], local.at[9])
    wait_send(lower(t), i_s.at[6])
    wait_recv(down.at[t], i_r.at[6])
    wait_send(wd_ref.at[t], i_s.at[1])
    wait_send(gain_ref, i_s.at[2])
    a, b = rows_of(other)
    wait_send(a, i_s.at[3])
    wait_send(b, i_s.at[4])
    for n in range(6):
        wait_send(GT.at[0], gs.at[n])
    for kind in range(3):
        sent(kind)
    wait_send(STG.at[0, pl.ds(0, 3), t], gss.at[2])
    wait_send(STG.at[0, pl.ds(0, 3), t], gss.at[3])
    for j in range(9):
        scattered(j)
    G_sent()


def finish_kernel(len_ref, pre, first, down, gain, out, first_out, down_out, gain_out, a, b, c, e, ins, outs, rest):
    n = pre.shape[1] // SLOTS
    cols = lambda i: pl.ds(i * SLOTS, SLOTS)
    load = lambda i: pltpu.make_async_copy(pre.at[:, cols(i)], a.at[i], ins.at[i])
    save = lambda i: pltpu.make_async_copy(b.at[i], out.at[:, 0, cols(i)], outs.at[i])
    for i in range(n):
        load(i).start()
    passed = ((first, c, first_out, 0), (down, e, down_out, 2))
    for src, between, dst, at in passed:
        pltpu.make_async_copy(src, between, rest.at[at]).start()
    share = gain_out.shape[1]
    back = lax.rem(D - lax.axis_index("dp") * share, D)
    gain_out[...] = pltpu.roll(jnp.broadcast_to(gain[...], (8, D)), back, 1)[:1, :share]
    for i in range(n):
        load(i).wait()
        start, shift = 0, 0
        for j in range(4):
            shift = shift + jnp.where(len_ref[i, j] == LONGEST, start, 0)
            start = start + len_ref[i, j]
        b[i] = pltpu.roll(a[i], shift, 1)[:D - 1]
        save(i).start()
    for src, between, dst, at in passed:
        pltpu.make_async_copy(src, between, rest.at[at]).wait()
        pltpu.make_async_copy(between, dst, rest.at[at + 1]).start()
    for i in range(n):
        save(i).wait()
    for src, between, dst, at in passed:
        pltpu.make_async_copy(between, dst, rest.at[at + 1]).wait()


def layer(lengths, mask, gain, stream, w, wd):
    T = stream.shape[2] // 2
    dma = lambda *shape: pltpu.SemaphoreType.DMA(shape)
    bulk = lambda *shape: pltpu.VMEM(shape, bf16)
    full = lambda *shape: pltpu.VMEM(shape, f32)
    scratch = [
        bulk(4, 4, 2, 96, D), bulk(4, 4, 2, 96, D), bulk(2, 4, 4, 2, 48, D),
        full(D, T), full(D, T), full(8, T), full(8, T),
        bulk(3 * D, T), bulk(D, T), bulk(D, T), bulk(D, T), bulk(D, T),
        full(D, T), full(D, T), full(T // SLOTS, 2, TILE, TILE), full(16, T), full(8, T),
        full(2, 1, D), full(2, D, 128), full(D, 128), full(2, 1, D), full(6, 1, D), full(4, 1, D),
        bulk(2, 4, 2, 2, 48, D), bulk(2, 4, 2, 48, D), bulk(SETS, 4, 2, 48, D), bulk(SETS, 2, 2, 48, D), bulk(SETS, 2, 48, D),
        bulk(3, 2, 48, D), bulk(4, 2, 48, D), bulk(2, 4, 48, D),
        dma(3, 4), dma(3, 4), dma(3, 4, 4), dma(3, 4, 4),
        dma(SETS, 2), dma(SETS, 2), dma(SETS, 2), dma(SETS, 2), dma(SETS), dma(SETS),
        dma(SETS, 2), dma(3), dma(4), dma(2, 4),
        dma(8), dma(8), dma(11), dma(6), dma(6), dma(4), dma(4), dma(4), dma(4),
    ]
    out, first, down, gains, _, _ = pl.pallas_call(
        layer_kernel,
        in_specs=[S, V, HBM, HBM, HBM, HBM],
        out_specs=[HBM, HBM, HBM, V, HBM, HBM],
        out_shape=[
            sds(D, 2 * T), sds(2, 96, D), sds(2, 48, D), sds(1, D), sds(D, T), sds(3 * D, T, dtype=bf16),
        ],
        scratch_shapes=scratch,
        compiler_params=pltpu.CompilerParams(collective_id=1, has_side_effects=True, vmem_limit_bytes=VMEM_MOST),
        name="layer",
    )(lengths, mask, gain, stream, w.reshape(2, 96, D), wd.reshape(2, 48, D))
    share = D // lax.axis_size("dp")
    final, first, down, gains = pl.pallas_call(
        finish_kernel,
        in_specs=[S, HBM, HBM, HBM, V],
        out_specs=[HBM, HBM, HBM, V],
        out_shape=[sds(D - 1, 1, 2 * T), sds(2, 96, D), sds(2, 48, D), sds(1, share)],
        scratch_shapes=[full(4, D, SLOTS), full(4, D - 1, SLOTS), full(2, 96, D), full(2, 48, D), dma(4), dma(4), dma(4)],
        compiler_params=pltpu.CompilerParams(vmem_limit_bytes=VMEM_MOST),
        name="finish",
    )(lengths, out, first, down, gains)
    return final, first.reshape(192, D), down.reshape(96, D), gains


def separate(own, stream, w, wd, gain, doc_lengths, pad_mask, sections, groups):
    s, d = own
    stream = jnp.pad(stream[:, 0], ((0, 1), (0, 0)))
    gain = jnp.broadcast_to(gain[0][:, None], (D, 128))
    T = stream.shape[1] // sections
    nb = T // SLOTS
    own_docs = lax.dynamic_slice_in_dim(doc_lengths, s * nb, nb, axis=0)
    ends = jnp.stack([jnp.sum(own_docs[:, : j + 1], axis=1) for j in range(own_docs.shape[1])], axis=1)
    mask = lax.dynamic_slice_in_dim(pad_mask, s * T, T, axis=0).astype(f32)
    mask = jnp.broadcast_to(mask[None], (8, T))
    weights = lax.all_gather(lax.all_gather(w, "dp", axis=0, tiled=True), "section")
    wd_full = lax.all_gather(wd, ("section", "dp"), axis=0, tiled=True)
    both = lax.all_gather(stream, "section")
    x, g = lax.dynamic_slice_in_dim(both, s * T, T, axis=2)
    gains = lax.all_gather(gain, "section")
    qkv, att, lse, h0, x1, h1 = run_attn_fwd(ends, x, gains[0], gains[1], mask, weights[0])
    out1, dy, gw1, gwd, gg1 = run_ffn(g, gains[1], mask, x1, h1, weights[1], wd_full)
    out0, gw0, gg0 = run_attn_bwd(ends, x, gains[0], mask, weights[0], qkv, att, lse, h0, dy)
    gw = jnp.stack([gw0, gw1])
    gg = jnp.stack([gg0, gg1])
    first = lax.psum_scatter(gw.astype(f32), "section", scatter_dimension=0)
    first = lax.psum_scatter(first, "dp", scatter_dimension=0, tiled=True)
    down = lax.psum_scatter(gwd.astype(f32), ("section", "dp"), scatter_dimension=0, tiled=True)
    outs = lax.all_gather(jnp.stack([out0, out1]), "section")
    out = jnp.concatenate([lax.dynamic_index_in_dim(outs[i], s, 0, False) for i in range(2)], axis=1)
    gain_total = lax.psum_scatter(lax.psum(jnp.sum(gg, axis=2), "dp"), "section", scatter_dimension=0)
    return out[: D - 1][:, None], first, down, gain_total[None]


def shards(sizes, stream_pair, norm_gains, first_proj, down_proj, doc_lengths, pad_mask):
    own = lax.axis_index("section"), lax.axis_index("dp")
    sections, groups = sizes
    stream = jnp.transpose(stream_pair, (2, 0, 1))
    w = jnp.transpose(first_proj[0])
    wd = jnp.transpose(down_proj)
    if sizes == (2, 16) and stream.shape[2] == 4 * SLOTS:
        out, first, down, gain_share = layer(doc_lengths, pad_mask[None], norm_gains, stream, w, wd)
    else:
        out, first, down, gain_total = separate(
            own, stream, w, wd, norm_gains, doc_lengths, pad_mask, sections, groups
        )
        share = D // groups
        gain_share = lax.dynamic_slice_in_dim(gain_total, own[1] * share, share, axis=1)
    return jnp.transpose(out, (1, 2, 0)), gain_share, jnp.transpose(first)[None], jnp.transpose(down)


def solution(mesh):
    placed = (
        P("section", "dp", None),
        P("section", None),
        P("section", None, "dp"),
        P(None, ("section", "dp")),
        P("dp", None),
        P("dp"),
    )
    return jax.shard_map(
        functools.partial(shards, (mesh.shape["section"], mesh.shape["dp"])),
        mesh=mesh,
        in_specs=placed,
        out_specs=(
            P("section", "dp", None),
            P("section", "dp"),
            P("section", None, "dp"),
            P(None, ("section", "dp")),
        ),
        check_vma=False,
    )
```
